32 devices in a mesh: rep: 8 (over y, x, core), grp: 4 (over z).
Axes of the slice: x: 2, y: 2, z: 4, core: 2. Of those that a mesh axis runs over, the one named last changes fastest.
Arguments:
- tokens: bfloat16 [8192, 576], P(('rep', 'grp')), may hold values from -40 to 40
- segments: int32 [8192], P(('rep', 'grp')), may hold values from 0 to 31, as said below
- out_grad: bfloat16 [8192, 576], P(('rep', 'grp')), may hold values from -6 to 6
- norm_gain: bfloat16 [576], P('grp'), may hold values from 0.25 to 1.75
- query_gain: bfloat16 [64], P('grp'), may hold values from 0.25 to 1.75
- key_gain: bfloat16 [64], P('grp'), may hold values from 0.25 to 1.75
- query_weight: bfloat16 [576, 576], P('grp'), may hold values from -0.25 to 0.25
- key_weight: bfloat16 [576, 192], P('grp'), may hold values from -0.25 to 0.25
- value_weight: bfloat16 [576, 192], P('grp'), may hold values from -0.25 to 0.25
- output_weight: bfloat16 [576, 576], P('grp'), may hold values from -2 to 2
- second_gain: bfloat16 [576], P('grp'), may hold values from 0.25 to 1.75
- gate_weight: bfloat16 [576, 1536], P('grp'), may hold values from -0.25 to 0.25
- up_weight: bfloat16 [576, 1536], P('grp'), may hold values from -0.25 to 0.25
- down_weight: bfloat16 [1536, 576], P('grp'), may hold values from -0.15625 to 0.15625
Outputs:
- layer_out: bfloat16 [8192, 576], P(('rep', 'grp'))
- token_grad: float32 [8192, 576], P(('rep', 'grp'))
- grad_norm_gain: float32 [576], P('grp')
- grad_query_gain: float32 [64], P('grp')
- grad_key_gain: float32 [64], P('grp')
- grad_query_weight: float32 [576, 576], P('grp')
- grad_key_weight: float32 [576, 192], P('grp')
- grad_value_weight: float32 [576, 192], P('grp')
- grad_output_weight: float32 [576, 576], P('grp')
- grad_second_gain: float32 [576], P('grp')
- grad_gate_weight: float32 [576, 1536], P('grp')
- grad_up_weight: float32 [576, 1536], P('grp')
- grad_down_weight: float32 [1536, 576], P('grp')
The draws below stay inside these ranges and needn't reach their ends.
Inputs may be any that keep to these rules, and one draw needn't show every extreme that they name: `segments`: segment numbers never fall along the tokens. Each sequence s holds three or four documents of 60 to 800 tokens; its first document is numbered 4 * s and its last 4 * s + 3, those between take numbers between these. One of its documents begins within the sequence's first 256 tokens and ends within its last 256.
All inputs are finite; a program needn't handle non-finite values.
Results may differ from the reference program's by a relative error of at most 0.012.
The reference program's roundings to bfloat16 on the way count: a program that leaves them out, or rounds other values in their place, can miss the bound.
Values may be sent and summed in bfloat16 or wider, within the bound.
No kernel may reach another device: no remote copies, remote signals or barrier semaphores. Data moves between devices by JAX's collectives and lax.ppermute only.
A program may use at most 128 MiB of HBM per device.

```python
import math
from functools import partial
import jax
import jax.numpy as jnp
from jax import lax

D = 576
HEADS = 9
KV_HEADS = 3
HEAD_DIM = 64
FF = 1536
TOK_DEV = 256
QW = 576
KVW = 192
SEQ_LEN = 1024
SEQS = 8
TOKENS = 8192
DOC_MIN = 60
DOC_MAX = 800


def draw_tokens(key, part):
    key = jax.random.fold_in(key, 11)
    noise_key, row_key, column_key = jax.random.split(key, 3)
    spread = 0.5 * math.log(10.0)
    row_scale = jnp.exp(jax.random.uniform(row_key, (TOKENS, 1), jnp.float32, -spread, spread))
    column_scale = jnp.exp(jax.random.uniform(column_key, (1, D), jnp.float32, -spread, spread))
    drawn = jax.random.truncated_normal(noise_key, -4.0, 4.0, (TOKENS, D), jnp.float32)
    return (drawn * row_scale * column_scale).astype(jnp.bfloat16)


def draw_segments(key, part):
    key = jax.random.fold_in(key, 23)
    head_key, long_key, coin_key, cut_key = jax.random.split(key, 4)
    head_length = jax.random.randint(head_key, (SEQS, 1), DOC_MIN, TOK_DEV)
    long_low = 3 * TOK_DEV + 1 - head_length
    long_high = jnp.minimum(DOC_MAX, SEQ_LEN - DOC_MIN - head_length)
    long_length = jax.random.randint(long_key, (SEQS, 1), long_low, long_high + 1)
    long_end = head_length + long_length
    tail_length = SEQ_LEN - long_end
    coin = jax.random.randint(coin_key, (SEQS, 1), 0, 2)
    cut_high = jnp.maximum(tail_length - DOC_MIN + 1, DOC_MIN + 1)
    cut_length = jax.random.randint(cut_key, (SEQS, 1), DOC_MIN, cut_high)
    split_tail = (coin == 1) & (tail_length >= 2 * DOC_MIN)
    third_start = jnp.where(split_tail, long_end + cut_length, long_end)
    positions = jnp.arange(SEQ_LEN, dtype=jnp.int32)[None, :]
    seq_base = 4 * jnp.arange(SEQS, dtype=jnp.int32)[:, None]
    doc_ids = seq_base + (positions >= head_length).astype(jnp.int32) + (positions >= long_end).astype(jnp.int32) + (positions >= third_start).astype(jnp.int32)
    return doc_ids.reshape(TOKENS).astype(jnp.int32)


def level_of(own_key, extent, shards, low, high):
    loudness = 1.0
    for position, parts in shards:
        heights = jax.random.uniform(jax.random.fold_in(jax.random.fold_in(own_key, 6), position), (parts,), jnp.float32, low / len(shards), high / len(shards))
        loudness = loudness * jnp.repeat(jnp.exp(heights), extent[position] // parts).reshape((-1,) + (1,) * (len(extent) - 1 - position))
    return loudness


def scatter_about(key, dims, scale, limit, cuts=(), held_as=jnp.bfloat16):
    loudness = level_of(key, dims, cuts, -0.22, 0.18) if cuts else 1.0
    drawn = jax.random.normal(key, dims, jnp.float32) * scale * loudness
    return jnp.minimum(jnp.maximum(drawn, -limit), limit).astype(held_as)


def setup_inputs(seed: int = 0) -> dict:
    seeds = jax.random.split(jax.random.key(seed), 15)
    tokens = draw_tokens(jax.random.fold_in(seeds[14], 71), 0)
    segments = draw_segments(jax.random.fold_in(seeds[14], 71), 0)
    out_grad = scatter_about(seeds[2], (TOKENS, D), 1.0, 6.0, ((0, 32),))
    norm_gain = jnp.clip(1.0 + 0.15 * jax.random.normal(seeds[3], (D,), jnp.float32), 0.25, 1.75).astype(jnp.bfloat16)
    query_gain = jnp.clip(1.0 + 0.15 * jax.random.normal(seeds[4], (HEAD_DIM,), jnp.float32), 0.25, 1.75).astype(jnp.bfloat16)
    key_gain = jnp.clip(1.0 + 0.15 * jax.random.normal(seeds[5], (HEAD_DIM,), jnp.float32), 0.25, 1.75).astype(jnp.bfloat16)
    query_weight = scatter_about(seeds[6], (D, QW), D ** -0.5, 0.25, ((0, 4),))
    key_weight = scatter_about(seeds[7], (D, KVW), D ** -0.5, 0.25, ((0, 4),))
    value_weight = scatter_about(seeds[8], (D, KVW), D ** -0.5, 0.25, ((0, 4),))
    output_weight = scatter_about(seeds[9], (QW, D), (D // 64) ** -0.5, 2.0, ((0, 4),))
    second_gain = jnp.clip(1.0 + 0.15 * jax.random.normal(seeds[10], (D,), jnp.float32), 0.25, 1.75).astype(jnp.bfloat16)
    gate_weight = scatter_about(seeds[11], (D, FF), D ** -0.5, 0.25, ((0, 4),))
    up_weight = scatter_about(seeds[12], (D, FF), D ** -0.5, 0.25, ((0, 4),))
    down_weight = scatter_about(seeds[13], (FF, D), FF ** -0.5, 0.15625, ((0, 4),))
    return dict(tokens=tokens, segments=segments, out_grad=out_grad, norm_gain=norm_gain, query_gain=query_gain, key_gain=key_gain, query_weight=query_weight, key_weight=key_weight, value_weight=value_weight, output_weight=output_weight, second_gain=second_gain, gate_weight=gate_weight, up_weight=up_weight, down_weight=down_weight)


NORM_EPS = 1e-05
ROPE_BASE = 100000.0
highest = lax.Precision.HIGHEST

@jax.custom_vjp
def low(v):
    return lax.optimization_barrier(v.astype(jnp.bfloat16)).astype(jnp.float32)

@jax.custom_vjp
def low_back(v):
    return v

def low_keep(v):
    return (low(v), None)

def low_pass(kept, grad):
    return (grad,)

def back_keep(v):
    return (v, None)

def back_low(kept, grad):
    return (low(grad),)
low.defvjp(low_keep, low_pass)
low_back.defvjp(back_keep, back_low)

def rms_scale(vector, gain_vec):
    return vector * lax.rsqrt(lax.optimization_barrier(jnp.mean(vector * vector, axis=-1, keepdims=True)) + NORM_EPS) * gain_vec

def rope_tables(positions, head_size):
    half_size = head_size // 2
    inverse = ROPE_BASE ** (-(jnp.arange(half_size, dtype=jnp.float32) * 2.0 / head_size))
    angles = positions.astype(jnp.float32)[:, None] * inverse[None, :]
    angles = jnp.concatenate([angles, angles], axis=-1)
    return (jnp.cos(angles)[:, None, :], jnp.sin(angles)[:, None, :])

def rotate(vector, cosine, sine_table):
    half_size = vector.shape[-1] // 2
    turned = jnp.concatenate([-vector[..., half_size:], vector[..., :half_size]], axis=-1)
    return vector * cosine + turned * sine_table

def attend_sequence(pieces):
    queries, keys, values, doc_ids = pieces
    key_order = jnp.arange(doc_ids.shape[0], dtype=jnp.int32)
    allowed = (doc_ids[:, None] == doc_ids[None, :]) & (key_order[None, :] <= key_order[:, None])
    scores = jnp.einsum('tkrd,skd->krts', queries, keys, precision=highest) * HEAD_DIM ** (-0.5)
    scores = low_back(scores)
    scores = jnp.where(allowed[None, None], scores, -1e+30)
    row_max = lax.optimization_barrier(jnp.max(scores, axis=-1, keepdims=True))
    exp_scores = jnp.exp(scores - row_max)
    probabilities = exp_scores / lax.optimization_barrier(jnp.sum(exp_scores, axis=-1, keepdims=True))
    return jnp.einsum('krts,skd->tkrd', low(probabilities), values, precision=highest)

def layer(doc_ids, positions, tokens, norm_gain, query_gain, key_gain, query_weight, key_weight, value_weight, output_weight, second_gain, gate_weight, up_weight, down_weight):
    group_size = HEADS // KV_HEADS
    cosine, sine_table = rope_tables(positions, HEAD_DIM)
    normed = low(rms_scale(tokens, norm_gain))
    query_proj = low_back(jnp.dot(normed, query_weight, precision=highest))
    key_proj = low_back(jnp.dot(normed, key_weight, precision=highest))
    value_proj = low(low_back(jnp.dot(normed, value_weight, precision=highest)))
    queries = low(rotate(rms_scale(query_proj.reshape(TOKENS, HEADS, HEAD_DIM), query_gain), cosine, sine_table))
    keys = low(rotate(rms_scale(key_proj.reshape(TOKENS, KV_HEADS, HEAD_DIM), key_gain), cosine, sine_table))
    attended = lax.map(jax.checkpoint(attend_sequence), (queries.reshape(SEQS, SEQ_LEN, KV_HEADS, group_size, HEAD_DIM), keys.reshape(SEQS, SEQ_LEN, KV_HEADS, HEAD_DIM), value_proj.reshape(SEQS, SEQ_LEN, KV_HEADS, HEAD_DIM), doc_ids.reshape(SEQS, SEQ_LEN)))
    attended = low(low_back(attended.reshape(TOKENS, HEADS * HEAD_DIM)))
    mixed = tokens + low_back(jnp.dot(attended, output_weight, precision=highest))
    mlp_normed = low(rms_scale(mixed, second_gain))
    gate_proj = low_back(jnp.dot(mlp_normed, gate_weight, precision=highest))
    up_proj = low_back(jnp.dot(mlp_normed, up_weight, precision=highest))
    hidden = low(jax.nn.silu(gate_proj) * up_proj)
    return mixed + low_back(jnp.dot(hidden, down_weight, precision=highest))

def place_tokens(doc_ids):
    key_order = jnp.arange(SEQ_LEN, dtype=jnp.int32)
    return key_order - lax.optimization_barrier(jnp.sum((doc_ids[None, :] < doc_ids[:, None]).astype(jnp.int32), axis=1))

def reference(tokens, segments, out_grad, norm_gain, query_gain, key_gain, query_weight, key_weight, value_weight, output_weight, second_gain, gate_weight, up_weight, down_weight):
    positions = lax.map(place_tokens, segments.reshape(SEQS, SEQ_LEN)).reshape(TOKENS)
    primals = [member.astype(jnp.float32) for member in (tokens, norm_gain, query_gain, key_gain, query_weight, key_weight, value_weight, output_weight, second_gain, gate_weight, up_weight, down_weight)]
    result, pullback = jax.vjp(partial(layer, segments, positions), *primals)
    grads = pullback(out_grad.astype(jnp.float32))
    return (result.astype(jnp.bfloat16), grads[0], grads[1], grads[2], grads[3], grads[4], grads[5], grads[6], grads[7], grads[8], grads[9], grads[10], grads[11])
```

```python
import jax
import jax.numpy as jnp
from jax import lax
from jax.sharding import PartitionSpec as P

NORM_EPS = 1e-05
ROPE_BASE = 100000.0


def rms_scale(vector, gain_vec):
    return (
        vector * lax.rsqrt(jnp.mean(vector * vector, axis=-1, keepdims=True) + NORM_EPS) * gain_vec
    )


def rope_tables(positions, head_size):
    half_size = head_size // 2
    inverse = ROPE_BASE ** (-(jnp.arange(half_size, dtype=jnp.float32) * 2.0 / head_size))
    angles = positions.astype(jnp.float32)[:, None] * inverse[None, :]
    angles = jnp.concatenate([angles, angles], axis=-1)
    return (jnp.cos(angles)[:, None, :], jnp.sin(angles)[:, None, :])


def rotate(vector, cosine, sine_table):
    half_size = vector.shape[-1] // 2
    turned = jnp.concatenate([-vector[..., half_size:], vector[..., :half_size]], axis=-1)
    return vector * cosine + turned * sine_table


def swiglu(gate_in, up_in):
    return jax.nn.silu(gate_in) * up_in


LANES = 128


def hop(value, bit):
    count = lax.axis_size("rep")
    return lax.ppermute(value, "rep", [(i, i ^ bit) for i in range(count)])


def shift(value, step):
    count = lax.axis_size("grp")
    return lax.ppermute(value, "grp", [(i, (i + step) % count) for i in range(count)])


def side(value, bit, axis=1):
    half = value.shape[axis] // 2
    return lax.dynamic_slice_in_dim(value, bit * half, half, axis)


def place(own, other, bit, axis=1):
    return jnp.where(
        bit == 0,
        jnp.concatenate([own, other], axis),
        jnp.concatenate([other, own], axis),
    )


def rep_bits():
    index = lax.axis_index("rep")
    return index & 1, (index >> 1) & 1, (index >> 2) & 1


def spread(first, second, axis=1):
    bit_c, bit_x, bit_y = rep_bits()
    first, second = place(first, hop(first, 4), bit_y, axis), place(second, hop(second, 2), bit_x, axis)
    first, second = place(first, hop(first, 2), bit_x, axis), place(second, hop(second, 4), bit_y, axis)
    first, second = place(first, hop(first, 1), bit_c, axis), place(second, hop(second, 1), bit_c, axis)
    return jnp.concatenate([first, second], axis)


def gather_pack(pack):
    count = lax.axis_size("grp")
    place_z = lax.axis_index("grp")
    bit_c, bit_x, bit_y = rep_bits()
    rows = pack.shape[0]
    part = rows // 16
    first = lax.dynamic_slice_in_dim(pack, (bit_c * 4 + bit_x * 2 + bit_y) * part, part, 0)
    second = lax.dynamic_slice_in_dim(
        pack, rows // 2 + (bit_c * 4 + bit_y * 2 + bit_x) * part, part, 0
    )
    own = jnp.concatenate([first, second], 0)
    stack = jnp.zeros((count,) + own.shape, own.dtype)
    stack = lax.dynamic_update_index_in_dim(stack, own, place_z, 0)
    for step in range(1, count):
        stack = lax.dynamic_update_index_in_dim(
            stack, shift(own, step), lax.rem(place_z + count - step, count), 0
        )
    return spread(stack[:, :part], stack[:, part:])


def reduce_pack(parts):
    f32 = jnp.float32
    kind = parts.dtype

    def add(one, two):
        return (one.astype(f32) + two.astype(f32)).astype(kind)

    count = lax.axis_size("grp")
    place_z = lax.axis_index("grp")
    bit_c, bit_x, bit_y = rep_bits()
    rows = parts.shape[1]

    def fold(value, bit, which):
        return add(side(value, bit), hop(side(value, 1 - bit), which))

    first, second = parts[:, : rows // 2], parts[:, rows // 2 :]
    first, second = fold(first, bit_c, 1), fold(second, bit_c, 1)
    first, second = fold(first, bit_x, 2), fold(second, bit_y, 4)
    first, second = fold(first, bit_y, 4), fold(second, bit_x, 2)
    both = jnp.concatenate([first, second], 1)
    total = lax.dynamic_index_in_dim(both, place_z, 0, False).astype(f32)
    for step in range(1, count):
        sent = lax.dynamic_index_in_dim(both, lax.rem(place_z + step, count), 0, False)
        total = total + shift(sent, step).astype(f32)
    total = total.astype(kind)
    bit = 8
    while bit < lax.axis_size("rep"):
        total = add(total, hop(total, bit))
        bit *= 2
    part = total.shape[0] // 2
    return spread(total[:part], total[part:], 0)


def to_blocks(weight):
    columns = weight.shape[-1]
    short = -columns % LANES
    if short:
        weight = jnp.pad(weight, [(0, 0)] * (weight.ndim - 1) + [(0, short)])
    blocks = [weight[..., at : at + LANES] for at in range(0, columns, LANES)]
    return jnp.concatenate(blocks, axis=-2)


def from_blocks(blocks, columns):
    count = -(-columns // LANES)
    rows = blocks.shape[-2] // count
    pieces = [blocks[..., at * rows : (at + 1) * rows, :] for at in range(count)]
    return jnp.concatenate(pieces, axis=-1)[..., :columns]


def fill(pieces, axis):
    whole = jnp.concatenate(pieces, axis)
    short = -whole.shape[axis] % 128
    width = [(0, 0)] * whole.ndim
    width[axis] = (0, short)
    return jnp.pad(whole, width)


def cut(pack, counts):
    at, pieces = 0, []
    for count in counts:
        pieces.append(pack[..., at : at + count, :])
        at += count
    return pieces


def rows_of(vector, count):
    short = count * LANES - vector.shape[-1]
    vector = jnp.pad(vector, [(0, 0)] * (vector.ndim - 1) + [(0, short)])
    return vector.reshape(vector.shape[:-1] + (count, LANES))


def lined(rows, length):
    return rows.reshape(rows.shape[:-2] + (-1,))[..., :length]


def body(
    tokens,
    segments,
    out_grad,
    norm_gain,
    query_gain,
    key_gain,
    query_weight,
    key_weight,
    value_weight,
    output_weight,
    second_gain,
    gate_weight,
    up_weight,
    down_weight,
):
    f32 = jnp.float32
    bf16 = jnp.bfloat16
    tok_rows = tokens.shape[0]
    groups = lax.axis_size("grp")
    head_size = query_gain.shape[0] * groups
    width = tokens.shape[1]
    shard = norm_gain.shape[0]
    q_width = query_weight.shape[1]
    kv_width = key_weight.shape[1]
    hidden_width = gate_weight.shape[1]
    own_hidden = down_weight.shape[0]
    proj = jnp.concatenate([query_weight, key_weight, value_weight], 1)
    proj_rows = -(-proj.shape[1] // LANES) * shard
    gain_rows = -(-shard // LANES)
    small_counts = (gain_rows, gain_rows, 1, 1)
    pack_a = fill(
        [
            to_blocks(proj),
            rows_of(norm_gain, gain_rows),
            rows_of(second_gain, gain_rows),
            rows_of(query_gain, 1),
            rows_of(key_gain, 1),
        ],
        0,
    )
    out_rows = -(-output_weight.shape[1] // LANES) * shard
    wide_rows = hidden_width // LANES * shard
    down_rows = own_hidden // LANES * width
    pack_b = fill(
        [to_blocks(gate_weight), to_blocks(up_weight), to_blocks(down_weight.T), to_blocks(output_weight)],
        0,
    )
    full_a = gather_pack(pack_a)
    full_b = gather_pack(pack_b)
    proj_all, first_gain_all, second_gain_all, query_gain_all, key_gain_all = cut(
        full_a, (proj_rows,) + small_counts
    )
    proj_all = from_blocks(proj_all, proj.shape[1]).reshape(width, -1)
    weight_query = proj_all[:, :q_width]
    weight_key = proj_all[:, q_width : q_width + kv_width]
    weight_value = proj_all[:, q_width + kv_width :]
    gain_first = lined(first_gain_all, shard).reshape(-1)
    gain_second = lined(second_gain_all, shard).reshape(-1)
    gain_query = lined(query_gain_all, head_size // groups).reshape(-1)
    gain_key = lined(key_gain_all, head_size // groups).reshape(-1)
    gate_all, up_all, down_all, output_all = cut(full_b, (wide_rows, wide_rows, down_rows, out_rows))
    weight_gate = from_blocks(gate_all, hidden_width).reshape(width, -1)
    weight_up = from_blocks(up_all, hidden_width).reshape(width, -1)
    weight_down = from_blocks(down_all, own_hidden).transpose(0, 2, 1).reshape(-1, width)
    weight_output = from_blocks(output_all, width).reshape(q_width, -1)
    kv_heads = weight_key.shape[1] // head_size
    query_heads = weight_query.shape[1] // head_size
    group_size = query_heads // kv_heads
    score_scale = head_size ** (-0.5)
    place_z = lax.axis_index("grp")
    key_count = groups * tok_rows
    own_order = jnp.arange(tok_rows, dtype=jnp.int32)
    query_index = place_z * tok_rows + own_order
    back = place_z - jnp.arange(groups, dtype=jnp.int32)
    key_index = (back[:, None] * tok_rows + own_order[None, :]).reshape(-1)
    held_segs = [segments]
    for step in range(1, groups):
        ahead = [(i, i + step) for i in range(groups - step)]
        held_segs.append(lax.ppermute(segments, "grp", ahead))
    key_segs = jnp.concatenate(held_segs)
    earlier = (key_segs[None, :] < segments[:, None]) & (key_index[None, :] >= 0)
    doc_starts = jnp.sum(earlier.astype(jnp.int32), axis=1)
    positions = query_index - doc_starts
    allowed = (
        (segments[:, None] == key_segs[None, :])
        & (key_index[None, :] <= query_index[:, None])
        & (key_index[None, :] >= 0)
    )
    cosine, sine_table = rope_tables(positions, head_size)

    def norm_rotate(raw_heads, gain_vec):
        return rotate(rms_scale(raw_heads, gain_vec), cosine, sine_table)

    inputs = tokens.astype(f32)
    normed, norm_back = jax.vjp(rms_scale, inputs, gain_first.astype(f32))
    normed_low = normed.astype(bf16)
    queries_raw = jnp.dot(normed_low, weight_query, preferred_element_type=f32)
    keys_raw = jnp.dot(normed_low, weight_key, preferred_element_type=f32)
    values_local = jnp.dot(normed_low, weight_value, preferred_element_type=f32).astype(bf16)
    query_rot, query_back = jax.vjp(
        norm_rotate, queries_raw.reshape(tok_rows, query_heads, head_size), gain_query.astype(f32)
    )
    key_rot, key_back = jax.vjp(
        norm_rotate, keys_raw.reshape(tok_rows, kv_heads, head_size), gain_key.astype(f32)
    )
    query_low = query_rot.astype(bf16).reshape(tok_rows, kv_heads, group_size, head_size)
    key_low = key_rot.astype(bf16).reshape(tok_rows, kv_heads * head_size)
    key_value = jnp.concatenate([key_low, values_local], 1)
    held = [key_value]
    for step in range(1, groups):
        ahead = [(i, i + step) for i in range(groups - step)]
        held.append(lax.ppermute(key_value, "grp", ahead))
    key_value = jnp.concatenate(held, 0)
    keys_all, values_all = key_value[:, :kv_width], key_value[:, kv_width:]
    keys_all = keys_all.reshape(key_count, kv_heads, head_size)
    values_all = values_all.reshape(key_count, kv_heads, head_size)
    scores = (
        jnp.einsum("tkrd,skd->krts", query_low, keys_all, preferred_element_type=f32) * score_scale
    )
    scores = jnp.where(allowed[None, None], scores, -1e30)
    row_max = jnp.max(scores, axis=-1, keepdims=True)
    exp_scores = jnp.exp(scores - row_max)
    row_sum = jnp.sum(exp_scores, axis=-1, keepdims=True)
    probabilities = exp_scores / row_sum
    log_sum = row_max + jnp.log(row_sum)
    attended = jnp.einsum(
        "krts,skd->tkrd", probabilities.astype(bf16), values_all, preferred_element_type=f32
    )
    attended = attended.reshape(tok_rows, query_heads * head_size).astype(bf16)
    mixed = inputs + jnp.dot(attended, weight_output, preferred_element_type=f32)
    mlp_normed, second_back = jax.vjp(rms_scale, mixed, gain_second.astype(f32))
    mlp_low = mlp_normed.astype(bf16)
    gate_proj = jnp.dot(mlp_low, weight_gate, preferred_element_type=f32)
    up_proj = jnp.dot(mlp_low, weight_up, preferred_element_type=f32)
    activated, gate_back = jax.vjp(swiglu, gate_proj, up_proj)
    hidden = activated.astype(bf16)
    layer_out = (mixed + jnp.dot(hidden, weight_down, preferred_element_type=f32)).astype(bf16)
    upstream = out_grad.astype(f32)
    down_grad = jnp.einsum("tf,td->fd", hidden, out_grad, preferred_element_type=f32)
    hidden_grad = jnp.einsum("td,fd->tf", out_grad, weight_down, preferred_element_type=f32)
    gate_grad, up_grad = gate_back(hidden_grad)
    gate_low = gate_grad.astype(bf16)
    up_low = up_grad.astype(bf16)
    gate_wgrad = jnp.einsum("td,tf->df", mlp_low, gate_low, preferred_element_type=f32)
    up_wgrad = jnp.einsum("td,tf->df", mlp_low, up_low, preferred_element_type=f32)
    normed2_grad = jnp.einsum(
        "tf,df->td", gate_low, weight_gate, preferred_element_type=f32
    ) + jnp.einsum("tf,df->td", up_low, weight_up, preferred_element_type=f32)
    mixed_part, second_ggrad = second_back(normed2_grad)
    mixed_grad = upstream + mixed_part
    branch_low = mixed_grad.astype(bf16)
    output_wgrad = jnp.einsum("tq,td->qd", attended, branch_low, preferred_element_type=f32)
    early = fill(
        [
            to_blocks(gate_wgrad.reshape(groups, shard, -1)),
            to_blocks(up_wgrad.reshape(groups, shard, -1)),
            to_blocks(down_grad.T.reshape(width, groups, -1).transpose(1, 0, 2)),
            to_blocks(output_wgrad.reshape(groups, shard, -1)),
        ],
        1,
    ).astype(bf16)
    early = reduce_pack(early)
    attended_grad = jnp.einsum(
        "td,qd->tq", branch_low, weight_output, preferred_element_type=f32
    ).astype(bf16)
    attended_grad = attended_grad.reshape(tok_rows, kv_heads, group_size, head_size)
    scores = (
        jnp.einsum("tkrd,skd->krts", query_low, keys_all, preferred_element_type=f32) * score_scale
    )
    scores = jnp.where(allowed[None, None], scores, -1e30)
    probabilities = jnp.exp(scores - log_sum)
    probs_grad = jnp.einsum("tkrd,skd->krts", attended_grad, values_all, preferred_element_type=f32)
    row_delta = jnp.sum(probabilities * probs_grad, axis=-1, keepdims=True)
    scores_low = (probabilities * (probs_grad - row_delta)).astype(bf16)
    queries_grad = (
        jnp.einsum("krts,skd->tkrd", scores_low, keys_all, preferred_element_type=f32) * score_scale
    )
    keys_part = (
        jnp.einsum("krts,tkrd->skd", scores_low, query_low, preferred_element_type=f32)
        * score_scale
    )
    values_part = jnp.einsum(
        "krts,tkrd->skd", probabilities.astype(bf16), attended_grad, preferred_element_type=f32
    )
    part = jnp.concatenate(
        [keys_part.reshape(key_count, kv_width), values_part.reshape(key_count, kv_width)], 1
    )
    part = part.reshape(groups, tok_rows, 2 * kv_width)
    total = part[0]
    for step in range(1, groups):
        behind = [(i + step, i) for i in range(groups - step)]
        total = total + lax.ppermute(part[step].astype(bf16), "grp", behind).astype(f32)
    keys_grad, values_grad = total[:, :kv_width], total[:, kv_width:]
    query_raw_grad, query_ggrad = query_back(queries_grad.reshape(tok_rows, query_heads, head_size))
    key_raw_grad, key_ggrad = key_back(keys_grad.reshape(tok_rows, kv_heads, head_size))
    query_plow = query_raw_grad.reshape(tok_rows, query_heads * head_size).astype(bf16)
    key_plow = key_raw_grad.reshape(tok_rows, kv_heads * head_size).astype(bf16)
    value_plow = values_grad.astype(bf16)
    query_wgrad = jnp.einsum("td,tq->dq", normed_low, query_plow, preferred_element_type=f32)
    key_wgrad = jnp.einsum("td,tq->dq", normed_low, key_plow, preferred_element_type=f32)
    value_wgrad = jnp.einsum("td,tq->dq", normed_low, value_plow, preferred_element_type=f32)
    normed_grad = jnp.einsum("tq,dq->td", query_plow, weight_query, preferred_element_type=f32)
    normed_grad = normed_grad + jnp.einsum(
        "tq,dq->td", key_plow, weight_key, preferred_element_type=f32
    )
    normed_grad = normed_grad + jnp.einsum(
        "tq,dq->td", value_plow, weight_value, preferred_element_type=f32
    )
    input_part, first_ggrad = norm_back(normed_grad)
    token_grad = mixed_grad + input_part
    proj_wgrad = jnp.concatenate([query_wgrad, key_wgrad, value_wgrad], 1)
    late = fill(
        [
            to_blocks(proj_wgrad.reshape(groups, shard, -1)),
            rows_of(first_ggrad.reshape(groups, -1), gain_rows),
            rows_of(second_ggrad.reshape(groups, -1), gain_rows),
            rows_of(query_ggrad.reshape(groups, -1), 1),
            rows_of(key_ggrad.reshape(groups, -1), 1),
        ],
        1,
    ).astype(bf16)
    late = reduce_pack(late)
    proj_sum, first_sum, second_sum, query_sum, key_sum = cut(late, (proj_rows,) + small_counts)
    proj_sum = from_blocks(proj_sum, proj.shape[1]).astype(f32)
    gate_sum, up_sum, down_sum, output_sum = cut(early, (wide_rows, wide_rows, down_rows, out_rows))
    return (
        layer_out,
        token_grad,
        lined(first_sum, shard).astype(f32),
        lined(query_sum, head_size // groups).astype(f32),
        lined(key_sum, head_size // groups).astype(f32),
        proj_sum[:, :q_width],
        proj_sum[:, q_width : q_width + kv_width],
        proj_sum[:, q_width + kv_width :],
        from_blocks(output_sum, width).astype(f32),
        lined(second_sum, shard).astype(f32),
        from_blocks(gate_sum, hidden_width).astype(f32),
        from_blocks(up_sum, hidden_width).astype(f32),
        from_blocks(down_sum, own_hidden).T.astype(f32),
    )


def solution(mesh):
    placed = (
        P(("rep", "grp"), None),
        P(("rep", "grp")),
        P(("rep", "grp"), None),
        P("grp"),
        P("grp"),
        P("grp"),
        P("grp", None),
        P("grp", None),
        P("grp", None),
        P("grp", None),
        P("grp"),
        P("grp", None),
        P("grp", None),
        P("grp", None),
    )
    return jax.shard_map(
        body,
        mesh=mesh,
        in_specs=placed,
        out_specs=(
            P(("rep", "grp"), None),
            P(("rep", "grp"), None),
            P("grp"),
            P("grp"),
            P("grp"),
            P("grp", None),
            P("grp", None),
            P("grp", None),
            P("grp", None),
            P("grp"),
            P("grp", None),
            P("grp", None),
            P("grp", None),
        ),
        check_vma=False,
    )
```

```python
import functools

import jax
import jax.numpy as jnp
from jax import lax
from jax.experimental import pallas as pl
from jax.experimental.pallas import tpu as pltpu
from jax.sharding import PartitionSpec as P

NORM_EPS = 1e-05
ROPE_BASE = 100000.0
LANES = 128
SMALL = 16
MIB = 1024 * 1024


def vmem():
    return pl.BlockSpec(memory_space=pltpu.VMEM)


def smem():
    return pl.BlockSpec(memory_space=pltpu.SMEM)


def hbm():
    return pl.BlockSpec(memory_space=pl.ANY)


def shape(dims, kind):
    return jax.ShapeDtypeStruct(dims, kind)


def options(mebibytes):
    return pltpu.CompilerParams(vmem_limit_bytes=mebibytes * MIB)


def cost(flops, mebibytes):
    return pl.CostEstimate(flops=flops, bytes_accessed=mebibytes * MIB, transcendentals=0)


def hop(value, bit):
    count = lax.axis_size("rep")
    return lax.ppermute(value, "rep", [(i, i ^ bit) for i in range(count)])


def shift(value, step):
    count = lax.axis_size("grp")
    return lax.ppermute(value, "grp", [(i, (i + step) % count) for i in range(count)])


def rep_bits():
    index = lax.axis_index("rep")
    return index & 1, (index >> 1) & 1, (index >> 2) & 1


def spread_pieces(first, second):
    first = jnp.stack([first, hop(first, 4)])
    second = jnp.stack([second, hop(second, 2)])
    first, second = (first, hop(first, 2)), (second, hop(second, 4))
    return [piece for path in (first, second) for piece in path + tuple(hop(p, 1) for p in path)]


def add_low(one, two):
    return (one.astype(jnp.float32) + two.astype(jnp.float32)).astype(one.dtype)


def reduce_pieces(keep, send):
    f32 = jnp.float32
    got = hop(send, 1)
    first, second = add_low(keep[0, 0], got[0, 0]), add_low(keep[1, 0], got[1, 0])
    far_first, far_second = add_low(keep[0, 1], got[0, 1]), add_low(keep[1, 1], got[1, 1])
    got_first, got_second = hop(far_first, 2), hop(far_second, 4)
    near_first, near_second = add_low(first[0], got_first[0]), add_low(second[0], got_second[0])
    far_first, far_second = add_low(first[1], got_first[1]), add_low(second[1], got_second[1])
    got_first, got_second = hop(far_first, 4), hop(far_second, 2)
    both = [
        jnp.stack([add_low(near_first[d], got_first[d]), add_low(near_second[d], got_second[d])])
        for d in range(lax.axis_size("grp"))
    ]
    total = both[0].astype(f32)
    for step in range(1, len(both)):
        total = total + shift(both[step], step).astype(f32)
    total = total.astype(keep.dtype)
    bit = 8
    while bit < lax.axis_size("rep"):
        total = add_low(total, hop(total, bit))
        bit *= 2
    return total[0], total[1]


def reduce_blocks(keep, send):
    f32 = jnp.float32
    got = hop(send, 1)
    sums = [add_low(keep[j], got[j]) for j in range(4)]
    across, along, both = hop(sums[2], 2), hop(sums[1], 4), hop(sums[3], 6)
    groups = lax.axis_size("grp")
    parts = [
        (
            sums[0][d].astype(f32)
            + across[d].astype(f32)
            + along[d].astype(f32)
            + both[d].astype(f32)
        ).astype(keep.dtype)
        for d in range(groups)
    ]
    total = parts[0].astype(f32)
    for step in range(1, groups):
        total = total + shift(parts[step], step).astype(f32)
    total = total.astype(keep.dtype)
    bit = 8
    while bit < lax.axis_size("rep"):
        total = add_low(total, hop(total, bit))
        bit *= 2
    return total


def spread_blocks(own):
    near = jnp.stack([own, hop(own, 4), hop(own, 2), hop(own, 6)])
    return near, hop(near, 1)


def rows_of(vector, count):
    short = count * LANES - vector.shape[0]
    return jnp.pad(vector, (0, short)).reshape(count, LANES)


def lined(rows, length):
    return rows.reshape(rows.shape[0], -1)[:, :length].reshape(1, -1)


def place_scalars():
    bit_c, bit_x, bit_y = rep_bits()
    return jnp.stack([lax.axis_index("grp"), bit_c, bit_x, bit_y]).astype(jnp.int32)


def piece_row(where, path, core, high, low, rows):
    high_bit, low_bit = (where[2], where[3]) if path == 0 else (where[3], where[2])
    index = (where[1] ^ core) * 4 + (high_bit ^ high) * 2 + (low_bit ^ low)
    return pl.multiple_of(path * (rows // 2) + index * (rows // 16), 16)


def piece_list():
    return [(p, c, h, l) for p in range(2) for c in range(2) for h in range(2) for l in range(2)]


def dot(one, two, contract=(1, 0)):
    return lax.dot_general(
        one, two, (((contract[0],), (contract[1],)), ((), ())), preferred_element_type=jnp.float32
    )


def pack_first_kernel(where, query, key, value, small, out, blocks):
    shard = query.shape[0]
    whole = jnp.concatenate([query[...], key[...], value[...]], 1)
    for j in range(blocks.shape[0]):
        stop = min((j + 1) * LANES, whole.shape[1])
        blocks[j, :, : stop - j * LANES] = whole[:, j * LANES : stop]
        if stop < (j + 1) * LANES:
            blocks[j, :, stop - j * LANES :] = jnp.zeros(
                (shard, (j + 1) * LANES - stop), whole.dtype
            )
    out[:shard, :] = blocks[where[1] * 4 + where[2] * 2 + where[3]]
    out[shard:, :] = small[...]


def pack_second_kernel(where, gate, up, down, output, out, pack):
    shard, hidden_width = gate.shape
    width = output.shape[1]
    rows = pack.shape[0]
    part = rows // 16
    at = 0
    for weight in (gate, up):
        for j in range(0, hidden_width, LANES):
            pack[at : at + shard, :] = weight[:, j : j + LANES]
            at += shard
    for j in range(0, down.shape[0], LANES):
        pack[at : at + width, :] = (
            down[j : j + LANES, :].astype(jnp.float32).T.astype(pack.dtype)
        )
        at += width
    for j in range(0, width, LANES):
        stop = min(j + LANES, width)
        pack[at : at + shard, : stop - j] = output[:, j:stop]
        if stop < j + LANES:
            pack[at : at + shard, stop - j :] = jnp.zeros((shard, j + LANES - stop), pack.dtype)
        at += shard
    if at < rows:
        pack[at:, :] = jnp.zeros((rows - at, LANES), pack.dtype)
    for path in range(2):
        row = piece_row(where, path, 0, 0, 0, rows)
        out[path] = pack[pl.ds(row, part), :]


def run_pack_first(where, query, key, value, small):
    shard = query.shape[0]
    return pl.pallas_call(
        pack_first_kernel,
        out_shape=shape((shard + SMALL, LANES), query.dtype),
        in_specs=[smem()] + [vmem()] * 4,
        out_specs=vmem(),
        scratch_shapes=[pltpu.VMEM((8, shard, LANES), query.dtype)],
        compiler_params=options(16),
        cost_estimate=cost(0, 1),
        name="pack_first",
    )(where, query, key, value, small)


def run_pack_second(where, gate, up, down, output):
    shard, hidden_width = gate.shape
    width = output.shape[1]
    used = (2 * hidden_width + -(-width // LANES) * LANES) // LANES * shard
    used += down.shape[0] // LANES * width
    rows = -(-used // 256) * 256
    return pl.pallas_call(
        pack_second_kernel,
        out_shape=shape((2, rows // 16, LANES), gate.dtype),
        in_specs=[smem()] + [vmem()] * 4,
        out_specs=vmem(),
        scratch_shapes=[pltpu.VMEM((rows, LANES), gate.dtype)],
        compiler_params=options(16),
        cost_estimate=cost(0, 3),
        name="pack_second",
    )(where, gate, up, down, output)


def block_at(where, core, across, along):
    return (where[1] ^ core) * 4 + (where[2] ^ across) * 2 + (where[3] ^ along)


def unit_heads(raw, head_size):
    pairs = []
    for at in range(0, raw.shape[1], head_size):
        head = raw[:, at : at + head_size]
        factor = lax.rsqrt(jnp.mean(head * head, axis=1, keepdims=True) + NORM_EPS)
        pairs.append((head * factor, factor))
    return pairs


def proj_kernel(sizes, where, near, far, tokens, gain, head_gains, cosine, sine, *refs):
    f32, bf16 = jnp.float32, jnp.bfloat16
    q_width, kv_width, head_size = sizes
    normed_out, raw_out, query_out, kv_out, weights_out, weights, sem = refs
    count, groups, shard, _ = weights.shape
    copies = []
    for core in range(2):
        for across in range(2):
            for along in range(2):
                block = block_at(where, core, across, along)
                for behind in range(groups):
                    pltpu.make_async_copy(
                        (far if core else near).at[across * 2 + along, behind],
                        weights.at[block, lax.rem(where[0] + groups - behind, groups)],
                        sem,
                    ).start()
    inputs = tokens[...].astype(f32)
    scale = lax.rsqrt(jnp.mean(inputs * inputs, axis=1, keepdims=True) + NORM_EPS)
    normed = (inputs * scale * gain[...]).astype(bf16)
    normed_out[...] = normed
    pltpu.make_async_copy(weights, weights, sem).wait()
    flat = jnp.concatenate([weights[j].reshape(groups * shard, LANES) for j in range(count)], 1)
    weights_out[...] = flat
    raw = dot(normed, flat)
    raw_out[...] = raw[:, : q_width + kv_width]
    half = head_size // 2
    cos, sin = cosine[...], sine[...]

    def turn(head):
        one, two = head[:, :half], head[:, half:]
        return jnp.concatenate([one * cos - two * sin, two * cos + one * sin], 1)

    heads = []
    for at, (unit, _) in enumerate(unit_heads(raw[:, : q_width + kv_width], head_size)):
        row = 0 if at * head_size < q_width else 1
        heads.append(turn(unit * head_gains[row : row + 1, :]).astype(bf16))
    queries = jnp.concatenate(heads[: q_width // head_size], 1)
    query_out[...] = (queries.astype(f32) * head_size ** (-0.5)).astype(bf16)
    values = raw[:, q_width + kv_width : q_width + 2 * kv_width].astype(bf16)
    kv_out[...] = jnp.concatenate(heads[q_width // head_size :] + [values], 1)


def run_proj(where, near, far, tokens, gain, head_gains, cosine, sine, sizes):
    f32, bf16 = jnp.float32, jnp.bfloat16
    q_width, kv_width, _ = sizes
    toks, width = tokens.shape
    _, groups, shard, _ = near.shape
    return pl.pallas_call(
        functools.partial(proj_kernel, sizes),
        out_shape=(
            shape((toks, width), bf16),
            shape((toks, q_width + kv_width), f32),
            shape((toks, q_width), bf16),
            shape((toks, 2 * kv_width), bf16),
            shape((width, 8 * LANES), bf16),
        ),
        in_specs=[smem(), hbm(), hbm()] + [vmem()] * 5,
        out_specs=(vmem(),) * 5,
        scratch_shapes=[pltpu.VMEM((8, groups, shard, LANES), bf16), pltpu.SemaphoreType.DMA],
        compiler_params=options(32),
        cost_estimate=cost(2 * toks * width * 1024, 6),
        name="proj",
    )(where, near, far, tokens, gain, head_gains, cosine, sine)


def attend_kernel(sizes, query, own_seg, key_seg, *refs):
    f32, bf16 = jnp.float32, jnp.bfloat16
    q_width, kv_width, head_size = sizes
    held = refs[: len(refs) - 3]
    attended, probs, bias = refs[len(refs) - 3 :]
    toks = query.shape[0]
    same = own_seg[...] == key_seg[...]
    order = lax.broadcasted_iota(jnp.int32, same.shape, 0) - lax.broadcasted_iota(
        jnp.int32, same.shape, 1
    )
    later = lax.broadcasted_iota(jnp.int32, same.shape, 1) >= toks
    bias[...] = jnp.where(same & ((order >= 0) | later), 0.0, -1e30)
    outs = []
    per = q_width // kv_width
    for g in range(kv_width // head_size):
        cols = slice(g * head_size, (g + 1) * head_size)
        keys = jnp.concatenate([kv[:, cols] for kv in held], 0)
        cols = slice(kv_width + g * head_size, kv_width + (g + 1) * head_size)
        values = jnp.concatenate([kv[:, cols] for kv in held], 0)
        for head in range(g * per, (g + 1) * per):
            scores = dot(query[:, head * head_size : (head + 1) * head_size], keys, (1, 1))
            scores = scores + bias[...]
            powers = jnp.exp(scores - jnp.max(scores, axis=1, keepdims=True))
            share = 1.0 / jnp.sum(powers, axis=1, keepdims=True)
            low = (powers * share).astype(bf16)
            probs[head] = low
            outs.append(dot(low, values))
    attended[...] = jnp.concatenate(outs, 1).astype(bf16)


def run_attend(query, own_seg, key_seg, held, sizes):
    bf16 = jnp.bfloat16
    q_width, kv_width, head_size = sizes
    toks = query.shape[0]
    keys = toks * len(held)
    heads = q_width // head_size
    return pl.pallas_call(
        functools.partial(attend_kernel, sizes),
        out_shape=(shape((toks, q_width), bf16), shape((heads, toks, keys), bf16)),
        in_specs=[vmem()] * (3 + len(held)),
        out_specs=(vmem(), vmem()),
        scratch_shapes=[pltpu.VMEM((toks, keys), jnp.float32)],
        compiler_params=options(40),
        cost_estimate=cost(16 * toks * keys * q_width, 8),
        name="attend",
    )(query, own_seg, key_seg, *held)


def attend_back_kernel(sizes, query, grad, probs, *refs):
    f32, bf16 = jnp.float32, jnp.bfloat16
    q_width, kv_width, head_size = sizes
    groups = (len(refs) - 1) // 2
    held = refs[:groups]
    query_grad = refs[groups]
    kv_grads = refs[groups + 1 :]
    toks = query.shape[0]
    per = q_width // kv_width
    query_t = query[...].astype(f32).T.astype(bf16)
    grad_t = grad[...].astype(f32).T.astype(bf16)
    outs, key_parts, value_parts = [], [], []
    for g in range(kv_width // head_size):
        cols = slice(g * head_size, (g + 1) * head_size)
        keys = jnp.concatenate([kv[:, cols] for kv in held], 0)
        cols = slice(kv_width + g * head_size, kv_width + (g + 1) * head_size)
        values = jnp.concatenate([kv[:, cols] for kv in held], 0)
        key_t = value_t = None
        for head in range(g * per, (g + 1) * per):
            cols = slice(head * head_size, (head + 1) * head_size)
            low = probs[head]
            share = low.astype(f32)
            weighed = share * dot(grad[:, cols], values, (1, 1))
            scores = (weighed - share * jnp.sum(weighed, axis=1, keepdims=True)).astype(bf16)
            outs.append(dot(scores, keys))
            key_one = dot(query_t[cols, :], scores)
            value_one = dot(grad_t[cols, :], low)
            key_t = key_one if key_t is None else key_t + key_one
            value_t = value_one if value_t is None else value_t + value_one
        key_parts.append(key_t)
        value_parts.append(value_t)
    query_grad[...] = jnp.concatenate(outs, 1) * head_size ** (-0.5)
    both = jnp.concatenate(key_parts + value_parts, 0)
    for at, out in enumerate(kv_grads):
        out[...] = both[:, at * toks : (at + 1) * toks].T.astype(out.dtype)


def run_attend_back(query, grad, probs, held, sizes):
    f32, bf16 = jnp.float32, jnp.bfloat16
    q_width, kv_width, head_size = sizes
    toks = query.shape[0]
    keys = toks * len(held)
    return pl.pallas_call(
        functools.partial(attend_back_kernel, sizes),
        out_shape=(shape((toks, q_width), f32),)
        + tuple(shape((toks, 2 * kv_width), bf16) for _ in held),
        in_specs=[vmem()] * (3 + len(held)),
        out_specs=(vmem(),) * (1 + len(held)),
        compiler_params=options(48),
        cost_estimate=cost(30 * toks * keys * q_width, 8),
        name="attend_back",
    )(query, grad, probs, *held)


def mlp_kernel(shard, hidden_width, where, *refs):
    f32, bf16 = jnp.float32, jnp.bfloat16
    pieces = refs[:8]
    attended, tokens, out_grad, gain = refs[8:12]
    layer_out, mixed_grad, attended_grad, gain_grad, keep, send = refs[12:18]
    weights, grads, sem_in, sem_out = refs[18:]
    groups, rows, _ = weights.shape
    part = rows // 16
    width = tokens.shape[1]
    for path, core, high, low in piece_list():
        row = piece_row(where, path, core, high, low, rows)
        for behind in range(groups):
            pltpu.make_async_copy(
                pieces[path * 4 + core * 2 + high].at[low, behind],
                weights.at[lax.rem(where[0] + groups - behind, groups), pl.ds(row, part)],
                sem_in,
            ).start()
    out_t = out_grad[...].astype(f32).T.astype(bf16)
    att_t = attended[...].astype(f32).T.astype(bf16)
    pltpu.make_async_copy(weights, weights, sem_in).wait()

    wide = hidden_width // LANES
    down_at = 2 * wide * shard
    own_blocks = wide // groups
    out_at = down_at + own_blocks * width
    out_blocks = -(-width // LANES)
    used = out_at + out_blocks * shard

    def column(at):
        return weights[:, at : at + shard, :].reshape(groups * shard, LANES)

    def store(at, block):
        block = block.astype(bf16)
        for owner in range(groups):
            grads[owner, at : at + shard, :] = block[owner * shard : (owner + 1) * shard]

    if used < rows:
        grads[:, used:, :] = jnp.zeros((groups, rows - used, LANES), bf16)
    output_w = jnp.concatenate(
        [column(out_at + j * shard) for j in range(out_blocks)], 1
    )[:, :width]
    mixed = tokens[...].astype(f32) + dot(attended[...], output_w)
    scale = lax.rsqrt(jnp.mean(mixed * mixed, axis=1, keepdims=True) + NORM_EPS)
    unit = mixed * scale
    gained = gain[...]
    normed = (unit * gained).astype(bf16)
    normed_t = (unit * gained).T.astype(bf16)
    upstream = out_grad[...]
    back = jnp.zeros(mixed.shape, f32)
    ahead = mixed
    step = 2
    for pair in range(0, wide, step):
        some = range(pair, min(pair + step, wide))
        gate_w = jnp.concatenate([column(f * shard) for f in some], 1)
        up_w = jnp.concatenate([column((wide + f) * shard) for f in some], 1)
        down_w = []
        for f in some:
            at = down_at + f % own_blocks * width
            down_w.append(weights[f // own_blocks, at : at + width, :])
        down_w = jnp.concatenate(down_w, 1)
        gate = dot(normed, gate_w)
        up = dot(normed, up_w)
        hidden_grad = dot(upstream, down_w)
        sigmoid = 1.0 / (1.0 + jnp.exp(-gate))
        silu = gate * sigmoid
        hidden = (silu * up).astype(bf16)
        gate_low = (hidden_grad * up * (sigmoid * (1.0 + gate * (1.0 - sigmoid)))).astype(bf16)
        up_low = (hidden_grad * silu).astype(bf16)
        ahead = ahead + dot(hidden, down_w, (1, 1))
        back = back + dot(gate_low, gate_w, (1, 1)) + dot(up_low, up_w, (1, 1))
        gate_wg = dot(normed_t, gate_low)
        up_wg = dot(normed_t, up_low)
        down_wg = dot(out_t, hidden).astype(bf16)
        for at, f in enumerate(some):
            cols = slice(at * LANES, (at + 1) * LANES)
            store(f * shard, gate_wg[:, cols])
            store((wide + f) * shard, up_wg[:, cols])
            down_row = down_at + f % own_blocks * width
            grads[f // own_blocks, down_row : down_row + width, :] = down_wg[:, cols]
    layer_out[...] = ahead.astype(bf16)
    gain_grad[...] = jnp.sum(back * unit, axis=0, keepdims=True)
    inner = back * gained
    through = scale * (inner - unit * jnp.mean(inner * unit, axis=1, keepdims=True))
    mixed_back = upstream.astype(f32) + through
    mixed_grad[...] = mixed_back
    branch = mixed_back.astype(bf16)
    attended_grad[...] = dot(branch, output_w, (1, 1)).astype(bf16)
    output_wg = dot(att_t, branch)
    for j in range(out_blocks):
        block = output_wg[:, j * LANES : min((j + 1) * LANES, width)]
        if block.shape[1] < LANES:
            block = jnp.concatenate(
                [block, jnp.zeros((block.shape[0], LANES - block.shape[1]), f32)], 1
            )
        store(out_at + j * shard, block)
    for path, core, high, low in piece_list():
        row = piece_row(where, path, core, high, low, rows)
        for step in range(groups):
            pltpu.make_async_copy(
                grads.at[lax.rem(where[0] + step, groups), pl.ds(row, part)],
                (send if core else keep).at[path, high, low, step],
                sem_out.at[core],
            ).start()
    pltpu.make_async_copy(keep, keep, sem_out.at[0]).wait()
    pltpu.make_async_copy(send, send, sem_out.at[1]).wait()


def run_mlp(pieces, attended, tokens, out_grad, gain, hidden_width):
    f32, bf16 = jnp.float32, jnp.bfloat16
    groups = lax.axis_size("grp")
    toks, width = tokens.shape
    part = pieces[0].shape[2]
    rows = part * 16
    packed = shape((2, 2, 2, groups, part, LANES), bf16)
    return pl.pallas_call(
        functools.partial(mlp_kernel, width // groups, hidden_width),
        out_shape=(
            shape((toks, width), bf16),
            shape((toks, width), f32),
            shape((toks, width), bf16),
            shape((1, width), f32),
            packed,
            packed,
        ),
        in_specs=[smem()] + [hbm()] * 8 + [vmem()] * 4,
        out_specs=(vmem(),) * 4 + (hbm(),) * 2,
        scratch_shapes=[
            pltpu.VMEM((groups, rows, LANES), bf16),
            pltpu.VMEM((groups, rows, LANES), bf16),
            pltpu.SemaphoreType.DMA,
            pltpu.SemaphoreType.DMA((2,)),
        ],
        compiler_params=pltpu.CompilerParams(vmem_limit_bytes=48 * 1024 * 1024),
        cost_estimate=pl.CostEstimate(
            flops=18 * toks * width * hidden_width, bytes_accessed=26 * 1024 * 1024, transcendentals=0
        ),
        name="mlp",
    )(place_scalars(), *pieces, attended, tokens, out_grad, gain)


def last_kernel(sizes, where, query_grad, raw, normed, tokens, mixed_grad, gain, head_gains, cosine, sine, weights, second, *refs):
    f32, bf16 = jnp.float32, jnp.bfloat16
    q_width, kv_width, head_size = sizes
    kv_parts = refs[: len(refs) - 5]
    token_grad, keep, send, grads, sem = refs[len(refs) - 5 :]
    count, groups, rows, _ = grads.shape
    width = tokens.shape[1]
    shard = width // groups
    half = head_size // 2
    cos, sin = cosine[...], sine[...]
    kv_grad = kv_parts[0][...].astype(f32)
    for part in kv_parts[1:]:
        kv_grad = kv_grad + part[...].astype(f32)
    lows, head_sums = [], [jnp.zeros((1, head_size), f32)] * 2
    for at, (unit, factor) in enumerate(unit_heads(raw[...], head_size)):
        kind = 0 if at * head_size < q_width else 1
        source, place = (query_grad, at * head_size) if kind == 0 else (kv_grad, at * head_size - q_width)
        one = source[:, place : place + half]
        two = source[:, place + half : place + head_size]
        back = jnp.concatenate([one * cos + two * sin, two * cos - one * sin], 1)
        head_sums[kind] = head_sums[kind] + jnp.sum(back * unit, axis=0, keepdims=True)
        inner = back * head_gains[kind : kind + 1, :]
        lows.append(factor * (inner - unit * jnp.mean(inner * unit, axis=1, keepdims=True)))
    lows.append(kv_grad[:, kv_width:])
    short = count * LANES - q_width - 2 * kv_width
    if short:
        lows.append(jnp.zeros((tokens.shape[0], short), f32))
    low = jnp.concatenate(lows, 1).astype(bf16)
    back = dot(low, weights[...], (1, 1))
    inputs = tokens[...].astype(f32)
    scale = lax.rsqrt(jnp.mean(inputs * inputs, axis=1, keepdims=True) + NORM_EPS)
    unit = inputs * scale
    first = jnp.sum(back * unit, axis=0, keepdims=True)
    inner = back * gain[...]
    token_grad[...] = mixed_grad[...] + scale * (
        inner - unit * jnp.mean(inner * unit, axis=1, keepdims=True)
    )
    normed_t = normed[...].astype(f32).T.astype(bf16)
    products = dot(normed_t, low).astype(bf16)
    for j in range(count):
        for owner in range(groups):
            grads[j, owner, :shard, :] = products[
                owner * shard : (owner + 1) * shard, j * LANES : (j + 1) * LANES
            ]
            grads[j, owner, shard:, :] = jnp.zeros((rows - shard, LANES), bf16)

    def line(vector):
        short = LANES - vector.shape[1]
        return jnp.concatenate([vector, jnp.zeros((1, short), f32)], 1) if short else vector

    head_part = head_size // groups
    for owner in range(groups):
        lines = []
        for vector in (first, second[...]):
            mine = vector[:, owner * shard : (owner + 1) * shard]
            lines += [line(mine[:, at : at + LANES]) for at in range(0, shard, LANES)]
        for vector in head_sums:
            lines.append(line(vector[:, owner * head_part : (owner + 1) * head_part]))
        lines.append(jnp.zeros((rows - shard - len(lines), LANES), f32))
        grads[0, owner, shard:, :] = jnp.concatenate(lines, 0).astype(bf16)
    for core in range(2):
        for across in range(2):
            for along in range(2):
                block = block_at(where, core, across, along)
                for step in range(groups):
                    pltpu.make_async_copy(
                        grads.at[block, lax.rem(where[0] + step, groups)],
                        (send if core else keep).at[across * 2 + along, step],
                        sem.at[core],
                    ).start()
    pltpu.make_async_copy(keep, keep, sem.at[0]).wait()
    pltpu.make_async_copy(send, send, sem.at[1]).wait()


def run_last(where, query_grad, raw, normed, tokens, mixed_grad, gain, head_gains, cosine, sine, weights, second, kv_parts, sizes):
    f32, bf16 = jnp.float32, jnp.bfloat16
    toks, width = tokens.shape
    groups = lax.axis_size("grp")
    rows = width // groups + SMALL
    packed = shape((4, groups, rows, LANES), bf16)
    return pl.pallas_call(
        functools.partial(last_kernel, sizes),
        out_shape=(shape((toks, width), f32), packed, packed),
        in_specs=[smem()] + [vmem()] * (11 + len(kv_parts)),
        out_specs=(vmem(), hbm(), hbm()),
        scratch_shapes=[
            pltpu.VMEM((8, groups, rows, LANES), bf16),
            pltpu.SemaphoreType.DMA((2,)),
        ],
        compiler_params=options(40),
        cost_estimate=cost(4 * toks * width * 1024, 8),
        name="last",
    )(where, query_grad, raw, normed, tokens, mixed_grad, gain, head_gains, cosine, sine, weights, second, *kv_parts)


def unpack_late_kernel(sizes, where, near, far, query, key, value, first, second, query_gain, key_gain, blocks, sem):
    f32 = jnp.float32
    q_width, kv_width, _ = sizes
    for core in range(2):
        for across in range(2):
            for along in range(2):
                pltpu.make_async_copy(
                    (far if core else near).at[across * 2 + along],
                    blocks.at[block_at(where, core, across, along)],
                    sem,
                ).start()
    pltpu.make_async_copy(blocks, blocks, sem).wait()
    shard = query.shape[0]
    whole = jnp.concatenate([blocks[j, :shard, :] for j in range(blocks.shape[0])], 1).astype(f32)
    query[...] = whole[:, :q_width]
    key[...] = whole[:, q_width : q_width + kv_width]
    value[...] = whole[:, q_width + kv_width : q_width + 2 * kv_width]
    lines = blocks[0, shard:, :].astype(f32)
    row = 0
    for out in (first, second, query_gain, key_gain):
        for at in range(0, out.shape[1], LANES):
            stop = min(at + LANES, out.shape[1])
            out[:, at:stop] = lines[row : row + 1, : stop - at]
            row += 1


def run_unpack_late(where, near, far, sizes, shard, head_part):
    f32 = jnp.float32
    q_width, kv_width, _ = sizes
    return pl.pallas_call(
        functools.partial(unpack_late_kernel, sizes),
        out_shape=(
            shape((shard, q_width), f32),
            shape((shard, kv_width), f32),
            shape((shard, kv_width), f32),
            shape((1, shard), f32),
            shape((1, shard), f32),
            shape((1, head_part), f32),
            shape((1, head_part), f32),
        ),
        in_specs=[smem(), hbm(), hbm()],
        out_specs=(vmem(),) * 7,
        scratch_shapes=[pltpu.VMEM((8,) + near.shape[1:], near.dtype), pltpu.SemaphoreType.DMA],
        compiler_params=options(16),
        cost_estimate=cost(0, 2),
        name="unpack_late",
    )(where, near, far)


def unpack_kernel(shard, hidden_width, where, *refs):
    f32 = jnp.float32
    pieces = refs[:8]
    gate, up, down, output = refs[8:12]
    pack, sem = refs[12:]
    rows = pack.shape[0]
    part = rows // 16
    for path, core, high, low in piece_list():
        row = piece_row(where, path, core, high, low, rows)
        pltpu.make_async_copy(
            pieces[path * 4 + core * 2 + high].at[low], pack.at[pl.ds(row, part)], sem
        ).start()
    pltpu.make_async_copy(pack, pack, sem).wait()
    wide = hidden_width // LANES
    width = output.shape[1]
    for f in range(wide):
        gate[:, f * LANES : (f + 1) * LANES] = pack[f * shard : (f + 1) * shard].astype(f32)
        up[:, f * LANES : (f + 1) * LANES] = pack[
            (wide + f) * shard : (wide + f + 1) * shard
        ].astype(f32)
    at = 2 * wide * shard
    for j in range(down.shape[0] // LANES):
        down[j * LANES : (j + 1) * LANES, :] = pack[at : at + width].astype(f32).T
        at += width
    for j in range(0, width, LANES):
        stop = min(j + LANES, width)
        output[:, j:stop] = pack[at : at + shard].astype(f32)[:, : stop - j]
        at += shard


def run_unpack(pieces, shard, width, hidden_width, own_hidden):
    f32 = jnp.float32
    rows = pieces[0].shape[1] * 16
    return pl.pallas_call(
        functools.partial(unpack_kernel, shard, hidden_width),
        out_shape=(
            shape((shard, hidden_width), f32),
            shape((shard, hidden_width), f32),
            shape((own_hidden, width), f32),
            shape((shard, width), f32),
        ),
        in_specs=[smem()] + [hbm()] * 8,
        out_specs=(vmem(),) * 4,
        scratch_shapes=[pltpu.VMEM((rows, LANES), jnp.bfloat16), pltpu.SemaphoreType.DMA],
        compiler_params=pltpu.CompilerParams(vmem_limit_bytes=24 * 1024 * 1024),
        cost_estimate=pl.CostEstimate(flops=0, bytes_accessed=6 * 1024 * 1024, transcendentals=0),
        name="unpack",
    )(place_scalars(), *pieces)


def body(
    tokens,
    segments,
    out_grad,
    norm_gain,
    query_gain,
    key_gain,
    query_weight,
    key_weight,
    value_weight,
    output_weight,
    second_gain,
    gate_weight,
    up_weight,
    down_weight,
):
    f32, bf16 = jnp.float32, jnp.bfloat16
    groups = lax.axis_size("grp")
    place_z = lax.axis_index("grp")
    where = place_scalars()
    toks, width = tokens.shape
    shard = norm_gain.shape[0]
    head_part = query_gain.shape[0]
    head_size = head_part * groups
    hidden_width = gate_weight.shape[1]
    sizes = (query_weight.shape[1], key_weight.shape[1], head_size)

    gain_rows = -(-shard // LANES)
    seg_rows = -(-toks // LANES)
    small = jnp.concatenate(
        [
            rows_of(norm_gain, gain_rows),
            rows_of(second_gain, gain_rows),
            rows_of(query_gain, 1),
            rows_of(key_gain, 1),
            rows_of(segments.astype(bf16), seg_rows),
        ]
    )
    small = jnp.pad(small, ((0, SMALL - small.shape[0]), (0, 0)))
    own_first = run_pack_first(where, query_weight, key_weight, value_weight, small)
    first_z = [own_first] + [shift(own_first, step) for step in range(1, groups)]
    own_second = run_pack_second(where, gate_weight, up_weight, down_weight, output_weight)
    second_z = [own_second] + [shift(own_second, step) for step in range(1, groups)]
    near, far = spread_blocks(jnp.stack([held[:shard] for held in first_z]))

    small_behind = jnp.stack([held[shard:] for held in first_z]).astype(f32)
    small_all = small_behind[lax.rem(place_z + groups - jnp.arange(groups), groups)]
    at = 0
    gains = []
    for count, length in ((gain_rows, shard), (gain_rows, shard), (1, head_part), (1, head_part)):
        gains.append(lined(small_all[:, at : at + count], length))
        at += count
    gain_first, gain_second, gain_query, gain_key = gains
    head_gains = jnp.concatenate([gain_query, gain_key])
    segs = small_behind[:, at : at + seg_rows].reshape(groups, -1)[:, :toks]
    there = (place_z >= jnp.arange(groups))[:, None]
    key_seg = jnp.where(there, segs, -1.0).reshape(1, -1)
    own_seg = segs[0][:, None]
    earlier = ((key_seg < own_seg) & (key_seg >= 0.0)).astype(jnp.int32)
    positions = place_z * toks + jnp.arange(toks, dtype=jnp.int32) - jnp.sum(earlier, axis=1)
    half = head_size // 2
    inverse = ROPE_BASE ** (-(jnp.arange(half, dtype=f32) * 2.0 / head_size))
    angles = positions.astype(f32)[:, None] * inverse[None, :]
    cosine, sine = jnp.cos(angles), jnp.sin(angles)

    second_z, near, far = lax.optimization_barrier((second_z, near, far))
    pieces = spread_pieces(
        jnp.stack([held[0] for held in second_z]), jnp.stack([held[1] for held in second_z])
    )
    normed, raw, query, key_value, proj_weights = run_proj(
        where, near, far, tokens, gain_first, head_gains, cosine, sine, sizes
    )
    held = [key_value]
    for step in range(1, groups):
        ahead = [(i, i + step) for i in range(groups - step)]
        held.append(lax.ppermute(key_value, "grp", ahead))
    attended, probs = run_attend(query, own_seg, key_seg, held, sizes)
    layer_out, mixed_grad, attended_grad, second_sum, keep, send = run_mlp(
        pieces, attended, tokens, out_grad, gain_second, hidden_width
    )
    early = spread_pieces(*reduce_pieces(keep, send))
    query_grad, *kv_parts = run_attend_back(query, attended_grad, probs, held, sizes)
    kv_back = [kv_parts[0]]
    for step in range(1, groups):
        behind = [(i + step, i) for i in range(groups - step)]
        kv_back.append(lax.ppermute(kv_parts[step], "grp", behind))
    token_grad, late_keep, late_send = run_last(
        where, query_grad, raw, normed, tokens, mixed_grad, gain_first, head_gains, cosine, sine,
        proj_weights, second_sum, kv_back, sizes,
    )
    late = spread_blocks(reduce_blocks(late_keep, late_send))
    gate_sum, up_sum, down_sum, output_sum = run_unpack(
        early, shard, width, hidden_width, down_weight.shape[0]
    )
    query_sum, key_sum, value_sum, first_sum, second_sum, query_gsum, key_gsum = run_unpack_late(
        where, *late, sizes, shard, head_part
    )
    return (
        layer_out,
        token_grad,
        first_sum.reshape(-1),
        query_gsum.reshape(-1),
        key_gsum.reshape(-1),
        query_sum,
        key_sum,
        value_sum,
        output_sum,
        second_sum.reshape(-1),
        gate_sum,
        up_sum,
        down_sum,
    )


def solution(mesh):
    placed = (
        P(("rep", "grp"), None),
        P(("rep", "grp")),
        P(("rep", "grp"), None),
        P("grp"),
        P("grp"),
        P("grp"),
        P("grp", None),
        P("grp", None),
        P("grp", None),
        P("grp", None),
        P("grp"),
        P("grp", None),
        P("grp", None),
        P("grp", None),
    )
    return jax.shard_map(
        body,
        mesh=mesh,
        in_specs=placed,
        out_specs=(
            P(("rep", "grp"), None),
            P(("rep", "grp"), None),
            P("grp"),
            P("grp"),
            P("grp"),
            P("grp", None),
            P("grp", None),
            P("grp", None),
            P("grp", None),
            P("grp"),
            P("grp", None),
            P("grp", None),
            P("grp", None),
        ),
        check_vma=False,
    )
```

```python
import functools

import jax
import jax.numpy as jnp
from jax import lax
from jax.experimental import pallas as pl
from jax.experimental.pallas import tpu as pltpu
from jax.sharding import PartitionSpec as P

NORM_EPS = 1e-05
ROPE_BASE = 100000.0
LANES = 128
SMALL = 16
MIB = 1024 * 1024
BIG = 58


def vmem():
    return pl.BlockSpec(memory_space=pltpu.VMEM)


def smem():
    return pl.BlockSpec(memory_space=pltpu.SMEM)


def hbm():
    return pl.BlockSpec(memory_space=pl.ANY)


def shape(dims, kind):
    return jax.ShapeDtypeStruct(dims, kind)


def options(mebibytes):
    return pltpu.CompilerParams(vmem_limit_bytes=mebibytes * MIB)


def cost():
    return pl.CostEstimate(flops=1, bytes_accessed=1024, transcendentals=0)


class Staged:
    def __init__(self, source, target, sem):
        self.copy = pltpu.make_async_copy(source, target, sem)
        self.copy.start()
        self.target, self.waiting = target, True
        self.shape, self.dtype = target.shape, target.dtype

    def wait(self):
        if self.waiting:
            self.copy.wait()
            self.waiting = False

    def __getitem__(self, index):
        self.wait()
        return self.target[index]


def staged_call(kernel, name, where, operands, held, out_shape, out_specs, scratch, mebibytes):
    count = len(operands)

    def whole(where_ref, *refs):
        sources, refs = refs[:count], refs[count:]
        targets, sems = refs[len(refs) - count - 1 : -1], refs[-1]
        rest = refs[: len(refs) - count - 1]
        staged = [
            Staged(source, target, sems.at[at])
            for at, (source, target) in enumerate(zip(sources, targets))
        ]
        kernel(where_ref, *staged, *rest)
        for operand in staged:
            operand.wait()

    return pl.pallas_call(
        whole,
        out_shape=out_shape,
        in_specs=[smem()] + [hbm()] * (count + len(held)),
        out_specs=out_specs,
        scratch_shapes=list(scratch)
        + [pltpu.VMEM(operand.shape, operand.dtype) for operand in operands]
        + [pltpu.SemaphoreType.DMA((count,))],
        compiler_params=options(mebibytes),
        cost_estimate=cost(),
        name=name,
    )(where, *operands, *held)


def hop(value, bit):
    count = lax.axis_size("rep")
    return lax.ppermute(value, "rep", [(i, i ^ bit) for i in range(count)])


def shift(value, step):
    count = lax.axis_size("grp")
    return lax.ppermute(value, "grp", [(i, (i + step) % count) for i in range(count)])


def rep_bits():
    index = lax.axis_index("rep")
    return index & 1, (index >> 1) & 1, (index >> 2) & 1


def hop_split(value, even, odd):
    count = lax.axis_size("rep")
    return lax.ppermute(value, "rep", [(i, i ^ (odd if i % 2 else even)) for i in range(count)])


def add_low(one, two):
    return (one.astype(jnp.float32) + two.astype(jnp.float32)).astype(one.dtype)


def fold_grp(parts):
    f32 = jnp.float32
    total = parts[0].astype(f32)
    for step in range(1, len(parts)):
        total = total + shift(parts[step], step).astype(f32)
    total = total.astype(parts[0].dtype)
    bit = 8
    while bit < lax.axis_size("rep"):
        total = add_low(total, hop(total, bit))
        bit *= 2
    return total


def fold_blocks(keep, send):
    f32 = jnp.float32
    got = hop(send, 1)
    sums = [add_low(keep[j], got[j]) for j in range(4)]
    across, along, both = hop(sums[2], 2), hop(sums[1], 4), hop(sums[3], 6)
    return [
        (
            sums[0][d].astype(f32)
            + across[d].astype(f32)
            + along[d].astype(f32)
            + both[d].astype(f32)
        ).astype(keep.dtype)
        for d in range(lax.axis_size("grp"))
    ]


def spread_blocks(own):
    near = jnp.stack([own, hop(own, 4), hop(own, 2), hop(own, 6)])
    return near, hop(near, 1)


def rows_of(vector, count):
    short = count * LANES - vector.shape[0]
    return jnp.pad(vector, (0, short)).reshape(count, LANES)


def lined(rows, length):
    return rows.reshape(rows.shape[0], -1)[:, :length].reshape(1, -1)


def place_scalars():
    bit_c, bit_x, bit_y = rep_bits()
    return jnp.stack([lax.axis_index("grp"), bit_c, bit_x, bit_y]).astype(jnp.int32)


def piece_row(where, core, high, low, rows):
    owner = where[1] ^ core
    first = jnp.where(owner == 0, where[2], where[3])
    second = jnp.where(owner == 0, where[3], where[2])
    index = owner * 4 + (first ^ high) * 2 + (second ^ low)
    return pl.multiple_of(index * (rows // 8), 16)


def piece_list():
    return [(c, h, l) for c in range(2) for h in range(2) for l in range(2)]


def dot(one, two, contract=(1, 0)):
    return lax.dot_general(
        one, two, (((contract[0],), (contract[1],)), ((), ())), preferred_element_type=jnp.float32
    )


def turned(value):
    return value.astype(jnp.float32).T.astype(value.dtype)


class Chunk:
    def __init__(self, dims, shares, has_out):
        self.shard, self.width, self.own, self.groups = dims
        self.shares, self.has_out = tuple(shares), has_out
        self.out_blocks = -(-self.width // LANES)
        self.rows_at, at = {}, 0
        if has_out:
            for j in range(self.out_blocks):
                self.rows_at["out", j] = at
                at += self.shard
        for share in self.shares:
            for kind in ("gate", "up"):
                for f in self.blocks(share):
                    self.rows_at[kind, f] = at
                    at += self.shard
            self.rows_at["down", share] = at
            at += self.width
        self.used = at
        self.rows = -(-at // 128) * 128
        self.part = self.rows // 8

    def blocks(self, share):
        return [owner * self.own + share for owner in range(self.groups)]


def chunks_of(shard, width, own_hidden, groups):
    own = own_hidden // LANES
    whole = (Chunk((shard, width, own, groups), range(own), True),)
    return whole, whole


def pack_first_kernel(where, query, key, value, small, out, blocks):
    shard = query.shape[0]
    whole = jnp.concatenate([query[...], key[...], value[...]], 1)
    for j in range(blocks.shape[0]):
        stop = min((j + 1) * LANES, whole.shape[1])
        blocks[j, :, : stop - j * LANES] = whole[:, j * LANES : stop]
        if stop < (j + 1) * LANES:
            blocks[j, :, stop - j * LANES :] = jnp.zeros(
                (shard, (j + 1) * LANES - stop), whole.dtype
            )
    out[:shard, :] = blocks[where[1] * 4 + where[2] * 2 + where[3]]
    out[shard:, :] = small[...]


def pack_second_kernel(chunks, where, gate, up, down_t, output, *refs):
    outs, packs = refs[: len(chunks)], refs[len(chunks) :]
    for chunk, out, pack in zip(chunks, outs, packs):
        shard, width = chunk.shard, chunk.width
        for (kind, j), at in chunk.rows_at.items():
            if kind == "down":
                pack[at : at + width, :] = down_t[:, j * LANES : (j + 1) * LANES]
                continue
            source = {"gate": gate, "up": up, "out": output}[kind]
            stop = min((j + 1) * LANES, source.shape[1])
            pack[at : at + shard, : stop - j * LANES] = source[:, j * LANES : stop]
            if stop < (j + 1) * LANES:
                pack[at : at + shard, stop - j * LANES :] = jnp.zeros(
                    (shard, (j + 1) * LANES - stop), pack.dtype
                )
        if chunk.used < chunk.rows:
            pack[chunk.used :, :] = jnp.zeros((chunk.rows - chunk.used, LANES), pack.dtype)
        row = piece_row(where, 0, 0, 0, chunk.rows)
        out[...] = pack[pl.ds(row, chunk.part), :]


def run_pack_first(where, query, key, value, small):
    shard = query.shape[0]
    return staged_call(
        pack_first_kernel,
        "pack_first",
        where,
        (query, key, value, small),
        (),
        shape((shard + SMALL, LANES), query.dtype),
        vmem(),
        [pltpu.VMEM((8, shard, LANES), query.dtype)],
        BIG,
    )


def run_pack_second(where, chunks, gate, up, down_t, output):
    kind = gate.dtype
    return staged_call(
        functools.partial(pack_second_kernel, chunks),
        "pack_second",
        where,
        (gate, up, down_t, output),
        (),
        tuple(shape((chunk.part, LANES), kind) for chunk in chunks),
        (vmem(),) * len(chunks),
        [pltpu.VMEM((chunk.rows, LANES), kind) for chunk in chunks],
        BIG,
    )


def block_at(where, core, across, along):
    return (where[1] ^ core) * 4 + (where[2] ^ across) * 2 + (where[3] ^ along)


def unit_heads(raw, head_size):
    pairs = []
    for at in range(0, raw.shape[1], head_size):
        head = raw[:, at : at + head_size]
        factor = lax.rsqrt(jnp.mean(head * head, axis=1, keepdims=True) + NORM_EPS)
        pairs.append((head * factor, factor))
    return pairs


def proj_kernel(sizes, where, near, far, tokens_t, gain, head_gains, cosine, sine, *refs):
    f32, bf16 = jnp.float32, jnp.bfloat16
    q_width, kv_width, head_size = sizes
    normed_out, raw_out, query_out, kv_out, weights_out = refs
    groups = near.shape[1]
    inputs = tokens_t[...].astype(f32).T
    scale = lax.rsqrt(jnp.mean(inputs * inputs, axis=1, keepdims=True) + NORM_EPS)
    normed = (inputs * scale * gain[...]).astype(bf16)
    normed_out[...] = normed
    for j in range(8):
        core, across, along = j // 4, j // 2 % 2, j % 2
        place = (where[2] ^ across) * 2 + (where[3] ^ along)
        pieces = []
        for owner in range(groups):
            behind = lax.rem(where[0] + groups - owner, groups)
            pieces.append(
                jnp.where(where[1] == core, near[place, behind], far[place, behind])
            )
        weights_out[:, j * LANES : (j + 1) * LANES] = jnp.concatenate(pieces, 0)
    flat = weights_out[...]
    raw = dot(normed, flat)
    raw_out[...] = raw[:, : q_width + kv_width]
    half = head_size // 2
    cos, sin = cosine[...], sine[...]

    def turn(head):
        one, two = head[:, :half], head[:, half:]
        return jnp.concatenate([one * cos - two * sin, two * cos + one * sin], 1)

    heads = []
    for at, (unit, _) in enumerate(unit_heads(raw[:, : q_width + kv_width], head_size)):
        row = 0 if at * head_size < q_width else 1
        heads.append(turn(unit * head_gains[row : row + 1, :]).astype(bf16))
    queries = jnp.concatenate(heads[: q_width // head_size], 1)
    query_out[...] = (queries.astype(f32) * head_size ** (-0.5)).astype(bf16)
    values = raw[:, q_width + kv_width : q_width + 2 * kv_width].astype(bf16)
    kv_out[...] = jnp.concatenate(heads[q_width // head_size :] + [values], 1)


def run_proj(where, near, far, tokens_t, gain, head_gains, cosine, sine, sizes):
    f32, bf16 = jnp.float32, jnp.bfloat16
    q_width, kv_width, _ = sizes
    width, toks = tokens_t.shape
    return pl.pallas_call(
        functools.partial(proj_kernel, sizes),
        out_shape=(
            shape((toks, width), bf16),
            shape((toks, q_width + kv_width), f32),
            shape((toks, q_width), bf16),
            shape((toks, 2 * kv_width), bf16),
            shape((width, 8 * LANES), bf16),
        ),
        in_specs=[smem()] + [vmem()] * 7,
        out_specs=(vmem(),) * 5,
        compiler_params=options(24),
        cost_estimate=cost(),
        name="proj",
    )(where, near, far, tokens_t, gain, head_gains, cosine, sine)


def attend_kernel(sizes, where, query, own_seg, key_seg, *refs):
    f32, bf16 = jnp.float32, jnp.bfloat16
    q_width, kv_width, head_size = sizes
    held = refs[: len(refs) - 5]
    attended, probs_out, bias, probs, sems = refs[len(refs) - 5 :]
    toks = query.shape[0]
    same = own_seg[...] == key_seg[...]
    order = lax.broadcasted_iota(jnp.int32, same.shape, 0) - lax.broadcasted_iota(
        jnp.int32, same.shape, 1
    )
    later = lax.broadcasted_iota(jnp.int32, same.shape, 1) >= toks
    bias[...] = jnp.where(same & ((order >= 0) | later), 0.0, -1e30)
    outs = []
    per = q_width // kv_width
    for g in range(kv_width // head_size):
        cols = slice(g * head_size, (g + 1) * head_size)
        keys = jnp.concatenate([kv[:, cols] for kv in held], 0)
        cols = slice(kv_width + g * head_size, kv_width + (g + 1) * head_size)
        values = jnp.concatenate([kv[:, cols] for kv in held], 0)
        for head in range(g * per, (g + 1) * per):
            scores = dot(query[:, head * head_size : (head + 1) * head_size], keys, (1, 1))
            scores = scores + bias[...]
            powers = jnp.exp(scores - jnp.max(scores, axis=1, keepdims=True))
            share = 1.0 / jnp.sum(powers, axis=1, keepdims=True)
            low = (powers * share).astype(bf16)
            probs[head] = low
            pltpu.make_async_copy(probs.at[head], probs_out.at[head], sems.at[head]).start()
            outs.append(dot(low, values))
    attended[...] = jnp.concatenate(outs, 1).astype(bf16)
    for head in range(probs.shape[0]):
        pltpu.make_async_copy(probs.at[head], probs_out.at[head], sems.at[head]).wait()


def run_attend(where, query, own_seg, key_seg, held, sizes):
    bf16 = jnp.bfloat16
    q_width, kv_width, head_size = sizes
    toks = query.shape[0]
    keys = toks * len(held)
    heads = q_width // head_size
    return staged_call(
        functools.partial(attend_kernel, sizes),
        "attend",
        where,
        (query, own_seg, key_seg, *held),
        (),
        (shape((toks, q_width), bf16), shape((heads, toks, keys), bf16)),
        (vmem(), hbm()),
        [
            pltpu.VMEM((toks, keys), jnp.float32),
            pltpu.VMEM((heads, toks, keys), bf16),
            pltpu.SemaphoreType.DMA((heads,)),
        ],
        BIG,
    )


def attend_back_kernel(sizes, where, query, grad, *refs):
    f32, bf16 = jnp.float32, jnp.bfloat16
    q_width, kv_width, head_size = sizes
    probs, sems = refs[-2:]
    refs = refs[:-2]
    groups = (len(refs) - 2) // 2
    probs_in = refs[groups]
    refs = refs[:groups] + refs[groups + 1 :]
    copies = [
        pltpu.make_async_copy(probs_in.at[head], probs.at[head], sems.at[head])
        for head in range(probs.shape[0])
    ]
    for copy in copies:
        copy.start()
    held = refs[:groups]
    query_grad = refs[groups]
    kv_grads = refs[groups + 1 :]
    toks = query.shape[0]
    per = q_width // kv_width
    query_t = query[...].astype(f32).T.astype(bf16)
    grad_t = grad[...].astype(f32).T.astype(bf16)
    outs, key_parts, value_parts = [], [], []
    for g in range(kv_width // head_size):
        cols = slice(g * head_size, (g + 1) * head_size)
        keys = jnp.concatenate([kv[:, cols] for kv in held], 0)
        cols = slice(kv_width + g * head_size, kv_width + (g + 1) * head_size)
        values = jnp.concatenate([kv[:, cols] for kv in held], 0)
        key_t = value_t = None
        for head in range(g * per, (g + 1) * per):
            cols = slice(head * head_size, (head + 1) * head_size)
            copies[head].wait()
            low = probs[head]
            share = low.astype(f32)
            weighed = share * dot(grad[:, cols], values, (1, 1))
            scores = (weighed - share * jnp.sum(weighed, axis=1, keepdims=True)).astype(bf16)
            outs.append(dot(scores, keys))
            key_one = dot(query_t[cols, :], scores)
            value_one = dot(grad_t[cols, :], low)
            key_t = key_one if key_t is None else key_t + key_one
            value_t = value_one if value_t is None else value_t + value_one
        key_parts.append(key_t)
        value_parts.append(value_t)
    query_grad[...] = jnp.concatenate(outs, 1) * head_size ** (-0.5)
    both = jnp.concatenate(key_parts + value_parts, 0)
    for at, out in enumerate(kv_grads):
        out[...] = both[:, at * toks : (at + 1) * toks].T.astype(out.dtype)


def run_attend_back(where, query, grad, probs, held, sizes):
    f32, bf16 = jnp.float32, jnp.bfloat16
    q_width, kv_width, head_size = sizes
    toks = query.shape[0]
    keys = toks * len(held)
    return staged_call(
        functools.partial(attend_back_kernel, sizes),
        "attend_back",
        where,
        (query, grad, *held),
        (probs,),
        (shape((toks, q_width), f32),) + tuple(shape((toks, 2 * kv_width), bf16) for _ in held),
        (vmem(),) * (1 + len(held)),
        [pltpu.VMEM(probs.shape, bf16), pltpu.SemaphoreType.DMA((probs.shape[0],))],
        BIG,
    )


def mlp_kernel(w_chunks, g_chunks, where, *refs):
    f32, bf16 = jnp.float32, jnp.bfloat16
    count = 4 * len(w_chunks)
    attended, tokens_t, out_grad_t, gain = refs[:4]
    pieces = refs[4 : count + 4]
    refs = refs[count + 4 :]
    layer_out_t, mixed_grad, attended_grad, gain_grad = refs[:4]
    packed, refs = refs[4 : 4 + 2 * len(g_chunks)], refs[4 + 2 * len(g_chunks) :]
    weights, refs = refs[: len(w_chunks)], refs[len(w_chunks) :]
    grads, (sem_in, sem_out) = refs[: len(g_chunks)], refs[len(g_chunks) :]
    width, toks = tokens_t.shape
    shard, groups, out_blocks = w_chunks[0].shard, w_chunks[0].groups, w_chunks[0].out_blocks
    for number, chunk in enumerate(w_chunks):
        for core, high, low in piece_list():
            row = piece_row(where, core, high, low, chunk.rows)
            for behind in range(groups):
                pltpu.make_async_copy(
                    pieces[number * 4 + core * 2 + high].at[low, behind],
                    weights[number].at[
                        lax.rem(where[0] + groups - behind, groups), pl.ds(row, chunk.part)
                    ],
                    sem_in.at[number],
                ).start()

    def leave(number):
        chunk = g_chunks[number]
        keep, send = packed[2 * number : 2 * number + 2]
        for core, high, low in piece_list():
            row = piece_row(where, core, high, low, chunk.rows)
            for step in range(groups):
                pltpu.make_async_copy(
                    grads[number].at[lax.rem(where[0] + step, groups), pl.ds(row, chunk.part)],
                    (send if core else keep).at[high, low, step],
                    sem_out.at[number, core],
                ).start()

    def column(number, kind, f):
        at = w_chunks[number].rows_at[kind, f]
        return weights[number][:, at : at + shard, :].reshape(groups * shard, LANES)

    def store(number, kind, f, block):
        at = g_chunks[number].rows_at[kind, f]
        for owner in range(groups):
            grads[number][owner, at : at + shard, :] = block[owner * shard : (owner + 1) * shard]

    out_t = out_grad_t[...]
    upstream = turned(out_t)
    inputs = tokens_t[...].astype(f32).T
    att_t = turned(attended[...])
    for number, chunk in enumerate(g_chunks):
        if chunk.used < chunk.rows:
            grads[number][:, chunk.used :, :] = jnp.zeros(
                (groups, chunk.rows - chunk.used, LANES), bf16
            )
    waited = 0

    def need(number):
        nonlocal waited
        while waited <= number:
            pltpu.make_async_copy(weights[waited], weights[waited], sem_in.at[waited]).wait()
            waited += 1

    need(0)
    output_w = jnp.concatenate([column(0, "out", j) for j in range(out_blocks)], 1)[:, :width]
    mixed = inputs + dot(attended[...], output_w)
    scale = lax.rsqrt(jnp.mean(mixed * mixed, axis=1, keepdims=True) + NORM_EPS)
    unit = mixed * scale
    gained = gain[...]
    normed = (unit * gained).astype(bf16)
    normed_t = turned(normed)
    back = jnp.zeros(mixed.shape, f32)
    ahead = mixed
    w_home = {share: number for number, chunk in enumerate(w_chunks) for share in chunk.shares}
    g_home = {share: number for number, chunk in enumerate(g_chunks) for share in chunk.shares}
    for share in range(w_chunks[0].own):
        source, sink = w_home[share], g_home[share]
        need(source)
        w_chunk, g_chunk = w_chunks[source], g_chunks[sink]
        blocks = w_chunk.blocks(share)
        down_at = w_chunk.rows_at["down", share]
        down_to = g_chunk.rows_at["down", share]
        for pair in range(0, len(blocks), 2):
            some = blocks[pair : pair + 2]
            gate_w = jnp.concatenate([column(source, "gate", f) for f in some], 1)
            up_w = jnp.concatenate([column(source, "up", f) for f in some], 1)
            down_w = jnp.concatenate(
                [weights[source][f // w_chunk.own, down_at : down_at + width, :] for f in some], 1
            )
            gate = dot(normed, gate_w)
            up = dot(normed, up_w)
            hidden_grad = dot(upstream, down_w)
            sigmoid = 1.0 / (1.0 + jnp.exp(-gate))
            silu = gate * sigmoid
            hidden = (silu * up).astype(bf16)
            gate_low = (hidden_grad * up * (sigmoid * (1.0 + gate * (1.0 - sigmoid)))).astype(bf16)
            up_low = (hidden_grad * silu).astype(bf16)
            ahead = ahead + dot(hidden, down_w, (1, 1))
            back = back + dot(gate_low, gate_w, (1, 1)) + dot(up_low, up_w, (1, 1))
            gate_wg = dot(normed_t, gate_low).astype(bf16)
            up_wg = dot(normed_t, up_low).astype(bf16)
            down_wg = dot(out_t, hidden).astype(bf16)
            for at, f in enumerate(some):
                cols = slice(at * LANES, (at + 1) * LANES)
                store(sink, "gate", f, gate_wg[:, cols])
                store(sink, "up", f, up_wg[:, cols])
                grads[sink][f // g_chunk.own, down_to : down_to + width, :] = down_wg[:, cols]
        if share == g_chunk.shares[-1] and not g_chunk.has_out:
            leave(sink)
    layer_out_t[...] = ahead.T.astype(bf16)
    gain_grad[...] = jnp.sum(back * unit, axis=0, keepdims=True)
    inner = back * gained
    through = scale * (inner - unit * jnp.mean(inner * unit, axis=1, keepdims=True))
    mixed_back = upstream.astype(f32) + through
    mixed_grad[...] = mixed_back
    branch = mixed_back.astype(bf16)
    attended_grad[...] = dot(branch, output_w, (1, 1)).astype(bf16)
    output_wg = dot(att_t, branch)
    last = len(g_chunks) - 1
    for j in range(out_blocks):
        block = output_wg[:, j * LANES : min((j + 1) * LANES, width)]
        if block.shape[1] < LANES:
            block = jnp.concatenate(
                [block, jnp.zeros((block.shape[0], LANES - block.shape[1]), f32)], 1
            )
        store(last, "out", j, block.astype(bf16))
    leave(last)
    for number in range(len(g_chunks)):
        for core in range(2):
            out = packed[2 * number + core]
            pltpu.make_async_copy(out, out, sem_out.at[number, core]).wait()


def run_mlp(where, w_chunks, g_chunks, pieces, attended, tokens_t, out_grad_t, gain):
    f32, bf16 = jnp.float32, jnp.bfloat16
    groups = w_chunks[0].groups
    width, toks = tokens_t.shape
    packed = []
    for chunk in g_chunks:
        packed += [shape((2, 2, groups, chunk.part, LANES), bf16)] * 2
    return staged_call(
        functools.partial(mlp_kernel, w_chunks, g_chunks),
        "mlp",
        where,
        (attended, tokens_t, out_grad_t, gain),
        pieces,
        (
            shape((width, toks), bf16),
            shape((toks, width), f32),
            shape((toks, width), bf16),
            shape((1, width), f32),
        )
        + tuple(packed),
        (vmem(),) * 4 + (hbm(),) * len(packed),
        [pltpu.VMEM((groups, chunk.rows, LANES), bf16) for chunk in w_chunks + g_chunks]
        + [
            pltpu.SemaphoreType.DMA((len(w_chunks),)),
            pltpu.SemaphoreType.DMA((len(g_chunks), 2)),
        ],
        BIG,
    )


def last_kernel(sizes, where, query_grad, raw, normed, tokens_t, mixed_grad, gain, head_gains, cosine, sine, weights, second, *refs):
    f32, bf16 = jnp.float32, jnp.bfloat16
    q_width, kv_width, head_size = sizes
    kv_parts = refs[: len(refs) - 4]
    token_grad_t, keep, send, grads = refs[len(refs) - 4 :]
    count, groups, rows, _ = grads.shape
    width, toks = tokens_t.shape
    shard = width // groups
    half = head_size // 2
    cos, sin = cosine[...], sine[...]
    kv_grad = kv_parts[0][...].astype(f32)
    for part in kv_parts[1:]:
        kv_grad = kv_grad + part[...].astype(f32)
    lows, head_sums = [], [jnp.zeros((1, head_size), f32)] * 2
    for at, (unit, factor) in enumerate(unit_heads(raw[...], head_size)):
        kind = 0 if at * head_size < q_width else 1
        source, place = (query_grad, at * head_size) if kind == 0 else (kv_grad, at * head_size - q_width)
        one = source[:, place : place + half]
        two = source[:, place + half : place + head_size]
        back = jnp.concatenate([one * cos + two * sin, two * cos - one * sin], 1)
        head_sums[kind] = head_sums[kind] + jnp.sum(back * unit, axis=0, keepdims=True)
        inner = back * head_gains[kind : kind + 1, :]
        lows.append(factor * (inner - unit * jnp.mean(inner * unit, axis=1, keepdims=True)))
    lows.append(kv_grad[:, kv_width:])
    short = count * LANES - q_width - 2 * kv_width
    if short:
        lows.append(jnp.zeros((toks, short), f32))
    low = jnp.concatenate(lows, 1).astype(bf16)
    back = dot(low, weights[...], (1, 1))
    inputs = tokens_t[...].astype(f32).T
    scale = lax.rsqrt(jnp.mean(inputs * inputs, axis=1, keepdims=True) + NORM_EPS)
    unit = inputs * scale
    first = jnp.sum(back * unit, axis=0, keepdims=True)
    inner = back * gain[...]
    whole = mixed_grad[...] + scale * (inner - unit * jnp.mean(inner * unit, axis=1, keepdims=True))
    token_grad_t[...] = whole.T
    normed_t = turned(normed[...])
    products = dot(normed_t, low).astype(bf16)
    for j in range(count):
        for owner in range(groups):
            grads[j, owner, :shard, :] = products[
                owner * shard : (owner + 1) * shard, j * LANES : (j + 1) * LANES
            ]
            grads[j, owner, shard:, :] = jnp.zeros((rows - shard, LANES), bf16)

    def line(vector):
        short = LANES - vector.shape[1]
        return jnp.concatenate([vector, jnp.zeros((1, short), f32)], 1) if short else vector

    head_part = head_size // groups
    for owner in range(groups):
        lines = []
        for vector in (first, second[...]):
            mine = vector[:, owner * shard : (owner + 1) * shard]
            lines += [line(mine[:, at : at + LANES]) for at in range(0, shard, LANES)]
        for vector in head_sums:
            lines.append(line(vector[:, owner * head_part : (owner + 1) * head_part]))
        lines.append(jnp.zeros((rows - shard - len(lines), LANES), f32))
        grads[0, owner, shard:, :] = jnp.concatenate(lines, 0).astype(bf16)
    for core in range(2):
        for across in range(2):
            for along in range(2):
                block = block_at(where, core, across, along)
                for step in range(groups):
                    owner = lax.rem(where[0] + step, groups)
                    (send if core else keep)[across * 2 + along, step] = grads[block, owner]


def run_last(where, query_grad, raw, normed, tokens_t, mixed_grad, gain, head_gains, cosine, sine, weights, second, kv_parts, sizes):
    f32, bf16 = jnp.float32, jnp.bfloat16
    width, toks = tokens_t.shape
    groups = lax.axis_size("grp")
    rows = width // groups + SMALL
    packed = shape((4, groups, rows, LANES), bf16)
    return pl.pallas_call(
        functools.partial(last_kernel, sizes),
        out_shape=(shape((width, toks), f32), packed, packed),
        in_specs=[smem()] + [vmem()] * (11 + len(kv_parts)),
        out_specs=(vmem(),) * 3,
        scratch_shapes=[pltpu.VMEM((8, groups, rows, LANES), bf16)],
        compiler_params=options(24),
        cost_estimate=cost(),
        name="last",
    )(where, query_grad, raw, normed, tokens_t, mixed_grad, gain, head_gains, cosine, sine, weights, second, *kv_parts)


def unpack_kernel(sizes, chunks, where, near, far, *refs):
    f32 = jnp.float32
    q_width, kv_width, _ = sizes
    gate, up, down_t, output, query, key, value = refs[:7]
    lines_out = refs[7:11]
    packs = refs[11 : 11 + len(chunks)]
    shard, width = chunks[0].shard, chunks[0].width
    projections = []
    small = None
    for core in range(2):
        for across in range(2):
            for along in range(2):
                place = (where[2] ^ across) * 2 + (where[3] ^ along)
                piece = jnp.where(where[1] == core, near[place], far[place])
                at = 0
                for chunk, pack in zip(chunks, packs):
                    high, low = (across, along) if core == 0 else (along, across)
                    row = (core * 4 + high * 2 + low) * chunk.part
                    pack[row : row + chunk.part, :] = piece[at : at + chunk.part]
                    at += chunk.part
                projections.append(piece[at : at + shard])
                if small is None:
                    small = piece[at + shard :].astype(f32)
    for chunk, pack in zip(chunks, packs):
        for (kind, j), at in chunk.rows_at.items():
            if kind == "down":
                down_t[:, j * LANES : (j + 1) * LANES] = pack[at : at + width].astype(f32)
                continue
            out = {"gate": gate, "up": up, "out": output}[kind]
            stop = min((j + 1) * LANES, out.shape[1])
            out[:, j * LANES : stop] = pack[at : at + shard].astype(f32)[:, : stop - j * LANES]
    whole = jnp.concatenate(projections, 1).astype(f32)
    query[...] = whole[:, :q_width]
    key[...] = whole[:, q_width : q_width + kv_width]
    value[...] = whole[:, q_width + kv_width : q_width + 2 * kv_width]
    row = 0
    for out in lines_out:
        for at in range(0, out.shape[1], LANES):
            stop = min(at + LANES, out.shape[1])
            out[:, at:stop] = small[row : row + 1, : stop - at]
            row += 1


def run_unpack(where, chunks, sizes, near, far, hidden_width, own_hidden, head_part):
    f32 = jnp.float32
    q_width, kv_width, _ = sizes
    shard, width = chunks[0].shard, chunks[0].width
    return staged_call(
        functools.partial(unpack_kernel, sizes, chunks),
        "unpack",
        where,
        (near, far),
        (),
        (
            shape((shard, hidden_width), f32),
            shape((shard, hidden_width), f32),
            shape((width, own_hidden), f32),
            shape((shard, width), f32),
            shape((shard, q_width), f32),
            shape((shard, kv_width), f32),
            shape((shard, kv_width), f32),
            shape((1, shard), f32),
            shape((1, shard), f32),
            shape((1, head_part), f32),
            shape((1, head_part), f32),
        ),
        (vmem(),) * 11,
        [pltpu.VMEM((chunk.rows, LANES), near.dtype) for chunk in chunks],
        BIG,
    )


def body(
    tokens,
    segments,
    out_grad,
    norm_gain,
    query_gain,
    key_gain,
    query_weight,
    key_weight,
    value_weight,
    output_weight,
    second_gain,
    gate_weight,
    up_weight,
    down_weight,
):
    f32, bf16 = jnp.float32, jnp.bfloat16
    groups = lax.axis_size("grp")
    place_z = lax.axis_index("grp")
    where = place_scalars()
    toks, width = tokens.shape
    shard = norm_gain.shape[0]
    head_part = query_gain.shape[0]
    head_size = head_part * groups
    hidden_width, own_hidden = gate_weight.shape[1], down_weight.shape[0]
    sizes = (query_weight.shape[1], key_weight.shape[1], head_size)
    w_chunks, g_chunks = chunks_of(shard, width, own_hidden, groups)
    tokens_t, out_grad_t = tokens.T, out_grad.T

    gain_rows = -(-shard // LANES)
    seg_rows = -(-toks // LANES)
    small = jnp.zeros((SMALL * LANES,), bf16)
    at = 0
    for line, count in (
        (norm_gain, gain_rows),
        (second_gain, gain_rows),
        (query_gain, 1),
        (key_gain, 1),
        (segments.astype(bf16), seg_rows),
    ):
        small = small + jnp.pad(line, (at, SMALL * LANES - at - line.shape[0]))
        at += count * LANES
    fence = lax.optimization_barrier
    (own_second,) = run_pack_second(
        where, w_chunks, gate_weight, up_weight, down_weight.T, output_weight
    )
    second_z = [own_second] + [shift(own_second, step) for step in range(1, groups)]
    _, small = fence((own_second, small))
    own_first = run_pack_first(
        where, query_weight, key_weight, value_weight, small.reshape(SMALL, LANES)
    )
    first_z = [own_first] + [shift(own_first, step) for step in range(1, groups)]
    near, far = spread_blocks(jnp.stack([held[:shard] for held in first_z]))

    small_behind = jnp.stack([held[shard:] for held in first_z]).astype(f32)
    small_all = small_behind[lax.rem(place_z + groups - jnp.arange(groups), groups)]
    at = 0
    gains = []
    for count, length in ((gain_rows, shard), (gain_rows, shard), (1, head_part), (1, head_part)):
        gains.append(lined(small_all[:, at : at + count], length))
        at += count
    gain_first, gain_second, gain_query, gain_key = gains
    head_gains = jnp.concatenate([gain_query, gain_key])
    segs = small_behind[:, at : at + seg_rows].reshape(groups, -1)[:, :toks]
    there = (place_z >= jnp.arange(groups))[:, None]
    key_seg = jnp.where(there, segs, -1.0).reshape(1, -1)
    own_seg = segs[0][:, None]
    earlier = ((key_seg < own_seg) & (key_seg >= 0.0)).astype(jnp.int32)
    positions = place_z * toks + jnp.arange(toks, dtype=jnp.int32) - jnp.sum(earlier, axis=1)
    half = head_size // 2
    inverse = ROPE_BASE ** (-(jnp.arange(half, dtype=f32) * 2.0 / head_size))
    angles = positions.astype(f32)[:, None] * inverse[None, :]
    cosine, sine = jnp.cos(angles), jnp.sin(angles)

    normed, raw, query, key_value, proj_weights = run_proj(
        where, near, far, tokens_t, gain_first, head_gains, cosine, sine, sizes
    )
    held = [key_value]
    for step in range(1, groups):
        ahead = [(i, i + step) for i in range(groups - step)]
        held.append(lax.ppermute(key_value, "grp", ahead))
    whole = jnp.stack(second_z)
    whole = jnp.stack([whole, hop_split(whole, 4, 2)])
    far_whole = hop_split(whole, 2, 4)
    whole, held = fence((whole, held))
    other = hop(whole, 1)
    attended, probs = run_attend(where, query, own_seg, key_seg, held, sizes)
    got, attended, other = fence((far_whole, attended, other))
    pieces = [whole, got, other, hop(got, 1)]
    layer_out_t, mixed_grad, attended_grad, second_sum, keep, send = run_mlp(
        where, w_chunks, g_chunks, pieces, attended, tokens_t, out_grad_t, gain_second
    )
    got = hop(send, 1)
    query_grad, *kv_parts = run_attend_back(where, query, attended_grad, probs, held, sizes)
    got, query_grad, kv_parts = fence((got, query_grad, kv_parts))
    kv_back = [kv_parts[0]]
    for step in range(1, groups):
        behind = [(i + step, i) for i in range(groups - step)]
        kv_back.append(lax.ppermute(kv_parts[step], "grp", behind))
    near, away = add_low(keep[0], got[0]), add_low(keep[1], got[1])
    got, kv_back = fence((hop_split(away, 2, 4), kv_back))
    near, away = add_low(near[0], got[0]), add_low(near[1], got[1])
    got = hop_split(away, 4, 2)
    token_grad_t, late_keep, late_send = run_last(
        where, query_grad, raw, normed, tokens_t, mixed_grad, gain_first, head_gains, cosine, sine,
        proj_weights, second_sum, kv_back, sizes,
    )
    got, late_keep, late_send = fence((got, late_keep, late_send))
    early = fold_grp([add_low(near[d], got[d]) for d in range(groups)])
    late = fold_blocks(late_keep, late_send)
    early, late = fence((early, late))
    near, far = spread_blocks(jnp.concatenate([early, fold_grp(late)]))
    (
        gate_sum, up_sum, down_sum_t, output_sum, query_sum, key_sum, value_sum,
        first_sum, second_sum, query_gsum, key_gsum,
    ) = run_unpack(where, g_chunks, sizes, near, far, hidden_width, own_hidden, head_part)
    return (
        layer_out_t.T,
        token_grad_t.T,
        first_sum.reshape(-1),
        query_gsum.reshape(-1),
        key_gsum.reshape(-1),
        query_sum,
        key_sum,
        value_sum,
        output_sum,
        second_sum.reshape(-1),
        gate_sum,
        up_sum,
        down_sum_t.T,
    )


def solution(mesh):
    placed = (
        P(("rep", "grp"), None),
        P(("rep", "grp")),
        P(("rep", "grp"), None),
        P("grp"),
        P("grp"),
        P("grp"),
        P("grp", None),
        P("grp", None),
        P("grp", None),
        P("grp", None),
        P("grp"),
        P("grp", None),
        P("grp", None),
        P("grp", None),
    )
    return jax.shard_map(
        body,
        mesh=mesh,
        in_specs=placed,
        out_specs=(
            P(("rep", "grp"), None),
            P(("rep", "grp"), None),
            P("grp"),
            P("grp"),
            P("grp"),
            P("grp", None),
            P("grp", None),
            P("grp", None),
            P("grp", None),
            P("grp"),
            P("grp", None),
            P("grp", None),
            P("grp", None),
        ),
        check_vma=False,
    )
```

```python
import functools

import jax
import jax.numpy as jnp
from jax import lax
from jax.experimental import pallas as pl
from jax.experimental.pallas import tpu as pltpu
from jax.sharding import PartitionSpec as P

NORM_EPS = 1e-05
ROPE_BASE = 100000.0
LANES = 128
SMALL = 16
MIB = 1024 * 1024
BIG = 58


def vmem():
    return pl.BlockSpec(memory_space=pltpu.VMEM)


def smem():
    return pl.BlockSpec(memory_space=pltpu.SMEM)


def hbm():
    return pl.BlockSpec(memory_space=pl.ANY)


def shape(dims, kind):
    return jax.ShapeDtypeStruct(dims, kind)


def options(mebibytes):
    return pltpu.CompilerParams(vmem_limit_bytes=mebibytes * MIB)


def cost():
    return pl.CostEstimate(flops=1, bytes_accessed=1024, transcendentals=0)


class Staged:
    def __init__(self, source, target, sem):
        self.copy = pltpu.make_async_copy(source, target, sem)
        self.copy.start()
        self.target, self.waiting = target, True
        self.shape, self.dtype = target.shape, target.dtype

    def wait(self):
        if self.waiting:
            self.copy.wait()
            self.waiting = False

    def __getitem__(self, index):
        self.wait()
        return self.target[index]


def staged_call(kernel, name, operands, out_shape, out_specs, scratch, mebibytes):
    kinds = [kind for kind, _ in operands]
    staged = [array for kind, array in operands if kind == "staged"]
    count = len(operands)

    def whole(*refs):
        sources, refs = refs[:count], refs[count:]
        if staged:
            targets, sems = refs[len(refs) - len(staged) - 1 : -1], refs[-1]
            refs = refs[: len(refs) - len(staged) - 1]
        given, at = [], 0
        for kind, source in zip(kinds, sources):
            if kind == "staged":
                source = Staged(source, targets[at], sems.at[at])
                at += 1
            given.append(source)
        kernel(*given, *refs)
        for operand in given:
            if isinstance(operand, Staged):
                operand.wait()

    specs = {"smem": smem, "vmem": vmem, "hbm": hbm, "staged": hbm}
    more = [pltpu.VMEM(array.shape, array.dtype) for array in staged]
    if staged:
        more.append(pltpu.SemaphoreType.DMA((len(staged),)))
    return pl.pallas_call(
        whole,
        out_shape=out_shape,
        in_specs=[specs[kind]() for kind in kinds],
        out_specs=out_specs,
        scratch_shapes=list(scratch) + more,
        compiler_params=options(mebibytes),
        cost_estimate=cost(),
        name=name,
    )(*[array for _, array in operands])


def kept(kind, *arrays):
    return [(kind, array) for array in arrays]


def hop(value, bit):
    count = lax.axis_size("rep")
    return lax.ppermute(value, "rep", [(i, i ^ bit) for i in range(count)])


def shift(value, step):
    count = lax.axis_size("grp")
    return lax.ppermute(value, "grp", [(i, (i + step) % count) for i in range(count)])


def rep_bits():
    index = lax.axis_index("rep")
    return index & 1, (index >> 1) & 1, (index >> 2) & 1


def hop_split(value, even, odd):
    count = lax.axis_size("rep")
    return lax.ppermute(value, "rep", [(i, i ^ (odd if i % 2 else even)) for i in range(count)])


def add_low(*values):
    total = values[0].astype(jnp.float32)
    for value in values[1:]:
        total = total + value.astype(jnp.float32)
    return total.astype(values[0].dtype)


def fold_grp(parts):
    f32 = jnp.float32
    total = parts[0].astype(f32)
    for step in range(1, len(parts)):
        total = total + shift(parts[step], step).astype(f32)
    total = total.astype(parts[0].dtype)
    bit = 8
    while bit < lax.axis_size("rep"):
        total = add_low(total, hop(total, bit))
        bit *= 2
    return total


def fold_blocks(keep, got):
    f32 = jnp.float32
    sums = [add_low(keep[j], got[j]) for j in range(4)]
    across, along, both = hop(sums[2], 2), hop(sums[1], 4), hop(sums[3], 6)
    return [
        (
            sums[0][d].astype(f32)
            + across[d].astype(f32)
            + along[d].astype(f32)
            + both[d].astype(f32)
        ).astype(keep.dtype)
        for d in range(lax.axis_size("grp"))
    ]


def spread_chip(own):
    return jnp.stack([own, hop(own, 4), hop(own, 2), hop(own, 6)])


def rows_of(vector, count):
    short = count * LANES - vector.shape[0]
    return jnp.pad(vector, (0, short)).reshape(count, LANES)


def lined(rows, length):
    return rows.reshape(rows.shape[0], -1)[:, :length].reshape(1, -1)


def place_scalars():
    bit_c, bit_x, bit_y = rep_bits()
    return jnp.stack([lax.axis_index("grp"), bit_c, bit_x, bit_y]).astype(jnp.int32)


def piece_row(where, core, high, low, rows):
    owner = where[1] ^ core
    first = jnp.where(owner == 0, where[2], where[3])
    second = jnp.where(owner == 0, where[3], where[2])
    index = owner * 4 + (first ^ high) * 2 + (second ^ low)
    return pl.multiple_of(index * (rows // 8), 16)


def piece_list():
    return [(c, h, l) for c in range(2) for h in range(2) for l in range(2)]


def dot(one, two, contract=(1, 0)):
    return lax.dot_general(
        one, two, (((contract[0],), (contract[1],)), ((), ())), preferred_element_type=jnp.float32
    )


def turned(value):
    return value.astype(jnp.float32).T.astype(value.dtype)


class Chunk:
    def __init__(self, dims, out_first):
        self.shard, self.width, self.own, self.groups = dims
        self.out_blocks = -(-self.width // LANES)
        self.rows_at, self.share_end, at = {}, [], 0

        def out_rows(at):
            for j in range(self.out_blocks):
                self.rows_at["out", j] = at
                at += self.shard
            return at

        if out_first:
            at = out_rows(at)
        self.out_end = at
        for share in range(self.own):
            for kind in ("gate", "up"):
                for f in self.blocks(share):
                    self.rows_at[kind, f] = at
                    at += self.shard
            self.rows_at["down", share] = at
            at += self.width
            self.share_end.append(at)
        if not out_first:
            at = out_rows(at)
        self.used = at
        self.rows = -(-at // 128) * 128
        self.part = self.rows // 8

    def blocks(self, share):
        return [owner * self.own + share for owner in range(self.groups)]


def chunks_of(shard, width, own_hidden, groups):
    dims = (shard, width, own_hidden // LANES, groups)
    return Chunk(dims, True), Chunk(dims, False)


def pack_kernel(chunk, where, query, key, value, gate, up, down_t, output, first, second, blocks, pack):
    shard, width = chunk.shard, chunk.width
    whole = jnp.concatenate([query[...], key[...], value[...]], 1)
    for j in range(blocks.shape[0]):
        stop = min((j + 1) * LANES, whole.shape[1])
        blocks[j, :, : stop - j * LANES] = whole[:, j * LANES : stop]
        if stop < (j + 1) * LANES:
            blocks[j, :, stop - j * LANES :] = jnp.zeros(
                (shard, (j + 1) * LANES - stop), whole.dtype
            )
    first[...] = blocks[where[1] * 4 + where[2] * 2 + where[3]]
    for (kind, j), at in chunk.rows_at.items():
        if kind == "down":
            pack[at : at + width, :] = down_t[:, j * LANES : (j + 1) * LANES]
            continue
        source = {"gate": gate, "up": up, "out": output}[kind]
        stop = min((j + 1) * LANES, source.shape[1])
        pack[at : at + shard, : stop - j * LANES] = source[:, j * LANES : stop]
        if stop < (j + 1) * LANES:
            pack[at : at + shard, stop - j * LANES :] = jnp.zeros(
                (shard, (j + 1) * LANES - stop), pack.dtype
            )
    if chunk.used < chunk.rows:
        pack[chunk.used :, :] = jnp.zeros((chunk.rows - chunk.used, LANES), pack.dtype)
    row = piece_row(where, 0, 0, 0, chunk.rows)
    second[...] = pack[pl.ds(row, chunk.part), :]


def run_pack(where, chunk, query, key, value, gate, up, down_t, output):
    kind = gate.dtype
    return staged_call(
        functools.partial(pack_kernel, chunk),
        "pack",
        kept("smem", where) + kept("staged", query, key, value, gate, up, down_t, output),
        (shape((chunk.shard, LANES), kind), shape((chunk.part, LANES), kind)),
        (vmem(), vmem()),
        [pltpu.VMEM((8, chunk.shard, LANES), kind), pltpu.VMEM((chunk.rows, LANES), kind)],
        BIG,
    )


def block_at(where, core, across, along):
    return (where[1] ^ core) * 4 + (where[2] ^ across) * 2 + (where[3] ^ along)


def unit_heads(raw, head_size):
    pairs = []
    for at in range(0, raw.shape[1], head_size):
        head = raw[:, at : at + head_size]
        factor = lax.rsqrt(jnp.mean(head * head, axis=1, keepdims=True) + NORM_EPS)
        pairs.append((head * factor, factor))
    return pairs


def proj_kernel(sizes, where, near, far, tokens_t, gain, head_gains, cosine, sine, *refs):
    f32, bf16 = jnp.float32, jnp.bfloat16
    q_width, kv_width, head_size = sizes
    normed_out, raw_out, query_out, kv_out, weights_out = refs
    groups = near.shape[1]
    inputs = tokens_t[...].astype(f32).T
    scale = lax.rsqrt(jnp.mean(inputs * inputs, axis=1, keepdims=True) + NORM_EPS)
    normed = (inputs * scale * gain[...]).astype(bf16)
    normed_out[...] = normed
    for j in range(8):
        core, across, along = j // 4, j // 2 % 2, j % 2
        place = (where[2] ^ across) * 2 + (where[3] ^ along)
        pieces = []
        for owner in range(groups):
            behind = lax.rem(where[0] + groups - owner, groups)
            pieces.append(
                jnp.where(where[1] == core, near[place, behind], far[place, behind])
            )
        weights_out[:, j * LANES : (j + 1) * LANES] = jnp.concatenate(pieces, 0)
    flat = weights_out[...]
    raw = dot(normed, flat)
    raw_out[...] = raw[:, : q_width + kv_width]
    half = head_size // 2
    cos, sin = cosine[...], sine[...]

    def turn(head):
        one, two = head[:, :half], head[:, half:]
        return jnp.concatenate([one * cos - two * sin, two * cos + one * sin], 1)

    heads = []
    for at, (unit, _) in enumerate(unit_heads(raw[:, : q_width + kv_width], head_size)):
        row = 0 if at * head_size < q_width else 1
        heads.append(turn(unit * head_gains[row : row + 1, :]).astype(bf16))
    queries = jnp.concatenate(heads[: q_width // head_size], 1)
    query_out[...] = (queries.astype(f32) * head_size ** (-0.5)).astype(bf16)
    values = raw[:, q_width + kv_width : q_width + 2 * kv_width].astype(bf16)
    kv_out[...] = jnp.concatenate(heads[q_width // head_size :] + [values], 1)


def run_proj(where, near, far, tokens_t, gain, head_gains, cosine, sine, sizes):
    f32, bf16 = jnp.float32, jnp.bfloat16
    q_width, kv_width, _ = sizes
    width, toks = tokens_t.shape
    return staged_call(
        functools.partial(proj_kernel, sizes),
        "proj",
        kept("smem", where)
        + kept("vmem", near, far)
        + kept("staged", tokens_t)
        + kept("vmem", gain, head_gains, cosine, sine),
        (
            shape((toks, width), bf16),
            shape((toks, q_width + kv_width), f32),
            shape((toks, q_width), bf16),
            shape((toks, 2 * kv_width), bf16),
            shape((width, 8 * LANES), bf16),
        ),
        (vmem(),) * 5,
        (),
        24,
    )


def attend_kernel(sizes, query, own_seg, key_seg, *refs):
    f32, bf16 = jnp.float32, jnp.bfloat16
    q_width, kv_width, head_size = sizes
    held = refs[: len(refs) - 6]
    attended, exact, probs_out, bias, probs, sems = refs[len(refs) - 6 :]
    toks = query.shape[0]
    same = own_seg[...] == key_seg[...]
    order = lax.broadcasted_iota(jnp.int32, same.shape, 0) - lax.broadcasted_iota(
        jnp.int32, same.shape, 1
    )
    later = lax.broadcasted_iota(jnp.int32, same.shape, 1) >= toks
    bias[...] = jnp.where(same & ((order >= 0) | later), 0.0, -1e30)
    outs = []
    per = q_width // kv_width
    for g in range(kv_width // head_size):
        cols = slice(g * head_size, (g + 1) * head_size)
        keys = jnp.concatenate([kv[:, cols] for kv in held], 0)
        cols = slice(kv_width + g * head_size, kv_width + (g + 1) * head_size)
        values = jnp.concatenate([kv[:, cols] for kv in held], 0)
        for head in range(g * per, (g + 1) * per):
            scores = dot(query[:, head * head_size : (head + 1) * head_size], keys, (1, 1))
            scores = scores + bias[...]
            powers = jnp.exp(scores)
            share = 1.0 / jnp.sum(powers, axis=1, keepdims=True)
            low = (powers * share).astype(bf16)
            probs[head] = low
            pltpu.make_async_copy(probs.at[head], probs_out.at[head], sems.at[head]).start()
            outs.append(dot(low, values))
    whole = jnp.concatenate(outs, 1)
    exact[...] = whole
    attended[...] = whole.astype(bf16)
    for head in range(probs.shape[0]):
        pltpu.make_async_copy(probs.at[head], probs_out.at[head], sems.at[head]).wait()


def run_attend(query, own_seg, key_seg, held, sizes):
    bf16 = jnp.bfloat16
    q_width, kv_width, head_size = sizes
    toks = query.shape[0]
    keys = toks * len(held)
    heads = q_width // head_size
    return staged_call(
        functools.partial(attend_kernel, sizes),
        "attend",
        kept("staged", query, own_seg, key_seg, *held),
        (
            shape((toks, q_width), bf16),
            shape((toks, q_width), jnp.float32),
            shape((heads, toks, keys), bf16),
        ),
        (vmem(), vmem(), hbm()),
        [
            pltpu.VMEM((toks, keys), jnp.float32),
            pltpu.VMEM((heads, toks, keys), bf16),
            pltpu.SemaphoreType.DMA((heads,)),
        ],
        BIG,
    )


def attend_back_kernel(sizes, query, grad, exact, *refs):
    f32, bf16 = jnp.float32, jnp.bfloat16
    q_width, kv_width, head_size = sizes
    probs, sems = refs[-2:]
    refs = refs[:-2]
    groups = (len(refs) - 2) // 2
    probs_in = refs[groups]
    refs = refs[:groups] + refs[groups + 1 :]
    copies = [
        pltpu.make_async_copy(probs_in.at[head], probs.at[head], sems.at[head])
        for head in range(probs.shape[0])
    ]
    for copy in copies:
        copy.start()
    held = refs[:groups]
    query_grad = refs[groups]
    kv_grads = refs[groups + 1 :]
    toks = query.shape[0]
    per = q_width // kv_width
    query_t = query[...].astype(f32).T.astype(bf16)
    grad_t = grad[...].astype(f32).T.astype(bf16)
    outs, key_parts, value_parts = [], [], []
    for g in range(kv_width // head_size):
        cols = slice(g * head_size, (g + 1) * head_size)
        keys = jnp.concatenate([kv[:, cols] for kv in held], 0)
        cols = slice(kv_width + g * head_size, kv_width + (g + 1) * head_size)
        values = jnp.concatenate([kv[:, cols] for kv in held], 0)
        key_t = value_t = None
        for head in range(g * per, (g + 1) * per):
            cols = slice(head * head_size, (head + 1) * head_size)
            copies[head].wait()
            low = probs[head]
            inner = jnp.sum(grad[:, cols].astype(f32) * exact[:, cols], axis=1, keepdims=True)
            scores = dot(grad[:, cols], values, (1, 1)) - inner
            scores = (low.astype(f32) * scores).astype(bf16)
            outs.append(dot(scores, keys))
            key_one = dot(query_t[cols, :], scores)
            value_one = dot(grad_t[cols, :], low)
            key_t = key_one if key_t is None else key_t + key_one
            value_t = value_one if value_t is None else value_t + value_one
        key_parts.append(key_t)
        value_parts.append(value_t)
    query_grad[...] = jnp.concatenate(outs, 1) * head_size ** (-0.5)
    both = jnp.concatenate(key_parts + value_parts, 0)
    for at, out in enumerate(kv_grads):
        out[...] = both[:, at * toks : (at + 1) * toks].T.astype(out.dtype)


def run_attend_back(query, grad, exact, probs, held, sizes):
    f32, bf16 = jnp.float32, jnp.bfloat16
    q_width, kv_width, head_size = sizes
    toks = query.shape[0]
    keys = toks * len(held)
    return staged_call(
        functools.partial(attend_back_kernel, sizes),
        "attend_back",
        kept("staged", query, grad, exact, *held) + kept("hbm", probs),
        (shape((toks, q_width), f32),) + tuple(shape((toks, 2 * kv_width), bf16) for _ in held),
        (vmem(),) * (1 + len(held)),
        [pltpu.VMEM(probs.shape, bf16), pltpu.SemaphoreType.DMA((probs.shape[0],))],
        BIG,
    )


def mlp_kernel(w_chunk, g_chunk, where, attended, tokens_t, out_grad_t, gain, *refs):
    f32, bf16 = jnp.float32, jnp.bfloat16
    pieces, refs = refs[:4], refs[4:]
    layer_out_t, mixed_grad, attended_grad, gain_grad, keep, send = refs[:6]
    weights, grads, sem_in, sem_out = refs[6:]
    width, toks = tokens_t.shape
    shard, groups, out_blocks = w_chunk.shard, w_chunk.groups, w_chunk.out_blocks

    def piece_place(number):
        core = number // 4
        first, second = (where[2], where[3]) if core == 0 else (where[3], where[2])
        return where[1] ^ core, first ^ (number // 2 % 2), second ^ (number % 2)

    for number in range(8):
        core, high, low = piece_place(number)
        for place in range(4):

            @pl.when(core * 2 + high == place)
            def _(number=number, low=low, place=place):
                pltpu.make_async_copy(
                    pieces[place].at[low],
                    weights.at[:, pl.ds(number * w_chunk.part, w_chunk.part)],
                    sem_in.at[number],
                ).start()

    waited = 0

    def need(rows):
        nonlocal waited
        while waited < 8 and waited * w_chunk.part < rows:
            here = weights.at[:, pl.ds(waited * w_chunk.part, w_chunk.part)]
            pltpu.make_async_copy(here, here, sem_in.at[waited]).wait()
            waited += 1

    left = 0

    def leave(rows):
        nonlocal left
        while left < 8 and (left + 1) * g_chunk.part <= rows:
            core, high, low = piece_place(left)
            for away, out in ((0, keep), (1, send)):

                @pl.when(core == away)
                def _(number=left, high=high, low=low, away=away, out=out):
                    pltpu.make_async_copy(
                        grads.at[:, pl.ds(number * g_chunk.part, g_chunk.part)],
                        out.at[high, low],
                        sem_out.at[away],
                    ).start()

            left += 1

    behind = [lax.rem(where[0] + groups - owner, groups) for owner in range(groups)]
    ahead_of = [lax.rem(owner + groups - where[0], groups) for owner in range(groups)]

    def column(kind, f):
        at = w_chunk.rows_at[kind, f]
        return jnp.concatenate([weights[place, at : at + shard, :] for place in behind], 0)

    def store(kind, f, block):
        at = g_chunk.rows_at[kind, f]
        for owner in range(groups):
            grads[ahead_of[owner], at : at + shard, :] = block[owner * shard : (owner + 1) * shard]

    out_t = out_grad_t[...]
    upstream = turned(out_t)
    inputs = tokens_t[...].astype(f32).T
    att_t = turned(attended[...])
    if g_chunk.used < g_chunk.rows:
        grads[:, g_chunk.used :, :] = jnp.zeros(
            (groups, g_chunk.rows - g_chunk.used, LANES), bf16
        )
    need(w_chunk.out_end)
    output_w = jnp.concatenate([column("out", j) for j in range(out_blocks)], 1)[:, :width]
    mixed = inputs + dot(attended[...], output_w)
    scale = lax.rsqrt(jnp.mean(mixed * mixed, axis=1, keepdims=True) + NORM_EPS)
    unit = mixed * scale
    gained = gain[...]
    normed = (unit * gained).astype(bf16)
    normed_t = turned(normed)
    back = jnp.zeros(mixed.shape, f32)
    ahead = mixed
    for share in range(w_chunk.own):
        need(w_chunk.share_end[share])
        blocks = w_chunk.blocks(share)
        down_at = w_chunk.rows_at["down", share]
        down_to = g_chunk.rows_at["down", share]
        for pair in range(0, len(blocks), 2):
            some = blocks[pair : pair + 2]
            gate_w = jnp.concatenate([column("gate", f) for f in some], 1)
            up_w = jnp.concatenate([column("up", f) for f in some], 1)
            down_w = jnp.concatenate(
                [weights[behind[f // w_chunk.own], down_at : down_at + width, :] for f in some], 1
            )
            gate = dot(normed, gate_w)
            up = dot(normed, up_w)
            hidden_grad = dot(upstream, down_w)
            sigmoid = 1.0 / (1.0 + jnp.exp(-gate))
            silu = gate * sigmoid
            hidden = (silu * up).astype(bf16)
            gate_low = (hidden_grad * up * (sigmoid * (1.0 + gate * (1.0 - sigmoid)))).astype(bf16)
            up_low = (hidden_grad * silu).astype(bf16)
            ahead = ahead + dot(hidden, down_w, (1, 1))
            back = back + dot(gate_low, gate_w, (1, 1)) + dot(up_low, up_w, (1, 1))
            gate_wg = dot(normed_t, gate_low).astype(bf16)
            up_wg = dot(normed_t, up_low).astype(bf16)
            down_wg = dot(out_t, hidden).astype(bf16)
            for at, f in enumerate(some):
                cols = slice(at * LANES, (at + 1) * LANES)
                store("gate", f, gate_wg[:, cols])
                store("up", f, up_wg[:, cols])
                grads[ahead_of[f // g_chunk.own], down_to : down_to + width, :] = down_wg[:, cols]
        leave(g_chunk.share_end[share])
    layer_out_t[...] = ahead.T.astype(bf16)
    gain_grad[...] = jnp.sum(back * unit, axis=0, keepdims=True)
    inner = back * gained
    through = scale * (inner - unit * jnp.mean(inner * unit, axis=1, keepdims=True))
    mixed_back = upstream.astype(f32) + through
    mixed_grad[...] = mixed_back
    branch = mixed_back.astype(bf16)
    attended_grad[...] = dot(branch, output_w, (1, 1)).astype(bf16)
    output_wg = dot(att_t, branch)
    for j in range(out_blocks):
        block = output_wg[:, j * LANES : min((j + 1) * LANES, width)]
        if block.shape[1] < LANES:
            block = jnp.concatenate(
                [block, jnp.zeros((block.shape[0], LANES - block.shape[1]), f32)], 1
            )
        store("out", j, block.astype(bf16))
    leave(g_chunk.rows)
    pltpu.make_async_copy(keep, keep, sem_out.at[0]).wait()
    pltpu.make_async_copy(send, send, sem_out.at[1]).wait()


def run_mlp(where, w_chunk, g_chunk, pieces, attended, tokens_t, out_grad_t, gain):
    f32, bf16 = jnp.float32, jnp.bfloat16
    groups = w_chunk.groups
    width, toks = tokens_t.shape
    packed = shape((2, 2, groups, g_chunk.part, LANES), bf16)
    return staged_call(
        functools.partial(mlp_kernel, w_chunk, g_chunk),
        "mlp",
        kept("smem", where) + kept("staged", attended, tokens_t, out_grad_t, gain) + kept("hbm", *pieces),
        (
            shape((width, toks), bf16),
            shape((toks, width), f32),
            shape((toks, width), bf16),
            shape((1, width), f32),
            packed,
            packed,
        ),
        (vmem(),) * 4 + (hbm(),) * 2,
        [pltpu.VMEM((groups, chunk.rows, LANES), bf16) for chunk in (w_chunk, g_chunk)]
        + [pltpu.SemaphoreType.DMA((8,)), pltpu.SemaphoreType.DMA((2,))],
        BIG,
    )


def heads_back(grad, raw, cos, sin, gain, head_size):
    half = head_size // 2
    lows, total = [], jnp.zeros((1, head_size), jnp.float32)
    for at, (unit, factor) in enumerate(unit_heads(raw, head_size)):
        at *= head_size
        one, two = grad[:, at : at + half], grad[:, at + half : at + head_size]
        back = jnp.concatenate([one * cos + two * sin, two * cos - one * sin], 1)
        total = total + jnp.sum(back * unit, axis=0, keepdims=True)
        inner = back * gain
        lows.append(factor * (inner - unit * jnp.mean(inner * unit, axis=1, keepdims=True)))
    return lows, total


def query_back_kernel(sizes, query_grad, raw, normed, head_gains, cosine, sine, weights, products, back, total):
    q_width, _, head_size = sizes
    lows, total[...] = heads_back(
        query_grad[...], raw[:, :q_width], cosine[...], sine[...], head_gains[0:1, :], head_size
    )
    low = jnp.concatenate(lows, 1).astype(products.dtype)
    back[...] = dot(low, weights[:, :q_width], (1, 1))
    products[...] = dot(turned(normed[...]), low).astype(products.dtype)


def run_query_back(query_grad, raw, normed, head_gains, cosine, sine, weights, sizes):
    f32 = jnp.float32
    q_width, _, head_size = sizes
    toks, width = normed.shape
    return staged_call(
        functools.partial(query_back_kernel, sizes),
        "query_back",
        kept("vmem", query_grad, raw, normed, head_gains, cosine, sine, weights),
        (shape((width, q_width), normed.dtype), shape((toks, width), f32), shape((1, head_size), f32)),
        (vmem(),) * 3,
        (),
        24,
    )


def last_kernel(sizes, where, products, back, q_total, raw, normed, tokens_t, mixed_grad, gain, head_gains, cosine, sine, weights, second, *refs):
    f32, bf16 = jnp.float32, jnp.bfloat16
    q_width, kv_width, head_size = sizes
    kv_parts = refs[: len(refs) - 4]
    token_grad_t, keep, send, grads = refs[len(refs) - 4 :]
    count, groups, rows, _ = grads.shape
    width, toks = tokens_t.shape
    shard = width // groups
    kv_grad = kv_parts[0][...].astype(f32)
    for part in kv_parts[1:]:
        kv_grad = kv_grad + part[...].astype(f32)
    lows, k_total = heads_back(
        kv_grad, raw[:, q_width:], cosine[...], sine[...], head_gains[1:2, :], head_size
    )
    low = jnp.concatenate(lows + [kv_grad[:, kv_width:]], 1).astype(bf16)
    short = count * LANES - q_width - 2 * kv_width
    pieces = [products[...], dot(turned(normed[...]), low).astype(bf16)]
    if short:
        pieces.append(jnp.zeros((width, short), bf16))
    blocks = jnp.concatenate(pieces, 1)
    for j in range(count):
        for owner in range(groups):
            grads[j, owner, :shard, :] = blocks[
                owner * shard : (owner + 1) * shard, j * LANES : (j + 1) * LANES
            ]
            grads[j, owner, shard:, :] = jnp.zeros((rows - shard, LANES), bf16)
    whole = back[...] + dot(low, weights[:, q_width : q_width + 2 * kv_width], (1, 1))
    inputs = tokens_t[...].astype(f32).T
    scale = lax.rsqrt(jnp.mean(inputs * inputs, axis=1, keepdims=True) + NORM_EPS)
    unit = inputs * scale
    first = jnp.sum(whole * unit, axis=0, keepdims=True)
    inner = whole * gain[...]
    whole = mixed_grad[...] + scale * (inner - unit * jnp.mean(inner * unit, axis=1, keepdims=True))
    token_grad_t[...] = whole.T

    def line(vector):
        short = LANES - vector.shape[1]
        return jnp.concatenate([vector, jnp.zeros((1, short), f32)], 1) if short else vector

    head_part = head_size // groups
    for owner in range(groups):
        lines = []
        for vector in (first, second[...]):
            mine = vector[:, owner * shard : (owner + 1) * shard]
            lines += [line(mine[:, at : at + LANES]) for at in range(0, shard, LANES)]
        for vector in (q_total[...], k_total):
            lines.append(line(vector[:, owner * head_part : (owner + 1) * head_part]))
        lines.append(jnp.zeros((rows - shard - len(lines), LANES), f32))
        grads[0, owner, shard:, :] = jnp.concatenate(lines, 0).astype(bf16)
    for core in range(2):
        for across in range(2):
            for along in range(2):
                block = block_at(where, core, across, along)
                for step in range(groups):
                    owner = lax.rem(where[0] + step, groups)
                    (send if core else keep)[across * 2 + along, step] = grads[block, owner]


def run_last(where, products, back, q_total, raw, normed, tokens_t, mixed_grad, gain, head_gains, cosine, sine, weights, second, kv_parts, sizes):
    width = tokens_t.shape[0]
    groups = lax.axis_size("grp")
    rows = width // groups + SMALL
    packed = shape((4, groups, rows, LANES), jnp.bfloat16)
    return staged_call(
        functools.partial(last_kernel, sizes),
        "last",
        kept("smem", where)
        + kept("vmem", products, back, q_total, raw, normed)
        + kept("staged", tokens_t)
        + kept("vmem", mixed_grad, gain, head_gains, cosine, sine, weights, second, *kv_parts),
        (shape(tokens_t.shape, jnp.float32), packed, packed),
        (vmem(),) * 3,
        [pltpu.VMEM((8, groups, rows, LANES), jnp.bfloat16)],
        24,
    )


def unpack_kernel(sizes, chunk, where, near, far, *refs):
    f32 = jnp.float32
    q_width, kv_width, _ = sizes
    gate, up, down_t, output, query, key, value = refs[:7]
    lines_out = refs[7:11]
    pack = refs[11]
    shard, width = chunk.shard, chunk.width
    projections = []
    small = None
    for core in range(2):
        for across in range(2):
            for along in range(2):
                place = (where[2] ^ across) * 2 + (where[3] ^ along)
                piece = jnp.where(where[1] == core, near[place], far[place])
                at = chunk.part
                high, low = (across, along) if core == 0 else (along, across)
                row = (core * 4 + high * 2 + low) * chunk.part
                pack[row : row + chunk.part, :] = piece[:at]
                projections.append(piece[at : at + shard])
                if small is None:
                    small = piece[at + shard :].astype(f32)
    for (kind, j), at in chunk.rows_at.items():
        if kind == "down":
            down_t[:, j * LANES : (j + 1) * LANES] = pack[at : at + width].astype(f32)
            continue
        out = {"gate": gate, "up": up, "out": output}[kind]
        stop = min((j + 1) * LANES, out.shape[1])
        out[:, j * LANES : stop] = pack[at : at + shard].astype(f32)[:, : stop - j * LANES]
    whole = jnp.concatenate(projections, 1).astype(f32)
    query[...] = whole[:, :q_width]
    key[...] = whole[:, q_width : q_width + kv_width]
    value[...] = whole[:, q_width + kv_width : q_width + 2 * kv_width]
    row = 0
    for out in lines_out:
        for at in range(0, out.shape[1], LANES):
            stop = min(at + LANES, out.shape[1])
            out[:, at:stop] = small[row : row + 1, : stop - at]
            row += 1


def run_unpack(where, chunk, sizes, near, far, hidden_width, own_hidden, head_part):
    f32 = jnp.float32
    q_width, kv_width, _ = sizes
    shard, width = chunk.shard, chunk.width
    return staged_call(
        functools.partial(unpack_kernel, sizes, chunk),
        "unpack",
        kept("smem", where) + kept("vmem", near, far),
        (
            shape((shard, hidden_width), f32),
            shape((shard, hidden_width), f32),
            shape((width, own_hidden), f32),
            shape((shard, width), f32),
            shape((shard, q_width), f32),
            shape((shard, kv_width), f32),
            shape((shard, kv_width), f32),
            shape((1, shard), f32),
            shape((1, shard), f32),
            shape((1, head_part), f32),
            shape((1, head_part), f32),
        ),
        (vmem(),) * 11,
        [pltpu.VMEM((chunk.rows, LANES), near.dtype)],
        24,
    )


def body(
    tokens,
    segments,
    out_grad,
    norm_gain,
    query_gain,
    key_gain,
    query_weight,
    key_weight,
    value_weight,
    output_weight,
    second_gain,
    gate_weight,
    up_weight,
    down_weight,
):
    f32, bf16 = jnp.float32, jnp.bfloat16
    groups = lax.axis_size("grp")
    place_z = lax.axis_index("grp")
    where = place_scalars()
    toks, width = tokens.shape
    shard = norm_gain.shape[0]
    head_part = query_gain.shape[0]
    head_size = head_part * groups
    hidden_width, own_hidden = gate_weight.shape[1], down_weight.shape[0]
    sizes = (query_weight.shape[1], key_weight.shape[1], head_size)
    w_chunk, g_chunk = chunks_of(shard, width, own_hidden, groups)
    tokens_t, out_grad_t = tokens.T, out_grad.T

    fence = lax.optimization_barrier
    own_first, own_second = run_pack(
        where, w_chunk, query_weight, key_weight, value_weight,
        gate_weight, up_weight, down_weight.T, output_weight,
    )
    first_z = [own_first] + [shift(own_first, step) for step in range(1, groups)]
    second_z = [own_second] + [shift(own_second, step) for step in range(1, groups)]

    gain_rows = -(-shard // LANES)
    seg_rows = -(-toks // LANES)
    _, segs = fence((own_first, segments))
    small = jnp.zeros((SMALL * LANES,), bf16)
    at = 0
    for line, count in (
        (norm_gain, gain_rows),
        (second_gain, gain_rows),
        (query_gain, 1),
        (key_gain, 1),
        (segs.astype(bf16), seg_rows),
    ):
        small = small + jnp.pad(line, (at, SMALL * LANES - at - line.shape[0]))
        at += count * LANES
    small = small.reshape(SMALL, LANES)
    small_behind = jnp.stack([small] + [shift(small, step) for step in range(1, groups)])

    small_behind = small_behind.astype(f32)
    small_all = small_behind[lax.rem(place_z + groups - jnp.arange(groups), groups)]
    at = 0
    gains = []
    for count, length in ((gain_rows, shard), (gain_rows, shard), (1, head_part), (1, head_part)):
        gains.append(lined(small_all[:, at : at + count], length))
        at += count
    gain_first, gain_second, gain_query, gain_key = gains
    head_gains = jnp.concatenate([gain_query, gain_key])
    segs = small_behind[:, at : at + seg_rows].reshape(groups, -1)[:, :toks]
    there = (place_z >= jnp.arange(groups))[:, None]
    key_seg = jnp.where(there, segs, -1.0).reshape(1, -1)
    own_seg = segs[0][:, None]
    earlier = ((key_seg < own_seg) & (key_seg >= 0.0)).astype(jnp.int32)
    positions = place_z * toks + jnp.arange(toks, dtype=jnp.int32) - jnp.sum(earlier, axis=1)
    half = head_size // 2
    inverse = ROPE_BASE ** (-(jnp.arange(half, dtype=f32) * 2.0 / head_size))
    angles = positions.astype(f32)[:, None] * inverse[None, :]
    cosine, sine = jnp.cos(angles), jnp.sin(angles)

    near = spread_chip(jnp.stack(first_z))
    near, second_z = fence((near, second_z))
    whole = jnp.stack(second_z)
    near, gain_first, gain_second, head_gains, cosine, sine, own_seg, key_seg = fence(
        (near, gain_first, gain_second, head_gains, cosine, sine, own_seg, key_seg)
    )
    normed, raw, query, key_value, proj_weights = run_proj(
        where, near, hop(near, 1), tokens_t, gain_first, head_gains, cosine, sine, sizes
    )
    held = [key_value]
    for step in range(1, groups):
        ahead = [(i, i + step) for i in range(groups - step)]
        held.append(lax.ppermute(key_value, "grp", ahead))
    whole = jnp.stack([whole, hop_split(whole, 4, 2)])
    far_whole = hop_split(whole, 2, 4)
    whole, held = fence((whole, held))
    other = hop(whole, 1)
    attended, exact, probs = run_attend(query, own_seg, key_seg, held, sizes)
    far_whole, attended, other = fence((far_whole, attended, other))
    pieces = [whole, far_whole, other, hop(far_whole, 1)]
    layer_out_t, mixed_grad, attended_grad, second_sum, keep, send = run_mlp(
        where, w_chunk, g_chunk, pieces, attended, tokens_t, out_grad_t, gain_second
    )
    got = hop(send, 1)
    query_grad, *kv_parts = run_attend_back(query, attended_grad, exact, probs, held, sizes)
    got, query_grad, kv_parts = fence((got, query_grad, kv_parts))
    kv_back = [kv_parts[0]]
    for step in range(1, groups):
        back = [(i + step, i) for i in range(groups - step)]
        kv_back.append(lax.ppermute(kv_parts[step], "grp", back))
    near_got = hop_split(add_low(keep[1], got[1]), 2, 4)
    query_parts = run_query_back(
        query_grad, raw, normed, head_gains, cosine, sine, proj_weights, sizes
    )
    near_got, kv_back, query_parts = fence((near_got, kv_back, query_parts))
    far_got = hop_split(add_low(keep[0, 1], got[0, 1], near_got[1]), 4, 2)
    token_grad_t, late_keep, late_send = run_last(
        where, *query_parts, raw, normed, tokens_t, mixed_grad, gain_first, head_gains, cosine, sine,
        proj_weights, second_sum, kv_back, sizes,
    )
    late_got = hop(late_send, 1)
    far_got, late_got = fence((far_got, late_got))
    early = fold_grp(
        [add_low(keep[0, 0, d], got[0, 0, d], near_got[0, d], far_got[d]) for d in range(groups)]
    )
    late = fold_blocks(late_keep, late_got)
    near = spread_chip(jnp.concatenate([early, fold_grp(late)]))
    far = hop(near, 1)
    (
        gate_sum, up_sum, down_sum_t, output_sum, query_sum, key_sum, value_sum,
        first_sum, second_sum, query_gsum, key_gsum,
    ) = run_unpack(where, g_chunk, sizes, near, far, hidden_width, own_hidden, head_part)
    return (
        layer_out_t.T,
        token_grad_t.T,
        first_sum.reshape(-1),
        query_gsum.reshape(-1),
        key_gsum.reshape(-1),
        query_sum,
        key_sum,
        value_sum,
        output_sum,
        second_sum.reshape(-1),
        gate_sum,
        up_sum,
        down_sum_t.T,
    )


def solution(mesh):
    placed = (
        P(("rep", "grp"), None),
        P(("rep", "grp")),
        P(("rep", "grp"), None),
        P("grp"),
        P("grp"),
        P("grp"),
        P("grp", None),
        P("grp", None),
        P("grp", None),
        P("grp", None),
        P("grp"),
        P("grp", None),
        P("grp", None),
        P("grp", None),
    )
    return jax.shard_map(
        body,
        mesh=mesh,
        in_specs=placed,
        out_specs=(
            P(("rep", "grp"), None),
            P(("rep", "grp"), None),
            P("grp"),
            P("grp"),
            P("grp"),
            P("grp", None),
            P("grp", None),
            P("grp", None),
            P("grp", None),
            P("grp"),
            P("grp", None),
            P("grp", None),
            P("grp", None),
        ),
        check_vma=False,
    )
```

```python
import functools

import jax
import jax.numpy as jnp
from jax import lax
from jax.experimental import pallas as pl
from jax.experimental.pallas import tpu as pltpu
from jax.sharding import PartitionSpec as P

NORM_EPS = 1e-05
ROPE_BASE = 100000.0
LANES = 128
SMALL = 16
MIB = 1024 * 1024
PROBS_AHEAD = 2
AHEAD = 4
BIG = 58


def vmem():
    return pl.BlockSpec(memory_space=pltpu.VMEM)


def smem():
    return pl.BlockSpec(memory_space=pltpu.SMEM)


def hbm():
    return pl.BlockSpec(memory_space=pl.ANY)


def shape(dims, kind):
    return jax.ShapeDtypeStruct(dims, kind)


def options(mebibytes):
    return pltpu.CompilerParams(vmem_limit_bytes=mebibytes * MIB)


def cost():
    return pl.CostEstimate(flops=1, bytes_accessed=1024, transcendentals=0)


class Staged:
    def __init__(self, source, target, sem):
        self.copy = pltpu.make_async_copy(source, target, sem)
        self.copy.start()
        self.target, self.waiting = target, True
        self.shape, self.dtype = target.shape, target.dtype

    def wait(self):
        if self.waiting:
            self.copy.wait()
            self.waiting = False

    def __getitem__(self, index):
        self.wait()
        return self.target[index]


def staged_call(kernel, name, operands, out_shape, out_specs, scratch, mebibytes):
    kinds = [kind for kind, _ in operands]
    staged = [array for kind, array in operands if kind == "staged"]
    count = len(operands)

    def whole(*refs):
        sources, refs = refs[:count], refs[count:]
        if staged:
            targets, sems = refs[len(refs) - len(staged) - 1 : -1], refs[-1]
            refs = refs[: len(refs) - len(staged) - 1]
        given, at = [], 0
        for kind, source in zip(kinds, sources):
            if kind == "staged":
                source = Staged(source, targets[at], sems.at[at])
                at += 1
            given.append(source)
        kernel(*given, *refs)
        for operand in given:
            if isinstance(operand, Staged):
                operand.wait()

    specs = {"smem": smem, "vmem": vmem, "hbm": hbm, "staged": hbm}
    more = [pltpu.VMEM(array.shape, array.dtype) for array in staged]
    if staged:
        more.append(pltpu.SemaphoreType.DMA((len(staged),)))
    return pl.pallas_call(
        whole,
        out_shape=out_shape,
        in_specs=[specs[kind]() for kind in kinds],
        out_specs=out_specs,
        scratch_shapes=list(scratch) + more,
        compiler_params=options(mebibytes),
        cost_estimate=cost(),
        name=name,
    )(*[array for _, array in operands])


def kept(kind, *arrays):
    return [(kind, array) for array in arrays]


def hop(value, bit):
    count = lax.axis_size("rep")
    return lax.ppermute(value, "rep", [(i, i ^ bit) for i in range(count)])


def shift(value, step):
    count = lax.axis_size("grp")
    return lax.ppermute(value, "grp", [(i, (i + step) % count) for i in range(count)])


def rep_bits():
    index = lax.axis_index("rep")
    return index & 1, (index >> 1) & 1, (index >> 2) & 1


def hop_split(value, even, odd):
    count = lax.axis_size("rep")
    return lax.ppermute(value, "rep", [(i, i ^ (odd if i % 2 else even)) for i in range(count)])


def add_low(*values):
    total = values[0].astype(jnp.float32)
    for value in values[1:]:
        total = total + value.astype(jnp.float32)
    return total.astype(values[0].dtype)


def fold_grp(parts):
    f32 = jnp.float32
    total = parts[0].astype(f32)
    for step in range(1, len(parts)):
        total = total + shift(parts[step], step).astype(f32)
    total = total.astype(parts[0].dtype)
    bit = 8
    while bit < lax.axis_size("rep"):
        total = add_low(total, hop(total, bit))
        bit *= 2
    return total


def fold_blocks(keep, got):
    f32 = jnp.float32
    sums = [add_low(keep[j], got[j]) for j in range(4)]
    across, along, both = hop(sums[2], 2), hop(sums[1], 4), hop(sums[3], 6)
    return [
        (
            sums[0][d].astype(f32)
            + across[d].astype(f32)
            + along[d].astype(f32)
            + both[d].astype(f32)
        ).astype(keep.dtype)
        for d in range(lax.axis_size("grp"))
    ]


def spread_chip(own):
    return jnp.stack([own, hop(own, 4), hop(own, 2), hop(own, 6)])


def rows_of(vector, count):
    short = count * LANES - vector.shape[0]
    return jnp.pad(vector, (0, short)).reshape(count, LANES)


def lined(rows, length):
    return rows.reshape(rows.shape[0], -1)[:, :length].reshape(1, -1)


def place_scalars():
    bit_c, bit_x, bit_y = rep_bits()
    return jnp.stack([lax.axis_index("grp"), bit_c, bit_x, bit_y]).astype(jnp.int32)


def piece_row(where, core, high, low, rows):
    owner = where[1] ^ core
    first = jnp.where(owner == 0, where[2], where[3])
    second = jnp.where(owner == 0, where[3], where[2])
    index = owner * 4 + (first ^ high) * 2 + (second ^ low)
    return pl.multiple_of(index * (rows // 8), 16)


def piece_list():
    return [(c, h, l) for c in range(2) for h in range(2) for l in range(2)]


def dot(one, two, contract=(1, 0)):
    return lax.dot_general(
        one, two, (((contract[0],), (contract[1],)), ((), ())), preferred_element_type=jnp.float32
    )


def turned(value):
    return value.astype(jnp.float32).T.astype(value.dtype)


class Chunk:
    def __init__(self, dims, out_first):
        self.shard, self.width, self.own, self.groups = dims
        self.out_blocks = -(-self.width // LANES)
        self.rows_at, self.share_end, at = {}, [], 0

        def out_rows(at):
            for j in range(self.out_blocks):
                self.rows_at["out", j] = at
                at += self.shard
            return at

        if out_first:
            at = out_rows(at)
        self.out_end = at
        for share in range(self.own):
            for kind in ("gate", "up"):
                for f in self.blocks(share):
                    self.rows_at[kind, f] = at
                    at += self.shard
            self.rows_at["down", share] = at
            at += self.width
            self.share_end.append(at)
        if not out_first:
            at = out_rows(at)
        self.used = at
        self.rows = -(-at // 128) * 128
        self.part = self.rows // 8

    def blocks(self, share):
        return [owner * self.own + share for owner in range(self.groups)]


def chunks_of(shard, width, own_hidden, groups):
    dims = (shard, width, own_hidden // LANES, groups)
    return Chunk(dims, True), Chunk(dims, False)


def pack_kernel(chunk, where, query, key, value, gate, up, down_t, output, first, second, blocks, pack):
    shard, width = chunk.shard, chunk.width
    whole = jnp.concatenate([query[...], key[...], value[...]], 1)
    for j in range(blocks.shape[0]):
        stop = min((j + 1) * LANES, whole.shape[1])
        blocks[j, :, : stop - j * LANES] = whole[:, j * LANES : stop]
        if stop < (j + 1) * LANES:
            blocks[j, :, stop - j * LANES :] = jnp.zeros(
                (shard, (j + 1) * LANES - stop), whole.dtype
            )
    first[...] = blocks[where[1] * 4 + where[2] * 2 + where[3]]
    for (kind, j), at in chunk.rows_at.items():
        if kind == "down":
            pack[at : at + width, :] = down_t[:, j * LANES : (j + 1) * LANES]
            continue
        source = {"gate": gate, "up": up, "out": output}[kind]
        stop = min((j + 1) * LANES, source.shape[1])
        pack[at : at + shard, : stop - j * LANES] = source[:, j * LANES : stop]
        if stop < (j + 1) * LANES:
            pack[at : at + shard, stop - j * LANES :] = jnp.zeros(
                (shard, (j + 1) * LANES - stop), pack.dtype
            )
    if chunk.used < chunk.rows:
        pack[chunk.used :, :] = jnp.zeros((chunk.rows - chunk.used, LANES), pack.dtype)
    row = piece_row(where, 0, 0, 0, chunk.rows)
    second[...] = pack[pl.ds(row, chunk.part), :]


def run_pack(where, chunk, query, key, value, gate, up, down_t, output):
    kind = gate.dtype
    return staged_call(
        functools.partial(pack_kernel, chunk),
        "pack",
        kept("smem", where) + kept("staged", query, key, value, gate, up, down_t, output),
        (shape((chunk.shard, LANES), kind), shape((chunk.part, LANES), kind)),
        (vmem(), vmem()),
        [pltpu.VMEM((8, chunk.shard, LANES), kind), pltpu.VMEM((chunk.rows, LANES), kind)],
        BIG,
    )


def block_at(where, core, across, along):
    return (where[1] ^ core) * 4 + (where[2] ^ across) * 2 + (where[3] ^ along)


def unit_heads(raw, head_size):
    pairs = []
    for at in range(0, raw.shape[1], head_size):
        head = raw[:, at : at + head_size]
        factor = lax.rsqrt(jnp.mean(head * head, axis=1, keepdims=True) + NORM_EPS)
        pairs.append((head * factor, factor))
    return pairs


def proj_kernel(sizes, where, near, far, tokens_t, gain, head_gains, cosine, sine, *refs):
    f32, bf16 = jnp.float32, jnp.bfloat16
    q_width, kv_width, head_size = sizes
    normed_out, raw_out, query_out, kv_out, weights_out = refs
    groups = near.shape[1]
    inputs = tokens_t[...].astype(f32).T
    scale = lax.rsqrt(jnp.mean(inputs * inputs, axis=1, keepdims=True) + NORM_EPS)
    normed = (inputs * scale * gain[...]).astype(bf16)
    normed_out[...] = normed
    for j in range(8):
        core, across, along = j // 4, j // 2 % 2, j % 2
        place = (where[2] ^ across) * 2 + (where[3] ^ along)
        pieces = []
        for owner in range(groups):
            behind = lax.rem(where[0] + groups - owner, groups)
            pieces.append(
                jnp.where(where[1] == core, near[place, behind], far[place, behind])
            )
        weights_out[:, j * LANES : (j + 1) * LANES] = jnp.concatenate(pieces, 0)
    flat = weights_out[...]
    raw = dot(normed, flat)
    raw_out[...] = raw[:, : q_width + kv_width]
    half = head_size // 2
    cos, sin = cosine[...], sine[...]

    def turn(head):
        one, two = head[:, :half], head[:, half:]
        return jnp.concatenate([one * cos - two * sin, two * cos + one * sin], 1)

    heads = []
    for at, (unit, _) in enumerate(unit_heads(raw[:, : q_width + kv_width], head_size)):
        row = 0 if at * head_size < q_width else 1
        heads.append(turn(unit * head_gains[row : row + 1, :]).astype(bf16))
    queries = jnp.concatenate(heads[: q_width // head_size], 1)
    query_out[...] = (queries.astype(f32) * head_size ** (-0.5)).astype(bf16)
    values = raw[:, q_width + kv_width : q_width + 2 * kv_width].astype(bf16)
    kv_out[...] = jnp.concatenate(heads[q_width // head_size :] + [values], 1)


def run_proj(where, near, far, tokens_t, gain, head_gains, cosine, sine, sizes):
    f32, bf16 = jnp.float32, jnp.bfloat16
    q_width, kv_width, _ = sizes
    width, toks = tokens_t.shape
    return staged_call(
        functools.partial(proj_kernel, sizes),
        "proj",
        kept("smem", where)
        + kept("vmem", near, far)
        + kept("staged", tokens_t)
        + kept("vmem", gain, head_gains, cosine, sine),
        (
            shape((toks, width), bf16),
            shape((toks, q_width + kv_width), f32),
            shape((toks, q_width), bf16),
            shape((toks, 2 * kv_width), bf16),
            shape((width, 8 * LANES), bf16),
        ),
        (vmem(),) * 5,
        (),
        24,
    )


def attend_kernel(sizes, query, own_seg, key_seg, *refs):
    f32, bf16 = jnp.float32, jnp.bfloat16
    q_width, kv_width, head_size = sizes
    held = refs[: len(refs) - 6]
    attended, exact, probs_out, bias, probs, sems = refs[len(refs) - 6 :]
    toks = query.shape[0]
    same = own_seg[...] == key_seg[...]
    order = lax.broadcasted_iota(jnp.int32, same.shape, 0) - lax.broadcasted_iota(
        jnp.int32, same.shape, 1
    )
    later = lax.broadcasted_iota(jnp.int32, same.shape, 1) >= toks
    bias[...] = jnp.where(same & ((order >= 0) | later), 0.0, -1e30)
    outs = []
    per = q_width // kv_width
    for g in range(kv_width // head_size):
        cols = slice(g * head_size, (g + 1) * head_size)
        keys = jnp.concatenate([kv[:, cols] for kv in held], 0)
        cols = slice(kv_width + g * head_size, kv_width + (g + 1) * head_size)
        values = jnp.concatenate([kv[:, cols] for kv in held], 0)
        for head in range(g * per, (g + 1) * per):
            scores = dot(query[:, head * head_size : (head + 1) * head_size], keys, (1, 1))
            scores = scores + bias[...]
            powers = jnp.exp(scores)
            share = 1.0 / jnp.sum(powers, axis=1, keepdims=True)
            low = (powers * share).astype(bf16)
            probs[head] = low
            pltpu.make_async_copy(probs.at[head], probs_out.at[head], sems.at[head]).start()
            outs.append(dot(low, values))
    whole = jnp.concatenate(outs, 1)
    exact[...] = whole
    attended[...] = whole.astype(bf16)
    for head in range(probs.shape[0]):
        pltpu.make_async_copy(probs.at[head], probs_out.at[head], sems.at[head]).wait()


def run_attend(query, own_seg, key_seg, held, sizes):
    bf16 = jnp.bfloat16
    q_width, kv_width, head_size = sizes
    toks = query.shape[0]
    keys = toks * len(held)
    heads = q_width // head_size
    return staged_call(
        functools.partial(attend_kernel, sizes),
        "attend",
        kept("staged", query, own_seg, key_seg, *held),
        (
            shape((toks, q_width), bf16),
            shape((toks, q_width), jnp.float32),
            shape((heads, toks, keys), bf16),
        ),
        (vmem(), vmem(), hbm()),
        [
            pltpu.VMEM((toks, keys), jnp.float32),
            pltpu.VMEM((heads, toks, keys), bf16),
            pltpu.SemaphoreType.DMA((heads,)),
        ],
        BIG,
    )


def attend_back_kernel(sizes, query, grad, exact, *refs):
    f32, bf16 = jnp.float32, jnp.bfloat16
    q_width, kv_width, head_size = sizes
    probs, sems = refs[-2:]
    refs = refs[:-2]
    groups = (len(refs) - 2) // 2
    probs_in = refs[groups]
    refs = refs[:groups] + refs[groups + 1 :]
    copies = [
        pltpu.make_async_copy(probs_in.at[head], probs.at[head], sems.at[head])
        for head in range(probs.shape[0])
    ]
    for copy in copies[:PROBS_AHEAD]:
        copy.start()
    held = refs[:groups]
    query_grad = refs[groups]
    kv_grads = refs[groups + 1 :]
    toks = query.shape[0]
    per = q_width // kv_width
    query_t = query[...].astype(f32).T.astype(bf16)
    grad_t = grad[...].astype(f32).T.astype(bf16)
    outs, key_parts, value_parts = [], [], []
    for g in range(kv_width // head_size):
        cols = slice(g * head_size, (g + 1) * head_size)
        keys = jnp.concatenate([kv[:, cols] for kv in held], 0)
        cols = slice(kv_width + g * head_size, kv_width + (g + 1) * head_size)
        values = jnp.concatenate([kv[:, cols] for kv in held], 0)
        key_t = value_t = None
        for head in range(g * per, (g + 1) * per):
            cols = slice(head * head_size, (head + 1) * head_size)
            copies[head].wait()
            if head + PROBS_AHEAD < len(copies):
                copies[head + PROBS_AHEAD].start()
            low = probs[head]
            inner = jnp.sum(grad[:, cols].astype(f32) * exact[:, cols], axis=1, keepdims=True)
            scores = dot(grad[:, cols], values, (1, 1)) - inner
            scores = (low.astype(f32) * scores).astype(bf16)
            outs.append(dot(scores, keys))
            key_one = dot(query_t[cols, :], scores)
            value_one = dot(grad_t[cols, :], low)
            key_t = key_one if key_t is None else key_t + key_one
            value_t = value_one if value_t is None else value_t + value_one
        key_parts.append(key_t)
        value_parts.append(value_t)
    query_grad[...] = jnp.concatenate(outs, 1) * head_size ** (-0.5)
    both = jnp.concatenate(key_parts + value_parts, 0)
    for at, out in enumerate(kv_grads):
        out[...] = both[:, at * toks : (at + 1) * toks].T.astype(out.dtype)


def run_attend_back(query, grad, exact, probs, held, sizes):
    f32, bf16 = jnp.float32, jnp.bfloat16
    q_width, kv_width, head_size = sizes
    toks = query.shape[0]
    keys = toks * len(held)
    return staged_call(
        functools.partial(attend_back_kernel, sizes),
        "attend_back",
        kept("staged", query, grad, exact, *held) + kept("hbm", probs),
        (shape((toks, q_width), f32),) + tuple(shape((toks, 2 * kv_width), bf16) for _ in held),
        (vmem(),) * (1 + len(held)),
        [pltpu.VMEM(probs.shape, bf16), pltpu.SemaphoreType.DMA((probs.shape[0],))],
        BIG,
    )


def mlp_kernel(w_chunk, g_chunk, where, attended, tokens_t, out_grad_t, gain, *refs):
    f32, bf16 = jnp.float32, jnp.bfloat16
    pieces, refs = refs[:4], refs[4:]
    layer_out_t, mixed_grad, attended_grad, gain_grad, keep, send = refs[:6]
    weights, grads, sem_in, sem_out = refs[6:]
    width, toks = tokens_t.shape
    shard, groups, out_blocks = w_chunk.shard, w_chunk.groups, w_chunk.out_blocks

    def piece_place(number):
        core = number // 4
        first, second = (where[2], where[3]) if core == 0 else (where[3], where[2])
        return where[1] ^ core, first ^ (number // 2 % 2), second ^ (number % 2)

    def fetch(number):
        core, high, low = piece_place(number)
        for place in range(4):

            @pl.when(core * 2 + high == place)
            def _():
                pltpu.make_async_copy(
                    pieces[place].at[low],
                    weights.at[:, pl.ds(number * w_chunk.part, w_chunk.part)],
                    sem_in.at[number],
                ).start()

    fetched = waited = 0

    def fetch_to(count):
        nonlocal fetched
        while fetched < min(count, 8):
            fetch(fetched)
            fetched += 1

    def need(rows):
        nonlocal waited
        while waited < 8 and waited * w_chunk.part < rows:
            fetch_to(waited + AHEAD)
            here = weights.at[:, pl.ds(waited * w_chunk.part, w_chunk.part)]
            pltpu.make_async_copy(here, here, sem_in.at[waited]).wait()
            waited += 1

    left = 0

    def leave(rows):
        nonlocal left
        while left < 8 and (left + 1) * g_chunk.part <= rows:
            core, high, low = piece_place(left)
            for away, out in ((0, keep), (1, send)):

                @pl.when(core == away)
                def _(number=left, high=high, low=low, away=away, out=out):
                    pltpu.make_async_copy(
                        grads.at[:, pl.ds(number * g_chunk.part, g_chunk.part)],
                        out.at[high, low],
                        sem_out.at[away],
                    ).start()

            left += 1

    behind = [lax.rem(where[0] + groups - owner, groups) for owner in range(groups)]
    ahead_of = [lax.rem(owner + groups - where[0], groups) for owner in range(groups)]

    def column(kind, f):
        at = w_chunk.rows_at[kind, f]
        return jnp.concatenate([weights[place, at : at + shard, :] for place in behind], 0)

    def store(kind, f, block):
        at = g_chunk.rows_at[kind, f]
        for owner in range(groups):
            grads[ahead_of[owner], at : at + shard, :] = block[owner * shard : (owner + 1) * shard]

    fetch_to(AHEAD)
    out_t = out_grad_t[...]
    upstream = turned(out_t)
    inputs = tokens_t[...].astype(f32).T
    att_t = turned(attended[...])
    if g_chunk.used < g_chunk.rows:
        grads[:, g_chunk.used :, :] = jnp.zeros(
            (groups, g_chunk.rows - g_chunk.used, LANES), bf16
        )
    need(w_chunk.out_end)
    output_w = jnp.concatenate([column("out", j) for j in range(out_blocks)], 1)[:, :width]
    mixed = inputs + dot(attended[...], output_w)
    scale = lax.rsqrt(jnp.mean(mixed * mixed, axis=1, keepdims=True) + NORM_EPS)
    unit = mixed * scale
    gained = gain[...]
    normed = (unit * gained).astype(bf16)
    normed_t = turned(normed)
    back = jnp.zeros(mixed.shape, f32)
    ahead = mixed
    for share in range(w_chunk.own):
        need(w_chunk.share_end[share])
        blocks = w_chunk.blocks(share)
        down_at = w_chunk.rows_at["down", share]
        down_to = g_chunk.rows_at["down", share]
        for pair in range(0, len(blocks), 2):
            some = blocks[pair : pair + 2]
            gate_w = jnp.concatenate([column("gate", f) for f in some], 1)
            up_w = jnp.concatenate([column("up", f) for f in some], 1)
            down_w = jnp.concatenate(
                [weights[behind[f // w_chunk.own], down_at : down_at + width, :] for f in some], 1
            )
            gate = dot(normed, gate_w)
            up = dot(normed, up_w)
            hidden_grad = dot(upstream, down_w)
            sigmoid = 1.0 / (1.0 + jnp.exp(-gate))
            silu = gate * sigmoid
            hidden = (silu * up).astype(bf16)
            gate_low = (hidden_grad * up * (sigmoid * (1.0 + gate * (1.0 - sigmoid)))).astype(bf16)
            up_low = (hidden_grad * silu).astype(bf16)
            ahead = ahead + dot(hidden, down_w, (1, 1))
            back = back + dot(gate_low, gate_w, (1, 1)) + dot(up_low, up_w, (1, 1))
            gate_wg = dot(normed_t, gate_low).astype(bf16)
            up_wg = dot(normed_t, up_low).astype(bf16)
            down_wg = dot(out_t, hidden).astype(bf16)
            for at, f in enumerate(some):
                cols = slice(at * LANES, (at + 1) * LANES)
                store("gate", f, gate_wg[:, cols])
                store("up", f, up_wg[:, cols])
                grads[ahead_of[f // g_chunk.own], down_to : down_to + width, :] = down_wg[:, cols]
        leave(g_chunk.share_end[share])
    layer_out_t[...] = ahead.T.astype(bf16)
    gain_grad[...] = jnp.sum(back * unit, axis=0, keepdims=True)
    inner = back * gained
    through = scale * (inner - unit * jnp.mean(inner * unit, axis=1, keepdims=True))
    mixed_back = upstream.astype(f32) + through
    mixed_grad[...] = mixed_back
    branch = mixed_back.astype(bf16)
    attended_grad[...] = dot(branch, output_w, (1, 1)).astype(bf16)
    output_wg = dot(att_t, branch)
    for j in range(out_blocks):
        block = output_wg[:, j * LANES : min((j + 1) * LANES, width)]
        if block.shape[1] < LANES:
            block = jnp.concatenate(
                [block, jnp.zeros((block.shape[0], LANES - block.shape[1]), f32)], 1
            )
        store("out", j, block.astype(bf16))
    leave(g_chunk.rows)
    pltpu.make_async_copy(keep, keep, sem_out.at[0]).wait()
    pltpu.make_async_copy(send, send, sem_out.at[1]).wait()


def run_mlp(where, w_chunk, g_chunk, pieces, attended, tokens_t, out_grad_t, gain):
    f32, bf16 = jnp.float32, jnp.bfloat16
    groups = w_chunk.groups
    width, toks = tokens_t.shape
    packed = shape((2, 2, groups, g_chunk.part, LANES), bf16)
    return staged_call(
        functools.partial(mlp_kernel, w_chunk, g_chunk),
        "mlp",
        kept("smem", where) + kept("staged", attended, tokens_t, out_grad_t, gain) + kept("hbm", *pieces),
        (
            shape((width, toks), bf16),
            shape((toks, width), f32),
            shape((toks, width), bf16),
            shape((1, width), f32),
            packed,
            packed,
        ),
        (vmem(),) * 4 + (hbm(),) * 2,
        [pltpu.VMEM((groups, chunk.rows, LANES), bf16) for chunk in (w_chunk, g_chunk)]
        + [pltpu.SemaphoreType.DMA((8,)), pltpu.SemaphoreType.DMA((2,))],
        BIG,
    )


def heads_back(grad, raw, cos, sin, gain, head_size):
    half = head_size // 2
    lows, total = [], jnp.zeros((1, head_size), jnp.float32)
    for at, (unit, factor) in enumerate(unit_heads(raw, head_size)):
        at *= head_size
        one, two = grad[:, at : at + half], grad[:, at + half : at + head_size]
        back = jnp.concatenate([one * cos + two * sin, two * cos - one * sin], 1)
        total = total + jnp.sum(back * unit, axis=0, keepdims=True)
        inner = back * gain
        lows.append(factor * (inner - unit * jnp.mean(inner * unit, axis=1, keepdims=True)))
    return lows, total


def query_back_kernel(sizes, query_grad, raw, normed, head_gains, cosine, sine, weights, products, back, total):
    q_width, _, head_size = sizes
    lows, total[...] = heads_back(
        query_grad[...], raw[:, :q_width], cosine[...], sine[...], head_gains[0:1, :], head_size
    )
    low = jnp.concatenate(lows, 1).astype(products.dtype)
    back[...] = dot(low, weights[:, :q_width], (1, 1))
    products[...] = dot(turned(normed[...]), low).astype(products.dtype)


def run_query_back(query_grad, raw, normed, head_gains, cosine, sine, weights, sizes):
    f32 = jnp.float32
    q_width, _, head_size = sizes
    toks, width = normed.shape
    return staged_call(
        functools.partial(query_back_kernel, sizes),
        "query_back",
        kept("vmem", query_grad, raw, normed, head_gains, cosine, sine, weights),
        (shape((width, q_width), normed.dtype), shape((toks, width), f32), shape((1, head_size), f32)),
        (vmem(),) * 3,
        (),
        24,
    )


def last_kernel(sizes, where, products, back, q_total, raw, normed, tokens_t, mixed_grad, gain, head_gains, cosine, sine, weights, second, *refs):
    f32, bf16 = jnp.float32, jnp.bfloat16
    q_width, kv_width, head_size = sizes
    kv_parts = refs[: len(refs) - 4]
    token_grad_t, keep, send, grads = refs[len(refs) - 4 :]
    count, groups, rows, _ = grads.shape
    width, toks = tokens_t.shape
    shard = width // groups
    kv_grad = kv_parts[0][...].astype(f32)
    for part in kv_parts[1:]:
        kv_grad = kv_grad + part[...].astype(f32)
    lows, k_total = heads_back(
        kv_grad, raw[:, q_width:], cosine[...], sine[...], head_gains[1:2, :], head_size
    )
    low = jnp.concatenate(lows + [kv_grad[:, kv_width:]], 1).astype(bf16)
    short = count * LANES - q_width - 2 * kv_width
    pieces = [products[...], dot(turned(normed[...]), low).astype(bf16)]
    if short:
        pieces.append(jnp.zeros((width, short), bf16))
    blocks = jnp.concatenate(pieces, 1)
    for j in range(count):
        for owner in range(groups):
            grads[j, owner, :shard, :] = blocks[
                owner * shard : (owner + 1) * shard, j * LANES : (j + 1) * LANES
            ]
            grads[j, owner, shard:, :] = jnp.zeros((rows - shard, LANES), bf16)
    whole = back[...] + dot(low, weights[:, q_width : q_width + 2 * kv_width], (1, 1))
    inputs = tokens_t[...].astype(f32).T
    scale = lax.rsqrt(jnp.mean(inputs * inputs, axis=1, keepdims=True) + NORM_EPS)
    unit = inputs * scale
    first = jnp.sum(whole * unit, axis=0, keepdims=True)
    inner = whole * gain[...]
    whole = mixed_grad[...] + scale * (inner - unit * jnp.mean(inner * unit, axis=1, keepdims=True))
    token_grad_t[...] = whole.T

    def line(vector):
        short = LANES - vector.shape[1]
        return jnp.concatenate([vector, jnp.zeros((1, short), f32)], 1) if short else vector

    head_part = head_size // groups
    for owner in range(groups):
        lines = []
        for vector in (first, second[...]):
            mine = vector[:, owner * shard : (owner + 1) * shard]
            lines += [line(mine[:, at : at + LANES]) for at in range(0, shard, LANES)]
        for vector in (q_total[...], k_total):
            lines.append(line(vector[:, owner * head_part : (owner + 1) * head_part]))
        lines.append(jnp.zeros((rows - shard - len(lines), LANES), f32))
        grads[0, owner, shard:, :] = jnp.concatenate(lines, 0).astype(bf16)
    for core in range(2):
        for across in range(2):
            for along in range(2):
                block = block_at(where, core, across, along)
                for step in range(groups):
                    owner = lax.rem(where[0] + step, groups)
                    (send if core else keep)[across * 2 + along, step] = grads[block, owner]


def run_last(where, products, back, q_total, raw, normed, tokens_t, mixed_grad, gain, head_gains, cosine, sine, weights, second, kv_parts, sizes):
    width = tokens_t.shape[0]
    groups = lax.axis_size("grp")
    rows = width // groups + SMALL
    packed = shape((4, groups, rows, LANES), jnp.bfloat16)
    return staged_call(
        functools.partial(last_kernel, sizes),
        "last",
        kept("smem", where)
        + kept("vmem", products, back, q_total, raw, normed)
        + kept("staged", tokens_t)
        + kept("vmem", mixed_grad, gain, head_gains, cosine, sine, weights, second, *kv_parts),
        (shape(tokens_t.shape, jnp.float32), packed, packed),
        (vmem(),) * 3,
        [pltpu.VMEM((8, groups, rows, LANES), jnp.bfloat16)],
        24,
    )


def unpack_kernel(sizes, chunk, where, near, far, *refs):
    f32 = jnp.float32
    q_width, kv_width, _ = sizes
    gate, up, down_t, output, query, key, value = refs[:7]
    lines_out = refs[7:11]
    pack = refs[11]
    shard, width = chunk.shard, chunk.width
    projections = []
    small = None
    for core in range(2):
        for across in range(2):
            for along in range(2):
                place = (where[2] ^ across) * 2 + (where[3] ^ along)
                piece = jnp.where(where[1] == core, near[place], far[place])
                at = chunk.part
                high, low = (across, along) if core == 0 else (along, across)
                row = (core * 4 + high * 2 + low) * chunk.part
                pack[row : row + chunk.part, :] = piece[:at]
                projections.append(piece[at : at + shard])
                if small is None:
                    small = piece[at + shard :].astype(f32)
    for (kind, j), at in chunk.rows_at.items():
        if kind == "down":
            down_t[:, j * LANES : (j + 1) * LANES] = pack[at : at + width].astype(f32)
            continue
        out = {"gate": gate, "up": up, "out": output}[kind]
        stop = min((j + 1) * LANES, out.shape[1])
        out[:, j * LANES : stop] = pack[at : at + shard].astype(f32)[:, : stop - j * LANES]
    whole = jnp.concatenate(projections, 1).astype(f32)
    query[...] = whole[:, :q_width]
    key[...] = whole[:, q_width : q_width + kv_width]
    value[...] = whole[:, q_width + kv_width : q_width + 2 * kv_width]
    row = 0
    for out in lines_out:
        for at in range(0, out.shape[1], LANES):
            stop = min(at + LANES, out.shape[1])
            out[:, at:stop] = small[row : row + 1, : stop - at]
            row += 1


def run_unpack(where, chunk, sizes, near, far, hidden_width, own_hidden, head_part):
    f32 = jnp.float32
    q_width, kv_width, _ = sizes
    shard, width = chunk.shard, chunk.width
    return staged_call(
        functools.partial(unpack_kernel, sizes, chunk),
        "unpack",
        kept("smem", where) + kept("vmem", near, far),
        (
            shape((shard, hidden_width), f32),
            shape((shard, hidden_width), f32),
            shape((width, own_hidden), f32),
            shape((shard, width), f32),
            shape((shard, q_width), f32),
            shape((shard, kv_width), f32),
            shape((shard, kv_width), f32),
            shape((1, shard), f32),
            shape((1, shard), f32),
            shape((1, head_part), f32),
            shape((1, head_part), f32),
        ),
        (vmem(),) * 11,
        [pltpu.VMEM((chunk.rows, LANES), near.dtype)],
        24,
    )


def body(
    tokens,
    segments,
    out_grad,
    norm_gain,
    query_gain,
    key_gain,
    query_weight,
    key_weight,
    value_weight,
    output_weight,
    second_gain,
    gate_weight,
    up_weight,
    down_weight,
):
    f32, bf16 = jnp.float32, jnp.bfloat16
    groups = lax.axis_size("grp")
    place_z = lax.axis_index("grp")
    where = place_scalars()
    toks, width = tokens.shape
    shard = norm_gain.shape[0]
    head_part = query_gain.shape[0]
    head_size = head_part * groups
    hidden_width, own_hidden = gate_weight.shape[1], down_weight.shape[0]
    sizes = (query_weight.shape[1], key_weight.shape[1], head_size)
    w_chunk, g_chunk = chunks_of(shard, width, own_hidden, groups)
    tokens_t, out_grad_t = tokens.T, out_grad.T

    fence = lax.optimization_barrier
    own_first, own_second = run_pack(
        where, w_chunk, query_weight, key_weight, value_weight,
        gate_weight, up_weight, down_weight.T, output_weight,
    )
    first_z = [own_first] + [shift(own_first, step) for step in range(1, groups)]
    second_z = [own_second] + [shift(own_second, step) for step in range(1, groups)]

    gain_rows = -(-shard // LANES)
    seg_rows = -(-toks // LANES)
    _, segs = fence((own_first, segments))
    small = jnp.zeros((SMALL * LANES,), bf16)
    at = 0
    for line, count in (
        (norm_gain, gain_rows),
        (second_gain, gain_rows),
        (query_gain, 1),
        (key_gain, 1),
        (segs.astype(bf16), seg_rows),
    ):
        small = small + jnp.pad(line, (at, SMALL * LANES - at - line.shape[0]))
        at += count * LANES
    small = small.reshape(SMALL, LANES)
    small_behind = jnp.stack([small] + [shift(small, step) for step in range(1, groups)])

    small_behind = small_behind.astype(f32)
    small_all = small_behind[lax.rem(place_z + groups - jnp.arange(groups), groups)]
    at = 0
    gains = []
    for count, length in ((gain_rows, shard), (gain_rows, shard), (1, head_part), (1, head_part)):
        gains.append(lined(small_all[:, at : at + count], length))
        at += count
    gain_first, gain_second, gain_query, gain_key = gains
    head_gains = jnp.concatenate([gain_query, gain_key])
    segs = small_behind[:, at : at + seg_rows].reshape(groups, -1)[:, :toks]
    there = (place_z >= jnp.arange(groups))[:, None]
    key_seg = jnp.where(there, segs, -1.0).reshape(1, -1)
    own_seg = segs[0][:, None]
    earlier = ((key_seg < own_seg) & (key_seg >= 0.0)).astype(jnp.int32)
    positions = place_z * toks + jnp.arange(toks, dtype=jnp.int32) - jnp.sum(earlier, axis=1)
    half = head_size // 2
    inverse = ROPE_BASE ** (-(jnp.arange(half, dtype=f32) * 2.0 / head_size))
    angles = positions.astype(f32)[:, None] * inverse[None, :]
    cosine, sine = jnp.cos(angles), jnp.sin(angles)

    near = spread_chip(jnp.stack(first_z))
    near, second_z = fence((near, second_z))
    whole = jnp.stack(second_z)
    near, gain_first, gain_second, head_gains, cosine, sine, own_seg, key_seg = fence(
        (near, gain_first, gain_second, head_gains, cosine, sine, own_seg, key_seg)
    )
    normed, raw, query, key_value, proj_weights = run_proj(
        where, near, hop(near, 1), tokens_t, gain_first, head_gains, cosine, sine, sizes
    )
    held = [key_value]
    for step in range(1, groups):
        ahead = [(i, i + step) for i in range(groups - step)]
        held.append(lax.ppermute(key_value, "grp", ahead))
    whole = jnp.stack([whole, hop_split(whole, 4, 2)])
    far_whole = hop_split(whole, 2, 4)
    whole, held = fence((whole, held))
    other = hop(whole, 1)
    attended, exact, probs = run_attend(query, own_seg, key_seg, held, sizes)
    far_whole, attended, other = fence((far_whole, attended, other))
    pieces = [whole, far_whole, other, hop(far_whole, 1)]
    layer_out_t, mixed_grad, attended_grad, second_sum, keep, send = run_mlp(
        where, w_chunk, g_chunk, pieces, attended, tokens_t, out_grad_t, gain_second
    )
    got = hop(send, 1)
    query_grad, *kv_parts = run_attend_back(query, attended_grad, exact, probs, held, sizes)
    got, query_grad, kv_parts = fence((got, query_grad, kv_parts))
    kv_back = [kv_parts[0]]
    for step in range(1, groups):
        back = [(i + step, i) for i in range(groups - step)]
        kv_back.append(lax.ppermute(kv_parts[step], "grp", back))
    near_got = hop_split(add_low(keep[1], got[1]), 2, 4)
    query_parts = run_query_back(
        query_grad, raw, normed, head_gains, cosine, sine, proj_weights, sizes
    )
    near_got, kv_back, query_parts = fence((near_got, kv_back, query_parts))
    far_got = hop_split(add_low(keep[0, 1], got[0, 1], near_got[1]), 4, 2)
    token_grad_t, late_keep, late_send = run_last(
        where, *query_parts, raw, normed, tokens_t, mixed_grad, gain_first, head_gains, cosine, sine,
        proj_weights, second_sum, kv_back, sizes,
    )
    late_got = hop(late_send, 1)
    far_got, late_got = fence((far_got, late_got))
    early = fold_grp(
        [add_low(keep[0, 0, d], got[0, 0, d], near_got[0, d], far_got[d]) for d in range(groups)]
    )
    late = fold_blocks(late_keep, late_got)
    near = spread_chip(jnp.concatenate([early, fold_grp(late)]))
    far = hop(near, 1)
    (
        gate_sum, up_sum, down_sum_t, output_sum, query_sum, key_sum, value_sum,
        first_sum, second_sum, query_gsum, key_gsum,
    ) = run_unpack(where, g_chunk, sizes, near, far, hidden_width, own_hidden, head_part)
    return (
        layer_out_t.T,
        token_grad_t.T,
        first_sum.reshape(-1),
        query_gsum.reshape(-1),
        key_gsum.reshape(-1),
        query_sum,
        key_sum,
        value_sum,
        output_sum,
        second_sum.reshape(-1),
        gate_sum,
        up_sum,
        down_sum_t.T,
    )


def solution(mesh):
    placed = (
        P(("rep", "grp"), None),
        P(("rep", "grp")),
        P(("rep", "grp"), None),
        P("grp"),
        P("grp"),
        P("grp"),
        P("grp", None),
        P("grp", None),
        P("grp", None),
        P("grp", None),
        P("grp"),
        P("grp", None),
        P("grp", None),
        P("grp", None),
    )
    return jax.shard_map(
        body,
        mesh=mesh,
        in_specs=placed,
        out_specs=(
            P(("rep", "grp"), None),
            P(("rep", "grp"), None),
            P("grp"),
            P("grp"),
            P("grp"),
            P("grp", None),
            P("grp", None),
            P("grp", None),
            P("grp", None),
            P("grp"),
            P("grp", None),
            P("grp", None),
            P("grp", None),
        ),
        check_vma=False,
    )
```

```python
import functools

import jax
import jax.numpy as jnp
from jax import lax
from jax.experimental import pallas as pl
from jax.experimental.pallas import tpu as pltpu
from jax.sharding import PartitionSpec as P

NORM_EPS = 1e-05
ROPE_BASE = 100000.0
LANES = 128
SMALL = 16
MIB = 1024 * 1024
PROBS_AHEAD = 2
AHEAD = 4
BIG = 58


def vmem():
    return pl.BlockSpec(memory_space=pltpu.VMEM)


def smem():
    return pl.BlockSpec(memory_space=pltpu.SMEM)


def hbm():
    return pl.BlockSpec(memory_space=pl.ANY)


def shape(dims, kind):
    return jax.ShapeDtypeStruct(dims, kind)


def options(mebibytes):
    return pltpu.CompilerParams(vmem_limit_bytes=mebibytes * MIB)


def cost():
    return pl.CostEstimate(flops=1, bytes_accessed=1024, transcendentals=0)


class Staged:
    def __init__(self, source, target, sem):
        self.copy = pltpu.make_async_copy(source, target, sem)
        self.copy.start()
        self.target, self.waiting = target, True
        self.shape, self.dtype = target.shape, target.dtype

    def wait(self):
        if self.waiting:
            self.copy.wait()
            self.waiting = False

    def __getitem__(self, index):
        self.wait()
        return self.target[index]


def staged_call(kernel, name, operands, out_shape, out_specs, scratch, mebibytes):
    kinds = [kind for kind, _ in operands]
    staged = [array for kind, array in operands if kind == "staged"]
    count = len(operands)

    def whole(*refs):
        sources, refs = refs[:count], refs[count:]
        if staged:
            targets, sems = refs[len(refs) - len(staged) - 1 : -1], refs[-1]
            refs = refs[: len(refs) - len(staged) - 1]
        given, at = [], 0
        for kind, source in zip(kinds, sources):
            if kind == "staged":
                source = Staged(source, targets[at], sems.at[at])
                at += 1
            given.append(source)
        kernel(*given, *refs)
        for operand in given:
            if isinstance(operand, Staged):
                operand.wait()

    specs = {"smem": smem, "vmem": vmem, "hbm": hbm, "staged": hbm}
    more = [pltpu.VMEM(array.shape, array.dtype) for array in staged]
    if staged:
        more.append(pltpu.SemaphoreType.DMA((len(staged),)))
    return pl.pallas_call(
        whole,
        out_shape=out_shape,
        in_specs=[specs[kind]() for kind in kinds],
        out_specs=out_specs,
        scratch_shapes=list(scratch) + more,
        compiler_params=options(mebibytes),
        cost_estimate=cost(),
        name=name,
    )(*[array for _, array in operands])


def kept(kind, *arrays):
    return [(kind, array) for array in arrays]


def hop(value, bit):
    count = lax.axis_size("rep")
    return lax.ppermute(value, "rep", [(i, i ^ bit) for i in range(count)])


def shift(value, step):
    count = lax.axis_size("grp")
    return lax.ppermute(value, "grp", [(i, (i + step) % count) for i in range(count)])


def rep_bits():
    index = lax.axis_index("rep")
    return index & 1, (index >> 1) & 1, (index >> 2) & 1


def hop_split(value, even, odd):
    count = lax.axis_size("rep")
    return lax.ppermute(value, "rep", [(i, i ^ (odd if i % 2 else even)) for i in range(count)])


def add_low(*values):
    total = values[0].astype(jnp.float32)
    for value in values[1:]:
        total = total + value.astype(jnp.float32)
    return total.astype(values[0].dtype)


def fold_grp(parts):
    f32 = jnp.float32
    total = parts[0].astype(f32)
    for step in range(1, len(parts)):
        total = total + shift(parts[step], step).astype(f32)
    total = total.astype(parts[0].dtype)
    bit = 8
    while bit < lax.axis_size("rep"):
        total = add_low(total, hop(total, bit))
        bit *= 2
    return total


def fold_blocks(keep, got):
    f32 = jnp.float32
    sums = [add_low(keep[j], got[j]) for j in range(4)]
    across, along, both = hop(sums[2], 2), hop(sums[1], 4), hop(sums[3], 6)
    return [
        (
            sums[0][d].astype(f32)
            + across[d].astype(f32)
            + along[d].astype(f32)
            + both[d].astype(f32)
        ).astype(keep.dtype)
        for d in range(lax.axis_size("grp"))
    ]


def spread_chip(own):
    return jnp.stack([own, hop(own, 4), hop(own, 2), hop(own, 6)])


def rows_of(vector, count):
    short = count * LANES - vector.shape[0]
    return jnp.pad(vector, (0, short)).reshape(count, LANES)


def lined(rows, length):
    return rows.reshape(rows.shape[0], -1)[:, :length].reshape(1, -1)


def place_scalars():
    bit_c, bit_x, bit_y = rep_bits()
    return jnp.stack([lax.axis_index("grp"), bit_c, bit_x, bit_y]).astype(jnp.int32)


def piece_row(where, core, high, low, rows):
    owner = where[1] ^ core
    first = jnp.where(owner == 0, where[2], where[3])
    second = jnp.where(owner == 0, where[3], where[2])
    index = owner * 4 + (first ^ high) * 2 + (second ^ low)
    return pl.multiple_of(index * (rows // 8), 16)


def piece_list():
    return [(c, h, l) for c in range(2) for h in range(2) for l in range(2)]


def dot(one, two, contract=(1, 0)):
    return lax.dot_general(
        one, two, (((contract[0],), (contract[1],)), ((), ())), preferred_element_type=jnp.float32
    )


def turned(value):
    return value.astype(jnp.float32).T.astype(value.dtype)


class Chunk:
    def __init__(self, dims, out_first):
        self.shard, self.width, self.own, self.groups = dims
        self.out_blocks = -(-self.width // LANES)
        self.rows_at, self.share_end, at = {}, [], 0

        def out_rows(at):
            for j in range(self.out_blocks):
                self.rows_at["out", j] = at
                at += self.shard
            return at

        if out_first:
            at = out_rows(at)
        self.out_end = at
        for share in range(self.own):
            for kind in ("gate", "up"):
                for f in self.blocks(share):
                    self.rows_at[kind, f] = at
                    at += self.shard
            self.rows_at["down", share] = at
            at += self.width
            self.share_end.append(at)
        if not out_first:
            at = out_rows(at)
        self.used = at
        self.rows = -(-at // 128) * 128
        self.part = self.rows // 8

    def blocks(self, share):
        return [owner * self.own + share for owner in range(self.groups)]


def chunks_of(shard, width, own_hidden, groups):
    dims = (shard, width, own_hidden // LANES, groups)
    return Chunk(dims, True), Chunk(dims, False)


def pack_kernel(chunk, where, query, key, value, gate, up, down_t, output, first, second, blocks, pack):
    shard, width = chunk.shard, chunk.width
    whole = jnp.concatenate([query[...], key[...], value[...]], 1)
    for j in range(blocks.shape[0]):
        stop = min((j + 1) * LANES, whole.shape[1])
        blocks[j, :, : stop - j * LANES] = whole[:, j * LANES : stop]
        if stop < (j + 1) * LANES:
            blocks[j, :, stop - j * LANES :] = jnp.zeros(
                (shard, (j + 1) * LANES - stop), whole.dtype
            )
    first[...] = blocks[where[1] * 4 + where[2] * 2 + where[3]]
    for (kind, j), at in chunk.rows_at.items():
        if kind == "down":
            pack[at : at + width, :] = down_t[:, j * LANES : (j + 1) * LANES]
            continue
        source = {"gate": gate, "up": up, "out": output}[kind]
        stop = min((j + 1) * LANES, source.shape[1])
        pack[at : at + shard, : stop - j * LANES] = source[:, j * LANES : stop]
        if stop < (j + 1) * LANES:
            pack[at : at + shard, stop - j * LANES :] = jnp.zeros(
                (shard, (j + 1) * LANES - stop), pack.dtype
            )
    if chunk.used < chunk.rows:
        pack[chunk.used :, :] = jnp.zeros((chunk.rows - chunk.used, LANES), pack.dtype)
    row = piece_row(where, 0, 0, 0, chunk.rows)
    second[...] = pack[pl.ds(row, chunk.part), :]


def run_pack(where, chunk, query, key, value, gate, up, down_t, output):
    kind = gate.dtype
    return staged_call(
        functools.partial(pack_kernel, chunk),
        "pack",
        kept("smem", where) + kept("staged", query, key, value, gate, up, down_t, output),
        (shape((chunk.shard, LANES), kind), shape((chunk.part, LANES), kind)),
        (vmem(), vmem()),
        [pltpu.VMEM((8, chunk.shard, LANES), kind), pltpu.VMEM((chunk.rows, LANES), kind)],
        BIG,
    )


def block_at(where, core, across, along):
    return (where[1] ^ core) * 4 + (where[2] ^ across) * 2 + (where[3] ^ along)


def unit_heads(raw, head_size):
    pairs = []
    for at in range(0, raw.shape[1], head_size):
        head = raw[:, at : at + head_size]
        factor = lax.rsqrt(jnp.mean(head * head, axis=1, keepdims=True) + NORM_EPS)
        pairs.append((head * factor, factor))
    return pairs


def proj_kernel(sizes, where, near, far, tokens_t, gain, head_gains, cosine, sine, *refs):
    f32, bf16 = jnp.float32, jnp.bfloat16
    q_width, kv_width, head_size = sizes
    normed_out, raw_out, query_out, kv_out, weights_out = refs
    groups = near.shape[1]
    inputs = tokens_t[...].astype(f32).T
    scale = lax.rsqrt(jnp.mean(inputs * inputs, axis=1, keepdims=True) + NORM_EPS)
    normed = (inputs * scale * gain[...]).astype(bf16)
    normed_out[...] = normed
    for j in range(8):
        core, across, along = j // 4, j // 2 % 2, j % 2
        place = (where[2] ^ across) * 2 + (where[3] ^ along)
        pieces = []
        for owner in range(groups):
            behind = lax.rem(where[0] + groups - owner, groups)
            pieces.append(
                jnp.where(where[1] == core, near[place, behind], far[place, behind])
            )
        weights_out[:, j * LANES : (j + 1) * LANES] = jnp.concatenate(pieces, 0)
    flat = weights_out[...]
    raw = dot(normed, flat)
    raw_out[...] = raw[:, : q_width + kv_width]
    half = head_size // 2
    cos, sin = cosine[...], sine[...]

    def turn(head):
        one, two = head[:, :half], head[:, half:]
        return jnp.concatenate([one * cos - two * sin, two * cos + one * sin], 1)

    heads = []
    for at, (unit, _) in enumerate(unit_heads(raw[:, : q_width + kv_width], head_size)):
        row = 0 if at * head_size < q_width else 1
        heads.append(turn(unit * head_gains[row : row + 1, :]).astype(bf16))
    queries = jnp.concatenate(heads[: q_width // head_size], 1)
    query_out[...] = (queries.astype(f32) * head_size ** (-0.5)).astype(bf16)
    values = raw[:, q_width + kv_width : q_width + 2 * kv_width].astype(bf16)
    kv_out[...] = jnp.concatenate(heads[q_width // head_size :] + [values], 1)


def run_proj(where, near, far, tokens_t, gain, head_gains, cosine, sine, sizes):
    f32, bf16 = jnp.float32, jnp.bfloat16
    q_width, kv_width, _ = sizes
    width, toks = tokens_t.shape
    return staged_call(
        functools.partial(proj_kernel, sizes),
        "proj",
        kept("smem", where)
        + kept("vmem", near, far)
        + kept("staged", tokens_t)
        + kept("vmem", gain, head_gains, cosine, sine),
        (
            shape((toks, width), bf16),
            shape((toks, q_width + kv_width), f32),
            shape((toks, q_width), bf16),
            shape((toks, 2 * kv_width), bf16),
            shape((width, 8 * LANES), bf16),
        ),
        (vmem(),) * 5,
        (),
        24,
    )


def attend_kernel(sizes, query, own_seg, key_seg, *refs):
    f32, bf16 = jnp.float32, jnp.bfloat16
    q_width, kv_width, head_size = sizes
    held = refs[: len(refs) - 6]
    attended, exact, probs_out, bias, probs, sems = refs[len(refs) - 6 :]
    toks = query.shape[0]
    same = own_seg[...] == key_seg[...]
    order = lax.broadcasted_iota(jnp.int32, same.shape, 0) - lax.broadcasted_iota(
        jnp.int32, same.shape, 1
    )
    later = lax.broadcasted_iota(jnp.int32, same.shape, 1) >= toks
    bias[...] = jnp.where(same & ((order >= 0) | later), 0.0, -1e30)
    outs = []
    per = q_width // kv_width
    for g in range(kv_width // head_size):
        cols = slice(g * head_size, (g + 1) * head_size)
        keys = jnp.concatenate([kv[:, cols] for kv in held], 0)
        cols = slice(kv_width + g * head_size, kv_width + (g + 1) * head_size)
        values = jnp.concatenate([kv[:, cols] for kv in held], 0)
        for head in range(g * per, (g + 1) * per):
            scores = dot(query[:, head * head_size : (head + 1) * head_size], keys, (1, 1))
            scores = scores + bias[...]
            powers = jnp.exp(scores)
            share = 1.0 / jnp.sum(powers, axis=1, keepdims=True)
            low = (powers * share).astype(bf16)
            probs[head] = low
            pltpu.make_async_copy(probs.at[head], probs_out.at[head], sems.at[head]).start()
            outs.append(dot(low, values))
    whole = jnp.concatenate(outs, 1)
    exact[...] = whole
    attended[...] = whole.astype(bf16)
    for head in range(probs.shape[0]):
        pltpu.make_async_copy(probs.at[head], probs_out.at[head], sems.at[head]).wait()


def run_attend(query, own_seg, key_seg, held, sizes):
    bf16 = jnp.bfloat16
    q_width, kv_width, head_size = sizes
    toks = query.shape[0]
    keys = toks * len(held)
    heads = q_width // head_size
    return staged_call(
        functools.partial(attend_kernel, sizes),
        "attend",
        kept("staged", query, own_seg, key_seg, *held),
        (
            shape((toks, q_width), bf16),
            shape((toks, q_width), jnp.float32),
            shape((heads, toks, keys), bf16),
        ),
        (vmem(), vmem(), hbm()),
        [
            pltpu.VMEM((toks, keys), jnp.float32),
            pltpu.VMEM((heads, toks, keys), bf16),
            pltpu.SemaphoreType.DMA((heads,)),
        ],
        BIG,
    )


def attend_back_kernel(sizes, query, grad, exact, *refs):
    f32, bf16 = jnp.float32, jnp.bfloat16
    q_width, kv_width, head_size = sizes
    probs, sems = refs[-2:]
    refs = refs[:-2]
    groups = (len(refs) - 2) // 2
    probs_in = refs[groups]
    refs = refs[:groups] + refs[groups + 1 :]
    copies = [
        pltpu.make_async_copy(probs_in.at[head], probs.at[head], sems.at[head])
        for head in range(probs.shape[0])
    ]
    for copy in copies[:PROBS_AHEAD]:
        copy.start()
    held = refs[:groups]
    query_grad = refs[groups]
    kv_grads = refs[groups + 1 :]
    toks = query.shape[0]
    per = q_width // kv_width
    query_t = query[...].astype(f32).T.astype(bf16)
    grad_t = grad[...].astype(f32).T.astype(bf16)
    outs, key_parts, value_parts = [], [], []
    for g in range(kv_width // head_size):
        cols = slice(g * head_size, (g + 1) * head_size)
        keys = jnp.concatenate([kv[:, cols] for kv in held], 0)
        cols = slice(kv_width + g * head_size, kv_width + (g + 1) * head_size)
        values = jnp.concatenate([kv[:, cols] for kv in held], 0)
        key_t = value_t = None
        for head in range(g * per, (g + 1) * per):
            cols = slice(head * head_size, (head + 1) * head_size)
            copies[head].wait()
            if head + PROBS_AHEAD < len(copies):
                copies[head + PROBS_AHEAD].start()
            low = probs[head]
            inner = jnp.sum(grad[:, cols].astype(f32) * exact[:, cols], axis=1, keepdims=True)
            scores = dot(grad[:, cols], values, (1, 1)) - inner
            scores = (low.astype(f32) * scores).astype(bf16)
            outs.append(dot(scores, keys))
            key_one = dot(query_t[cols, :], scores)
            value_one = dot(grad_t[cols, :], low)
            key_t = key_one if key_t is None else key_t + key_one
            value_t = value_one if value_t is None else value_t + value_one
        key_parts.append(key_t)
        value_parts.append(value_t)
    query_grad[...] = jnp.concatenate(outs, 1) * head_size ** (-0.5)
    both = jnp.concatenate(key_parts + value_parts, 0)
    for at, out in enumerate(kv_grads):
        out[...] = both[:, at * toks : (at + 1) * toks].T.astype(out.dtype)


def run_attend_back(query, grad, exact, probs, held, sizes):
    f32, bf16 = jnp.float32, jnp.bfloat16
    q_width, kv_width, head_size = sizes
    toks = query.shape[0]
    keys = toks * len(held)
    return staged_call(
        functools.partial(attend_back_kernel, sizes),
        "attend_back",
        kept("staged", query, grad, exact, *held) + kept("hbm", probs),
        (shape((toks, q_width), f32),) + tuple(shape((toks, 2 * kv_width), bf16) for _ in held),
        (vmem(),) * (1 + len(held)),
        [pltpu.VMEM(probs.shape, bf16), pltpu.SemaphoreType.DMA((probs.shape[0],))],
        36,
    )


def mlp_kernel(w_chunk, g_chunk, where, attended, tokens_t, out_grad_t, gain, *refs):
    f32, bf16 = jnp.float32, jnp.bfloat16
    pieces, refs = refs[:4], refs[4:]
    layer_out_t, mixed_grad, attended_grad, gain_grad, keep, send = refs[:6]
    weights, grads, sem_in, sem_out = refs[6:]
    width, toks = tokens_t.shape
    shard, groups, out_blocks = w_chunk.shard, w_chunk.groups, w_chunk.out_blocks

    def piece_place(number):
        core = number // 4
        first, second = (where[2], where[3]) if core == 0 else (where[3], where[2])
        return where[1] ^ core, first ^ (number // 2 % 2), second ^ (number % 2)

    def fetch(number):
        core, high, low = piece_place(number)
        for place in range(4):

            @pl.when(core * 2 + high == place)
            def _():
                pltpu.make_async_copy(
                    pieces[place].at[low],
                    weights.at[:, pl.ds(number * w_chunk.part, w_chunk.part)],
                    sem_in.at[number],
                ).start()

    fetched = waited = 0

    def fetch_to(count):
        nonlocal fetched
        while fetched < min(count, 8):
            fetch(fetched)
            fetched += 1

    def need(rows):
        nonlocal waited
        while waited < 8 and waited * w_chunk.part < rows:
            fetch_to(waited + AHEAD)
            here = weights.at[:, pl.ds(waited * w_chunk.part, w_chunk.part)]
            pltpu.make_async_copy(here, here, sem_in.at[waited]).wait()
            waited += 1

    left = 0

    def leave(rows):
        nonlocal left
        while left < 8 and (left + 1) * g_chunk.part <= rows:
            core, high, low = piece_place(left)
            for away, out in ((0, keep), (1, send)):

                @pl.when(core == away)
                def _(number=left, high=high, low=low, away=away, out=out):
                    pltpu.make_async_copy(
                        grads.at[:, pl.ds(number * g_chunk.part, g_chunk.part)],
                        out.at[high, low],
                        sem_out.at[away],
                    ).start()

            left += 1

    behind = [lax.rem(where[0] + groups - owner, groups) for owner in range(groups)]
    ahead_of = [lax.rem(owner + groups - where[0], groups) for owner in range(groups)]

    def column(kind, f):
        at = w_chunk.rows_at[kind, f]
        return jnp.concatenate([weights[place, at : at + shard, :] for place in behind], 0)

    def store(kind, f, block):
        at = g_chunk.rows_at[kind, f]
        for owner in range(groups):
            grads[ahead_of[owner], at : at + shard, :] = block[owner * shard : (owner + 1) * shard]

    fetch_to(AHEAD)
    out_t = out_grad_t[...]
    upstream = turned(out_t)
    inputs = tokens_t[...].astype(f32).T
    att_t = turned(attended[...])
    if g_chunk.used < g_chunk.rows:
        grads[:, g_chunk.used :, :] = jnp.zeros(
            (groups, g_chunk.rows - g_chunk.used, LANES), bf16
        )
    need(w_chunk.out_end)
    output_w = jnp.concatenate([column("out", j) for j in range(out_blocks)], 1)[:, :width]
    mixed = inputs + dot(attended[...], output_w)
    scale = lax.rsqrt(jnp.mean(mixed * mixed, axis=1, keepdims=True) + NORM_EPS)
    unit = mixed * scale
    gained = gain[...]
    normed = (unit * gained).astype(bf16)
    normed_t = turned(normed)
    back = jnp.zeros(mixed.shape, f32)
    ahead = mixed
    for share in range(w_chunk.own):
        need(w_chunk.share_end[share])
        blocks = w_chunk.blocks(share)
        down_at = w_chunk.rows_at["down", share]
        down_to = g_chunk.rows_at["down", share]
        for pair in range(0, len(blocks), 4):
            some = blocks[pair : pair + 4]
            gate_w = jnp.concatenate([column("gate", f) for f in some], 1)
            up_w = jnp.concatenate([column("up", f) for f in some], 1)
            down_w = jnp.concatenate(
                [weights[behind[f // w_chunk.own], down_at : down_at + width, :] for f in some], 1
            )
            gate = dot(normed, gate_w)
            up = dot(normed, up_w)
            hidden_grad = dot(upstream, down_w)
            sigmoid = 1.0 / (1.0 + jnp.exp(-gate))
            silu = gate * sigmoid
            hidden = (silu * up).astype(bf16)
            gate_low = (hidden_grad * up * (sigmoid * (1.0 + gate * (1.0 - sigmoid)))).astype(bf16)
            up_low = (hidden_grad * silu).astype(bf16)
            ahead = ahead + dot(hidden, down_w, (1, 1))
            back = back + dot(gate_low, gate_w, (1, 1)) + dot(up_low, up_w, (1, 1))
            gate_wg = dot(normed_t, gate_low).astype(bf16)
            up_wg = dot(normed_t, up_low).astype(bf16)
            down_wg = dot(out_t, hidden).astype(bf16)
            for at, f in enumerate(some):
                cols = slice(at * LANES, (at + 1) * LANES)
                store("gate", f, gate_wg[:, cols])
                store("up", f, up_wg[:, cols])
                grads[ahead_of[f // g_chunk.own], down_to : down_to + width, :] = down_wg[:, cols]
        leave(g_chunk.share_end[share])
    layer_out_t[...] = ahead.T.astype(bf16)
    gain_grad[...] = jnp.sum(back * unit, axis=0, keepdims=True)
    inner = back * gained
    through = scale * (inner - unit * jnp.mean(inner * unit, axis=1, keepdims=True))
    mixed_back = upstream.astype(f32) + through
    mixed_grad[...] = mixed_back
    branch = mixed_back.astype(bf16)
    attended_grad[...] = dot(branch, output_w, (1, 1)).astype(bf16)
    output_wg = dot(att_t, branch)
    for j in range(out_blocks):
        block = output_wg[:, j * LANES : min((j + 1) * LANES, width)]
        if block.shape[1] < LANES:
            block = jnp.concatenate(
                [block, jnp.zeros((block.shape[0], LANES - block.shape[1]), f32)], 1
            )
        store("out", j, block.astype(bf16))
    leave(g_chunk.rows)
    pltpu.make_async_copy(keep, keep, sem_out.at[0]).wait()
    pltpu.make_async_copy(send, send, sem_out.at[1]).wait()


def run_mlp(where, w_chunk, g_chunk, pieces, attended, tokens_t, out_grad_t, gain):
    f32, bf16 = jnp.float32, jnp.bfloat16
    groups = w_chunk.groups
    width, toks = tokens_t.shape
    packed = shape((2, 2, groups, g_chunk.part, LANES), bf16)
    return staged_call(
        functools.partial(mlp_kernel, w_chunk, g_chunk),
        "mlp",
        kept("smem", where) + kept("staged", attended, tokens_t, out_grad_t, gain) + kept("hbm", *pieces),
        (
            shape((width, toks), bf16),
            shape((toks, width), f32),
            shape((toks, width), bf16),
            shape((1, width), f32),
            packed,
            packed,
        ),
        (vmem(),) * 4 + (hbm(),) * 2,
        [pltpu.VMEM((groups, chunk.rows, LANES), bf16) for chunk in (w_chunk, g_chunk)]
        + [pltpu.SemaphoreType.DMA((8,)), pltpu.SemaphoreType.DMA((2,))],
        BIG,
    )


def heads_back(grad, raw, cos, sin, gain, head_size):
    half = head_size // 2
    lows, total = [], jnp.zeros((1, head_size), jnp.float32)
    for at, (unit, factor) in enumerate(unit_heads(raw, head_size)):
        at *= head_size
        one, two = grad[:, at : at + half], grad[:, at + half : at + head_size]
        back = jnp.concatenate([one * cos + two * sin, two * cos - one * sin], 1)
        total = total + jnp.sum(back * unit, axis=0, keepdims=True)
        inner = back * gain
        lows.append(factor * (inner - unit * jnp.mean(inner * unit, axis=1, keepdims=True)))
    return lows, total


def query_back_kernel(sizes, query_grad, raw, normed, head_gains, cosine, sine, weights, products, back, total):
    q_width, _, head_size = sizes
    lows, total[...] = heads_back(
        query_grad[...], raw[:, :q_width], cosine[...], sine[...], head_gains[0:1, :], head_size
    )
    low = jnp.concatenate(lows, 1).astype(products.dtype)
    back[...] = dot(low, weights[:, :q_width], (1, 1))
    products[...] = dot(turned(normed[...]), low).astype(products.dtype)


def run_query_back(query_grad, raw, normed, head_gains, cosine, sine, weights, sizes):
    f32 = jnp.float32
    q_width, _, head_size = sizes
    toks, width = normed.shape
    return staged_call(
        functools.partial(query_back_kernel, sizes),
        "query_back",
        kept("vmem", query_grad, raw, normed, head_gains, cosine, sine, weights),
        (shape((width, q_width), normed.dtype), shape((toks, width), f32), shape((1, head_size), f32)),
        (vmem(),) * 3,
        (),
        24,
    )


def last_kernel(sizes, where, products, back, q_total, raw, normed, tokens_t, mixed_grad, gain, head_gains, cosine, sine, weights, second, *refs):
    f32, bf16 = jnp.float32, jnp.bfloat16
    q_width, kv_width, head_size = sizes
    kv_parts = refs[: len(refs) - 4]
    token_grad_t, keep, send, grads = refs[len(refs) - 4 :]
    count, groups, rows, _ = grads.shape
    width, toks = tokens_t.shape
    shard = width // groups
    kv_grad = kv_parts[0][...].astype(f32)
    for part in kv_parts[1:]:
        kv_grad = kv_grad + part[...].astype(f32)
    lows, k_total = heads_back(
        kv_grad, raw[:, q_width:], cosine[...], sine[...], head_gains[1:2, :], head_size
    )
    low = jnp.concatenate(lows + [kv_grad[:, kv_width:]], 1).astype(bf16)
    short = count * LANES - q_width - 2 * kv_width
    pieces = [products[...], dot(turned(normed[...]), low).astype(bf16)]
    if short:
        pieces.append(jnp.zeros((width, short), bf16))
    blocks = jnp.concatenate(pieces, 1)
    for j in range(count):
        for owner in range(groups):
            grads[j, owner, :shard, :] = blocks[
                owner * shard : (owner + 1) * shard, j * LANES : (j + 1) * LANES
            ]
            grads[j, owner, shard:, :] = jnp.zeros((rows - shard, LANES), bf16)
    whole = back[...] + dot(low, weights[:, q_width : q_width + 2 * kv_width], (1, 1))
    inputs = tokens_t[...].astype(f32).T
    scale = lax.rsqrt(jnp.mean(inputs * inputs, axis=1, keepdims=True) + NORM_EPS)
    unit = inputs * scale
    first = jnp.sum(whole * unit, axis=0, keepdims=True)
    inner = whole * gain[...]
    whole = mixed_grad[...] + scale * (inner - unit * jnp.mean(inner * unit, axis=1, keepdims=True))
    token_grad_t[...] = whole.T

    def line(vector):
        short = LANES - vector.shape[1]
        return jnp.concatenate([vector, jnp.zeros((1, short), f32)], 1) if short else vector

    head_part = head_size // groups
    for owner in range(groups):
        lines = []
        for vector in (first, second[...]):
            mine = vector[:, owner * shard : (owner + 1) * shard]
            lines += [line(mine[:, at : at + LANES]) for at in range(0, shard, LANES)]
        for vector in (q_total[...], k_total):
            lines.append(line(vector[:, owner * head_part : (owner + 1) * head_part]))
        lines.append(jnp.zeros((rows - shard - len(lines), LANES), f32))
        grads[0, owner, shard:, :] = jnp.concatenate(lines, 0).astype(bf16)
    for core in range(2):
        for across in range(2):
            for along in range(2):
                block = block_at(where, core, across, along)
                for step in range(groups):
                    owner = lax.rem(where[0] + step, groups)
                    (send if core else keep)[across * 2 + along, step] = grads[block, owner]


def run_last(where, products, back, q_total, raw, normed, tokens_t, mixed_grad, gain, head_gains, cosine, sine, weights, second, kv_parts, sizes):
    width = tokens_t.shape[0]
    groups = lax.axis_size("grp")
    rows = width // groups + SMALL
    packed = shape((4, groups, rows, LANES), jnp.bfloat16)
    return staged_call(
        functools.partial(last_kernel, sizes),
        "last",
        kept("smem", where)
        + kept("vmem", products, back, q_total, raw, normed)
        + kept("staged", tokens_t)
        + kept("vmem", mixed_grad, gain, head_gains, cosine, sine, weights, second, *kv_parts),
        (shape(tokens_t.shape, jnp.float32), packed, packed),
        (vmem(),) * 3,
        [pltpu.VMEM((8, groups, rows, LANES), jnp.bfloat16)],
        24,
    )


def unpack_kernel(sizes, chunk, where, near, far, *refs):
    f32 = jnp.float32
    q_width, kv_width, _ = sizes
    gate, up, down_t, output, query, key, value = refs[:7]
    lines_out = refs[7:11]
    pack = refs[11]
    shard, width = chunk.shard, chunk.width
    projections = []
    small = None
    for core in range(2):
        for across in range(2):
            for along in range(2):
                place = (where[2] ^ across) * 2 + (where[3] ^ along)
                piece = jnp.where(where[1] == core, near[place], far[place])
                at = chunk.part
                high, low = (across, along) if core == 0 else (along, across)
                row = (core * 4 + high * 2 + low) * chunk.part
                pack[row : row + chunk.part, :] = piece[:at]
                projections.append(piece[at : at + shard])
                if small is None:
                    small = piece[at + shard :].astype(f32)
    for (kind, j), at in chunk.rows_at.items():
        if kind == "down":
            down_t[:, j * LANES : (j + 1) * LANES] = pack[at : at + width].astype(f32)
            continue
        out = {"gate": gate, "up": up, "out": output}[kind]
        stop = min((j + 1) * LANES, out.shape[1])
        out[:, j * LANES : stop] = pack[at : at + shard].astype(f32)[:, : stop - j * LANES]
    whole = jnp.concatenate(projections, 1).astype(f32)
    query[...] = whole[:, :q_width]
    key[...] = whole[:, q_width : q_width + kv_width]
    value[...] = whole[:, q_width + kv_width : q_width + 2 * kv_width]
    row = 0
    for out in lines_out:
        for at in range(0, out.shape[1], LANES):
            stop = min(at + LANES, out.shape[1])
            out[:, at:stop] = small[row : row + 1, : stop - at]
            row += 1


def run_unpack(where, chunk, sizes, near, far, hidden_width, own_hidden, head_part):
    f32 = jnp.float32
    q_width, kv_width, _ = sizes
    shard, width = chunk.shard, chunk.width
    return staged_call(
        functools.partial(unpack_kernel, sizes, chunk),
        "unpack",
        kept("smem", where) + kept("vmem", near, far),
        (
            shape((shard, hidden_width), f32),
            shape((shard, hidden_width), f32),
            shape((width, own_hidden), f32),
            shape((shard, width), f32),
            shape((shard, q_width), f32),
            shape((shard, kv_width), f32),
            shape((shard, kv_width), f32),
            shape((1, shard), f32),
            shape((1, shard), f32),
            shape((1, head_part), f32),
            shape((1, head_part), f32),
        ),
        (vmem(),) * 11,
        [pltpu.VMEM((chunk.rows, LANES), near.dtype)],
        24,
    )


def body(
    tokens,
    segments,
    out_grad,
    norm_gain,
    query_gain,
    key_gain,
    query_weight,
    key_weight,
    value_weight,
    output_weight,
    second_gain,
    gate_weight,
    up_weight,
    down_weight,
):
    f32, bf16 = jnp.float32, jnp.bfloat16
    groups = lax.axis_size("grp")
    place_z = lax.axis_index("grp")
    where = place_scalars()
    toks, width = tokens.shape
    shard = norm_gain.shape[0]
    head_part = query_gain.shape[0]
    head_size = head_part * groups
    hidden_width, own_hidden = gate_weight.shape[1], down_weight.shape[0]
    sizes = (query_weight.shape[1], key_weight.shape[1], head_size)
    w_chunk, g_chunk = chunks_of(shard, width, own_hidden, groups)
    tokens_t, out_grad_t = tokens.T, out_grad.T

    fence = lax.optimization_barrier
    own_first, own_second = run_pack(
        where, w_chunk, query_weight, key_weight, value_weight,
        gate_weight, up_weight, down_weight.T, output_weight,
    )
    first_z = [own_first] + [shift(own_first, step) for step in range(1, groups)]
    second_z = [own_second] + [shift(own_second, step) for step in range(1, groups)]

    gain_rows = -(-shard // LANES)
    seg_rows = -(-toks // LANES)
    _, segs = fence((own_first, segments))
    small = jnp.zeros((SMALL * LANES,), bf16)
    at = 0
    for line, count in (
        (norm_gain, gain_rows),
        (second_gain, gain_rows),
        (query_gain, 1),
        (key_gain, 1),
        (segs.astype(bf16), seg_rows),
    ):
        small = small + jnp.pad(line, (at, SMALL * LANES - at - line.shape[0]))
        at += count * LANES
    small = small.reshape(SMALL, LANES)
    small_behind = jnp.stack([small] + [shift(small, step) for step in range(1, groups)])

    small_behind = small_behind.astype(f32)
    small_all = small_behind[lax.rem(place_z + groups - jnp.arange(groups), groups)]
    at = 0
    gains = []
    for count, length in ((gain_rows, shard), (gain_rows, shard), (1, head_part), (1, head_part)):
        gains.append(lined(small_all[:, at : at + count], length))
        at += count
    gain_first, gain_second, gain_query, gain_key = gains
    head_gains = jnp.concatenate([gain_query, gain_key])
    segs = small_behind[:, at : at + seg_rows].reshape(groups, -1)[:, :toks]
    there = (place_z >= jnp.arange(groups))[:, None]
    key_seg = jnp.where(there, segs, -1.0).reshape(1, -1)
    own_seg = segs[0][:, None]
    earlier = ((key_seg < own_seg) & (key_seg >= 0.0)).astype(jnp.int32)
    positions = place_z * toks + jnp.arange(toks, dtype=jnp.int32) - jnp.sum(earlier, axis=1)
    half = head_size // 2
    inverse = ROPE_BASE ** (-(jnp.arange(half, dtype=f32) * 2.0 / head_size))
    angles = positions.astype(f32)[:, None] * inverse[None, :]
    cosine, sine = jnp.cos(angles), jnp.sin(angles)

    near = spread_chip(jnp.stack(first_z))
    near, second_z = fence((near, second_z))
    whole = jnp.stack(second_z)
    near, gain_first, gain_second, head_gains, cosine, sine, own_seg, key_seg = fence(
        (near, gain_first, gain_second, head_gains, cosine, sine, own_seg, key_seg)
    )
    normed, raw, query, key_value, proj_weights = run_proj(
        where, near, hop(near, 1), tokens_t, gain_first, head_gains, cosine, sine, sizes
    )
    held = [key_value]
    for step in range(1, groups):
        ahead = [(i, i + step) for i in range(groups - step)]
        held.append(lax.ppermute(key_value, "grp", ahead))
    whole = jnp.stack([whole, hop_split(whole, 4, 2)])
    far_whole = hop_split(whole, 2, 4)
    whole, held = fence((whole, held))
    other = hop(whole, 1)
    attended, exact, probs = run_attend(query, own_seg, key_seg, held, sizes)
    far_whole, attended, other = fence((far_whole, attended, other))
    pieces = [whole, far_whole, other, hop(far_whole, 1)]
    layer_out_t, mixed_grad, attended_grad, second_sum, keep, send = run_mlp(
        where, w_chunk, g_chunk, pieces, attended, tokens_t, out_grad_t, gain_second
    )
    got = hop(send, 1)
    query_grad, *kv_parts = run_attend_back(query, attended_grad, exact, probs, held, sizes)
    got, query_grad, kv_parts = fence((got, query_grad, kv_parts))
    kv_back = [kv_parts[0]]
    for step in range(1, groups):
        back = [(i + step, i) for i in range(groups - step)]
        kv_back.append(lax.ppermute(kv_parts[step], "grp", back))
    near_got = hop_split(add_low(keep[1], got[1]), 2, 4)
    query_parts = run_query_back(
        query_grad, raw, normed, head_gains, cosine, sine, proj_weights, sizes
    )
    near_got, kv_back, query_parts = fence((near_got, kv_back, query_parts))
    far_got = hop_split(add_low(keep[0, 1], got[0, 1], near_got[1]), 4, 2)
    token_grad_t, late_keep, late_send = run_last(
        where, *query_parts, raw, normed, tokens_t, mixed_grad, gain_first, head_gains, cosine, sine,
        proj_weights, second_sum, kv_back, sizes,
    )
    late_got = hop(late_send, 1)
    far_got, late_got = fence((far_got, late_got))
    early = fold_grp(
        [add_low(keep[0, 0, d], got[0, 0, d], near_got[0, d], far_got[d]) for d in range(groups)]
    )
    late = fold_blocks(late_keep, late_got)
    near = spread_chip(jnp.concatenate([early, fold_grp(late)]))
    far = hop(near, 1)
    (
        gate_sum, up_sum, down_sum_t, output_sum, query_sum, key_sum, value_sum,
        first_sum, second_sum, query_gsum, key_gsum,
    ) = run_unpack(where, g_chunk, sizes, near, far, hidden_width, own_hidden, head_part)
    return (
        layer_out_t.T,
        token_grad_t.T,
        first_sum.reshape(-1),
        query_gsum.reshape(-1),
        key_gsum.reshape(-1),
        query_sum,
        key_sum,
        value_sum,
        output_sum,
        second_sum.reshape(-1),
        gate_sum,
        up_sum,
        down_sum_t.T,
    )


def solution(mesh):
    placed = (
        P(("rep", "grp"), None),
        P(("rep", "grp")),
        P(("rep", "grp"), None),
        P("grp"),
        P("grp"),
        P("grp"),
        P("grp", None),
        P("grp", None),
        P("grp", None),
        P("grp", None),
        P("grp"),
        P("grp", None),
        P("grp", None),
        P("grp", None),
    )
    return jax.shard_map(
        body,
        mesh=mesh,
        in_specs=placed,
        out_specs=(
            P(("rep", "grp"), None),
            P(("rep", "grp"), None),
            P("grp"),
            P("grp"),
            P("grp"),
            P("grp", None),
            P("grp", None),
            P("grp", None),
            P("grp", None),
            P("grp"),
            P("grp", None),
            P("grp", None),
            P("grp", None),
        ),
        check_vma=False,
    )
```

```python
import functools

import jax
import jax.numpy as jnp
from jax import lax
from jax.experimental import pallas as pl
from jax.experimental.pallas import tpu as pltpu
from jax.sharding import PartitionSpec as P

NORM_EPS = 1e-05
ROPE_BASE = 100000.0
LANES = 128
SMALL = 16
MIB = 1024 * 1024
AHEAD = 4
BIG = 58


def vmem():
    return pl.BlockSpec(memory_space=pltpu.VMEM)


def smem():
    return pl.BlockSpec(memory_space=pltpu.SMEM)


def hbm():
    return pl.BlockSpec(memory_space=pl.ANY)


def shape(dims, kind):
    return jax.ShapeDtypeStruct(dims, kind)


def options(mebibytes):
    return pltpu.CompilerParams(vmem_limit_bytes=mebibytes * MIB)


def cost():
    return pl.CostEstimate(flops=1, bytes_accessed=1024, transcendentals=0)


class Staged:
    def __init__(self, source, target, sem):
        self.copy = pltpu.make_async_copy(source, target, sem)
        self.copy.start()
        self.target, self.waiting = target, True
        self.shape, self.dtype = target.shape, target.dtype

    def wait(self):
        if self.waiting:
            self.copy.wait()
            self.waiting = False

    def __getitem__(self, index):
        self.wait()
        return self.target[index]


def staged_call(kernel, name, operands, out_shape, out_specs, scratch, mebibytes):
    kinds = [kind for kind, _ in operands]
    staged = [array for kind, array in operands if kind == "staged"]
    count = len(operands)

    def whole(*refs):
        sources, refs = refs[:count], refs[count:]
        if staged:
            targets, sems = refs[len(refs) - len(staged) - 1 : -1], refs[-1]
            refs = refs[: len(refs) - len(staged) - 1]
        given, at = [], 0
        for kind, source in zip(kinds, sources):
            if kind == "staged":
                source = Staged(source, targets[at], sems.at[at])
                at += 1
            given.append(source)
        kernel(*given, *refs)
        for operand in given:
            if isinstance(operand, Staged):
                operand.wait()

    specs = {"smem": smem, "vmem": vmem, "hbm": hbm, "staged": hbm}
    more = [pltpu.VMEM(array.shape, array.dtype) for array in staged]
    if staged:
        more.append(pltpu.SemaphoreType.DMA((len(staged),)))
    return pl.pallas_call(
        whole,
        out_shape=out_shape,
        in_specs=[specs[kind]() for kind in kinds],
        out_specs=out_specs,
        scratch_shapes=list(scratch) + more,
        compiler_params=options(mebibytes),
        cost_estimate=cost(),
        name=name,
    )(*[array for _, array in operands])


def kept(kind, *arrays):
    return [(kind, array) for array in arrays]


def hop(value, bit):
    count = lax.axis_size("rep")
    return lax.ppermute(value, "rep", [(i, i ^ bit) for i in range(count)])


def shift(value, step):
    count = lax.axis_size("grp")
    return lax.ppermute(value, "grp", [(i, (i + step) % count) for i in range(count)])


def rep_bits():
    index = lax.axis_index("rep")
    return index & 1, (index >> 1) & 1, (index >> 2) & 1


def hop_split(value, even, odd):
    count = lax.axis_size("rep")
    return lax.ppermute(value, "rep", [(i, i ^ (odd if i % 2 else even)) for i in range(count)])


def add_low(*values):
    total = values[0].astype(jnp.float32)
    for value in values[1:]:
        total = total + value.astype(jnp.float32)
    return total.astype(values[0].dtype)


def fold_grp(parts):
    f32 = jnp.float32
    total = parts[0].astype(f32)
    for step in range(1, len(parts)):
        total = total + shift(parts[step], step).astype(f32)
    total = total.astype(parts[0].dtype)
    bit = 8
    while bit < lax.axis_size("rep"):
        total = add_low(total, hop(total, bit))
        bit *= 2
    return total


def fold_blocks(keep, got):
    f32 = jnp.float32
    sums = [add_low(keep[j], got[j]) for j in range(4)]
    across, along, both = hop(sums[2], 2), hop(sums[1], 4), hop(sums[3], 6)
    return [
        (
            sums[0][d].astype(f32)
            + across[d].astype(f32)
            + along[d].astype(f32)
            + both[d].astype(f32)
        ).astype(keep.dtype)
        for d in range(lax.axis_size("grp"))
    ]


def spread_chip(own):
    return jnp.stack([own, hop(own, 4), hop(own, 2), hop(own, 6)])


def rows_of(vector, count):
    short = count * LANES - vector.shape[0]
    return jnp.pad(vector, (0, short)).reshape(count, LANES)


def lined(rows, length):
    return rows.reshape(rows.shape[0], -1)[:, :length].reshape(1, -1)


def place_scalars():
    bit_c, bit_x, bit_y = rep_bits()
    return jnp.stack([lax.axis_index("grp"), bit_c, bit_x, bit_y]).astype(jnp.int32)


def piece_row(where, core, high, low, rows):
    owner = where[1] ^ core
    first = jnp.where(owner == 0, where[2], where[3])
    second = jnp.where(owner == 0, where[3], where[2])
    index = owner * 4 + (first ^ high) * 2 + (second ^ low)
    return pl.multiple_of(index * (rows // 8), 16)


def piece_list():
    return [(c, h, l) for c in range(2) for h in range(2) for l in range(2)]


def dot(one, two, contract=(1, 0)):
    return lax.dot_general(
        one, two, (((contract[0],), (contract[1],)), ((), ())), preferred_element_type=jnp.float32
    )


def turned(value):
    return value.astype(jnp.float32).T.astype(value.dtype)


class Chunk:
    def __init__(self, dims, out_first):
        self.shard, self.width, self.own, self.groups = dims
        self.out_blocks = -(-self.width // LANES)
        self.rows_at, self.share_end, at = {}, [], 0

        def out_rows(at):
            for j in range(self.out_blocks):
                self.rows_at["out", j] = at
                at += self.shard
            return at

        if out_first:
            at = out_rows(at)
        self.out_end = at
        for share in range(self.own):
            for kind in ("gate", "up"):
                for f in self.blocks(share):
                    self.rows_at[kind, f] = at
                    at += self.shard
            self.rows_at["down", share] = at
            at += self.width
            self.share_end.append(at)
        if not out_first:
            at = out_rows(at)
        self.used = at
        self.rows = -(-at // 128) * 128
        self.part = self.rows // 8

    def blocks(self, share):
        return [owner * self.own + share for owner in range(self.groups)]


def chunks_of(shard, width, own_hidden, groups):
    dims = (shard, width, own_hidden // LANES, groups)
    return Chunk(dims, True), Chunk(dims, False)


def pack_kernel(chunk, where, query, key, value, gate, up, down_t, output, first, second, blocks, pack):
    shard, width = chunk.shard, chunk.width
    whole = jnp.concatenate([query[...], key[...], value[...]], 1)
    for j in range(blocks.shape[0]):
        stop = min((j + 1) * LANES, whole.shape[1])
        blocks[j, :, : stop - j * LANES] = whole[:, j * LANES : stop]
        if stop < (j + 1) * LANES:
            blocks[j, :, stop - j * LANES :] = jnp.zeros(
                (shard, (j + 1) * LANES - stop), whole.dtype
            )
    first[...] = blocks[where[1] * 4 + where[2] * 2 + where[3]]
    for (kind, j), at in chunk.rows_at.items():
        if kind == "down":
            pack[at : at + width, :] = down_t[:, j * LANES : (j + 1) * LANES]
            continue
        source = {"gate": gate, "up": up, "out": output}[kind]
        stop = min((j + 1) * LANES, source.shape[1])
        pack[at : at + shard, : stop - j * LANES] = source[:, j * LANES : stop]
        if stop < (j + 1) * LANES:
            pack[at : at + shard, stop - j * LANES :] = jnp.zeros(
                (shard, (j + 1) * LANES - stop), pack.dtype
            )
    if chunk.used < chunk.rows:
        pack[chunk.used :, :] = jnp.zeros((chunk.rows - chunk.used, LANES), pack.dtype)
    row = piece_row(where, 0, 0, 0, chunk.rows)
    second[...] = pack[pl.ds(row, chunk.part), :]


def run_pack(where, chunk, query, key, value, gate, up, down_t, output):
    kind = gate.dtype
    return staged_call(
        functools.partial(pack_kernel, chunk),
        "pack",
        kept("smem", where) + kept("staged", query, key, value, gate, up, down_t, output),
        (shape((chunk.shard, LANES), kind), shape((chunk.part, LANES), kind)),
        (vmem(), vmem()),
        [pltpu.VMEM((8, chunk.shard, LANES), kind), pltpu.VMEM((chunk.rows, LANES), kind)],
        BIG,
    )


def block_at(where, core, across, along):
    return (where[1] ^ core) * 4 + (where[2] ^ across) * 2 + (where[3] ^ along)


def unit_heads(raw, head_size):
    pairs = []
    for at in range(0, raw.shape[1], head_size):
        head = raw[:, at : at + head_size]
        factor = lax.rsqrt(jnp.mean(head * head, axis=1, keepdims=True) + NORM_EPS)
        pairs.append((head * factor, factor))
    return pairs


def proj_kernel(sizes, where, near, far, tokens_t, gain, head_gains, cosine, sine, *refs):
    f32, bf16 = jnp.float32, jnp.bfloat16
    q_width, kv_width, head_size = sizes
    normed_out, raw_out, query_out, kv_out, weights_out = refs
    groups = near.shape[1]
    inputs = tokens_t[...].astype(f32).T
    scale = lax.rsqrt(jnp.mean(inputs * inputs, axis=1, keepdims=True) + NORM_EPS)
    normed = (inputs * scale * gain[...]).astype(bf16)
    normed_out[...] = normed
    for j in range(8):
        core, across, along = j // 4, j // 2 % 2, j % 2
        place = (where[2] ^ across) * 2 + (where[3] ^ along)
        pieces = []
        for owner in range(groups):
            behind = lax.rem(where[0] + groups - owner, groups)
            pieces.append(
                jnp.where(where[1] == core, near[place, behind], far[place, behind])
            )
        weights_out[:, j * LANES : (j + 1) * LANES] = jnp.concatenate(pieces, 0)
    flat = weights_out[...]
    raw = dot(normed, flat)
    raw_out[...] = raw[:, : q_width + kv_width]
    half = head_size // 2
    cos, sin = cosine[...], sine[...]

    def turn(head):
        one, two = head[:, :half], head[:, half:]
        return jnp.concatenate([one * cos - two * sin, two * cos + one * sin], 1)

    heads = []
    for at, (unit, _) in enumerate(unit_heads(raw[:, : q_width + kv_width], head_size)):
        row = 0 if at * head_size < q_width else 1
        heads.append(turn(unit * head_gains[row : row + 1, :]).astype(bf16))
    queries = jnp.concatenate(heads[: q_width // head_size], 1)
    query_out[...] = (queries.astype(f32) * head_size ** (-0.5)).astype(bf16)
    values = raw[:, q_width + kv_width : q_width + 2 * kv_width].astype(bf16)
    kv_out[...] = jnp.concatenate(heads[q_width // head_size :] + [values], 1)


def run_proj(where, near, far, tokens_t, gain, head_gains, cosine, sine, sizes):
    f32, bf16 = jnp.float32, jnp.bfloat16
    q_width, kv_width, _ = sizes
    width, toks = tokens_t.shape
    return staged_call(
        functools.partial(proj_kernel, sizes),
        "proj",
        kept("smem", where)
        + kept("vmem", near, far)
        + kept("staged", tokens_t)
        + kept("vmem", gain, head_gains, cosine, sine),
        (
            shape((toks, width), bf16),
            shape((toks, q_width + kv_width), f32),
            shape((toks, q_width), bf16),
            shape((toks, 2 * kv_width), bf16),
            shape((width, 8 * LANES), bf16),
        ),
        (vmem(),) * 5,
        (),
        24,
    )


def attend_kernel(sizes, query, own_seg, key_seg, *refs):
    f32, bf16 = jnp.float32, jnp.bfloat16
    q_width, kv_width, head_size = sizes
    held = refs[: len(refs) - 6]
    attended, exact, probs_out, bias, probs, sems = refs[len(refs) - 6 :]
    toks = query.shape[0]
    same = own_seg[...] == key_seg[...]
    order = lax.broadcasted_iota(jnp.int32, same.shape, 0) - lax.broadcasted_iota(
        jnp.int32, same.shape, 1
    )
    later = lax.broadcasted_iota(jnp.int32, same.shape, 1) >= toks
    bias[...] = jnp.where(same & ((order >= 0) | later), 0.0, -1e30)
    outs = []
    per = q_width // kv_width
    for g in range(kv_width // head_size):
        cols = slice(g * head_size, (g + 1) * head_size)
        keys = jnp.concatenate([kv[:, cols] for kv in held], 0)
        cols = slice(kv_width + g * head_size, kv_width + (g + 1) * head_size)
        values = jnp.concatenate([kv[:, cols] for kv in held], 0)
        for head in range(g * per, (g + 1) * per):
            scores = dot(query[:, head * head_size : (head + 1) * head_size], keys, (1, 1))
            scores = scores + bias[...]
            powers = jnp.exp(scores)
            share = 1.0 / jnp.sum(powers, axis=1, keepdims=True)
            low = (powers * share).astype(bf16)
            probs[head] = low
            pltpu.make_async_copy(probs.at[head], probs_out.at[head], sems.at[head]).start()
            outs.append(dot(low, values))
    whole = jnp.concatenate(outs, 1)
    exact[...] = whole
    attended[...] = whole.astype(bf16)
    for head in range(probs.shape[0]):
        pltpu.make_async_copy(probs.at[head], probs_out.at[head], sems.at[head]).wait()


def run_attend(query, own_seg, key_seg, held, sizes):
    bf16 = jnp.bfloat16
    q_width, kv_width, head_size = sizes
    toks = query.shape[0]
    keys = toks * len(held)
    heads = q_width // head_size
    return staged_call(
        functools.partial(attend_kernel, sizes),
        "attend",
        kept("staged", query, own_seg, key_seg, *held),
        (
            shape((toks, q_width), bf16),
            shape((toks, q_width), jnp.float32),
            shape((heads, toks, keys), bf16),
        ),
        (vmem(), vmem(), hbm()),
        [
            pltpu.VMEM((toks, keys), jnp.float32),
            pltpu.VMEM((heads, toks, keys), bf16),
            pltpu.SemaphoreType.DMA((heads,)),
        ],
        BIG,
    )


def attend_back_kernel(sizes, query, grad, exact, *refs):
    f32, bf16 = jnp.float32, jnp.bfloat16
    q_width, kv_width, head_size = sizes
    groups = (len(refs) - 2) // 2
    probs = refs[groups]
    refs = refs[:groups] + refs[groups + 1 :]
    held = refs[:groups]
    query_grad = refs[groups]
    kv_grads = refs[groups + 1 :]
    toks = query.shape[0]
    per = q_width // kv_width
    query_t = query[...].astype(f32).T.astype(bf16)
    grad_t = grad[...].astype(f32).T.astype(bf16)
    outs, key_parts, value_parts = [], [], []
    for g in range(kv_width // head_size):
        cols = slice(g * head_size, (g + 1) * head_size)
        keys = jnp.concatenate([kv[:, cols] for kv in held], 0)
        cols = slice(kv_width + g * head_size, kv_width + (g + 1) * head_size)
        values = jnp.concatenate([kv[:, cols] for kv in held], 0)
        key_t = value_t = None
        for head in range(g * per, (g + 1) * per):
            cols = slice(head * head_size, (head + 1) * head_size)
            low = probs[head]
            inner = jnp.sum(grad[:, cols].astype(f32) * exact[:, cols], axis=1, keepdims=True)
            scores = dot(grad[:, cols], values, (1, 1)) - inner
            scores = (low.astype(f32) * scores).astype(bf16)
            outs.append(dot(scores, keys))
            key_one = dot(query_t[cols, :], scores)
            value_one = dot(grad_t[cols, :], low)
            key_t = key_one if key_t is None else key_t + key_one
            value_t = value_one if value_t is None else value_t + value_one
        key_parts.append(key_t)
        value_parts.append(value_t)
    query_grad[...] = jnp.concatenate(outs, 1) * head_size ** (-0.5)
    both = jnp.concatenate(key_parts + value_parts, 0)
    for at, out in enumerate(kv_grads):
        out[...] = both[:, at * toks : (at + 1) * toks].T.astype(out.dtype)


def run_attend_back(query, grad, exact, probs, held, sizes):
    f32, bf16 = jnp.float32, jnp.bfloat16
    q_width, kv_width, head_size = sizes
    toks = query.shape[0]
    keys = toks * len(held)
    return staged_call(
        functools.partial(attend_back_kernel, sizes),
        "attend_back",
        kept("staged", query, grad, exact, *held) + kept("vmem", probs),
        (shape((toks, q_width), f32),) + tuple(shape((toks, 2 * kv_width), bf16) for _ in held),
        (vmem(),) * (1 + len(held)),
        (),
        36,
    )


def mlp_kernel(w_chunk, g_chunk, where, attended, tokens_t, out_grad_t, gain, *refs):
    f32, bf16 = jnp.float32, jnp.bfloat16
    pieces, refs = refs[:4], refs[4:]
    layer_out_t, mixed_grad, attended_grad, gain_grad, keep, send = refs[:6]
    weights, grads, sem_in, sem_out = refs[6:]
    width, toks = tokens_t.shape
    shard, groups, out_blocks = w_chunk.shard, w_chunk.groups, w_chunk.out_blocks

    def piece_place(number):
        core = number // 4
        first, second = (where[2], where[3]) if core == 0 else (where[3], where[2])
        return where[1] ^ core, first ^ (number // 2 % 2), second ^ (number % 2)

    def fetch(number):
        core, high, low = piece_place(number)
        for place in range(4):

            @pl.when(core * 2 + high == place)
            def _():
                pltpu.make_async_copy(
                    pieces[place].at[low],
                    weights.at[:, pl.ds(number * w_chunk.part, w_chunk.part)],
                    sem_in.at[number],
                ).start()

    fetched = waited = 0

    def fetch_to(count):
        nonlocal fetched
        while fetched < min(count, 8):
            fetch(fetched)
            fetched += 1

    def need(rows):
        nonlocal waited
        while waited < 8 and waited * w_chunk.part < rows:
            fetch_to(waited + AHEAD)
            here = weights.at[:, pl.ds(waited * w_chunk.part, w_chunk.part)]
            pltpu.make_async_copy(here, here, sem_in.at[waited]).wait()
            waited += 1

    left = 0

    def leave(rows):
        nonlocal left
        while left < 8 and (left + 1) * g_chunk.part <= rows:
            core, high, low = piece_place(left)
            for away, out in ((0, keep), (1, send)):

                @pl.when(core == away)
                def _(number=left, high=high, low=low, away=away, out=out):
                    pltpu.make_async_copy(
                        grads.at[:, pl.ds(number * g_chunk.part, g_chunk.part)],
                        out.at[high, low],
                        sem_out.at[away],
                    ).start()

            left += 1

    behind = [lax.rem(where[0] + groups - owner, groups) for owner in range(groups)]
    ahead_of = [lax.rem(owner + groups - where[0], groups) for owner in range(groups)]

    def column(kind, f):
        at = w_chunk.rows_at[kind, f]
        return jnp.concatenate([weights[place, at : at + shard, :] for place in behind], 0)

    def store(kind, f, block):
        at = g_chunk.rows_at[kind, f]
        for owner in range(groups):
            grads[ahead_of[owner], at : at + shard, :] = block[owner * shard : (owner + 1) * shard]

    fetch_to(AHEAD)
    out_t = out_grad_t[...]
    upstream = turned(out_t)
    inputs = tokens_t[...].astype(f32).T
    att_t = turned(attended[...])
    if g_chunk.used < g_chunk.rows:
        grads[:, g_chunk.used :, :] = jnp.zeros(
            (groups, g_chunk.rows - g_chunk.used, LANES), bf16
        )
    need(w_chunk.out_end)
    output_w = jnp.concatenate([column("out", j) for j in range(out_blocks)], 1)[:, :width]
    mixed = inputs + dot(attended[...], output_w)
    scale = lax.rsqrt(jnp.mean(mixed * mixed, axis=1, keepdims=True) + NORM_EPS)
    unit = mixed * scale
    gained = gain[...]
    normed = (unit * gained).astype(bf16)
    normed_t = turned(normed)
    back = jnp.zeros(mixed.shape, f32)
    ahead = mixed
    for share in range(w_chunk.own):
        need(w_chunk.share_end[share])
        blocks = w_chunk.blocks(share)
        down_at = w_chunk.rows_at["down", share]
        down_to = g_chunk.rows_at["down", share]
        for pair in range(0, len(blocks), 4):
            some = blocks[pair : pair + 4]
            gate_w = jnp.concatenate([column("gate", f) for f in some], 1)
            up_w = jnp.concatenate([column("up", f) for f in some], 1)
            down_w = jnp.concatenate(
                [weights[behind[f // w_chunk.own], down_at : down_at + width, :] for f in some], 1
            )
            gate = dot(normed, gate_w)
            up = dot(normed, up_w)
            hidden_grad = dot(upstream, down_w)
            sigmoid = 1.0 / (1.0 + jnp.exp(-gate))
            silu = gate * sigmoid
            hidden = (silu * up).astype(bf16)
            gate_low = (hidden_grad * up * (sigmoid * (1.0 + gate * (1.0 - sigmoid)))).astype(bf16)
            up_low = (hidden_grad * silu).astype(bf16)
            ahead = ahead + dot(hidden, down_w, (1, 1))
            back = back + dot(gate_low, gate_w, (1, 1)) + dot(up_low, up_w, (1, 1))
            gate_wg = dot(normed_t, gate_low).astype(bf16)
            up_wg = dot(normed_t, up_low).astype(bf16)
            down_wg = dot(out_t, hidden).astype(bf16)
            for at, f in enumerate(some):
                cols = slice(at * LANES, (at + 1) * LANES)
                store("gate", f, gate_wg[:, cols])
                store("up", f, up_wg[:, cols])
                grads[ahead_of[f // g_chunk.own], down_to : down_to + width, :] = down_wg[:, cols]
        leave(g_chunk.share_end[share])
    layer_out_t[...] = ahead.T.astype(bf16)
    gain_grad[...] = jnp.sum(back * unit, axis=0, keepdims=True)
    inner = back * gained
    through = scale * (inner - unit * jnp.mean(inner * unit, axis=1, keepdims=True))
    mixed_back = upstream.astype(f32) + through
    mixed_grad[...] = mixed_back
    branch = mixed_back.astype(bf16)
    attended_grad[...] = dot(branch, output_w, (1, 1)).astype(bf16)
    output_wg = dot(att_t, branch)
    for j in range(out_blocks):
        block = output_wg[:, j * LANES : min((j + 1) * LANES, width)]
        if block.shape[1] < LANES:
            block = jnp.concatenate(
                [block, jnp.zeros((block.shape[0], LANES - block.shape[1]), f32)], 1
            )
        store("out", j, block.astype(bf16))
    leave(g_chunk.rows)
    pltpu.make_async_copy(keep, keep, sem_out.at[0]).wait()
    pltpu.make_async_copy(send, send, sem_out.at[1]).wait()


def run_mlp(where, w_chunk, g_chunk, pieces, attended, tokens_t, out_grad_t, gain):
    f32, bf16 = jnp.float32, jnp.bfloat16
    groups = w_chunk.groups
    width, toks = tokens_t.shape
    packed = shape((2, 2, groups, g_chunk.part, LANES), bf16)
    return staged_call(
        functools.partial(mlp_kernel, w_chunk, g_chunk),
        "mlp",
        kept("smem", where) + kept("staged", attended, tokens_t, out_grad_t, gain) + kept("hbm", *pieces),
        (
            shape((width, toks), bf16),
            shape((toks, width), f32),
            shape((toks, width), bf16),
            shape((1, width), f32),
            packed,
            packed,
        ),
        (vmem(),) * 4 + (hbm(),) * 2,
        [pltpu.VMEM((groups, chunk.rows, LANES), bf16) for chunk in (w_chunk, g_chunk)]
        + [pltpu.SemaphoreType.DMA((8,)), pltpu.SemaphoreType.DMA((2,))],
        BIG,
    )


def heads_back(grad, raw, cos, sin, gain, head_size):
    half = head_size // 2
    lows, total = [], jnp.zeros((1, head_size), jnp.float32)
    for at, (unit, factor) in enumerate(unit_heads(raw, head_size)):
        at *= head_size
        one, two = grad[:, at : at + half], grad[:, at + half : at + head_size]
        back = jnp.concatenate([one * cos + two * sin, two * cos - one * sin], 1)
        total = total + jnp.sum(back * unit, axis=0, keepdims=True)
        inner = back * gain
        lows.append(factor * (inner - unit * jnp.mean(inner * unit, axis=1, keepdims=True)))
    return lows, total


def query_back_kernel(sizes, query_grad, raw, normed, head_gains, cosine, sine, weights, products, back, total):
    q_width, _, head_size = sizes
    lows, total[...] = heads_back(
        query_grad[...], raw[:, :q_width], cosine[...], sine[...], head_gains[0:1, :], head_size
    )
    low = jnp.concatenate(lows, 1).astype(products.dtype)
    back[...] = dot(low, weights[:, :q_width], (1, 1))
    products[...] = dot(turned(normed[...]), low).astype(products.dtype)


def run_query_back(query_grad, raw, normed, head_gains, cosine, sine, weights, sizes):
    f32 = jnp.float32
    q_width, _, head_size = sizes
    toks, width = normed.shape
    return staged_call(
        functools.partial(query_back_kernel, sizes),
        "query_back",
        kept("vmem", query_grad, raw, normed, head_gains, cosine, sine, weights),
        (shape((width, q_width), normed.dtype), shape((toks, width), f32), shape((1, head_size), f32)),
        (vmem(),) * 3,
        (),
        24,
    )


def last_kernel(sizes, where, products, back, q_total, raw, normed, tokens_t, mixed_grad, gain, head_gains, cosine, sine, weights, second, *refs):
    f32, bf16 = jnp.float32, jnp.bfloat16
    q_width, kv_width, head_size = sizes
    kv_parts = refs[: len(refs) - 4]
    token_grad_t, keep, send, grads = refs[len(refs) - 4 :]
    count, groups, rows, _ = grads.shape
    width, toks = tokens_t.shape
    shard = width // groups
    kv_grad = kv_parts[0][...].astype(f32)
    for part in kv_parts[1:]:
        kv_grad = kv_grad + part[...].astype(f32)
    lows, k_total = heads_back(
        kv_grad, raw[:, q_width:], cosine[...], sine[...], head_gains[1:2, :], head_size
    )
    low = jnp.concatenate(lows + [kv_grad[:, kv_width:]], 1).astype(bf16)
    short = count * LANES - q_width - 2 * kv_width
    pieces = [products[...], dot(turned(normed[...]), low).astype(bf16)]
    if short:
        pieces.append(jnp.zeros((width, short), bf16))
    blocks = jnp.concatenate(pieces, 1)
    for j in range(count):
        for owner in range(groups):
            grads[j, owner, :shard, :] = blocks[
                owner * shard : (owner + 1) * shard, j * LANES : (j + 1) * LANES
            ]
            grads[j, owner, shard:, :] = jnp.zeros((rows - shard, LANES), bf16)
    whole = back[...] + dot(low, weights[:, q_width : q_width + 2 * kv_width], (1, 1))
    inputs = tokens_t[...].astype(f32).T
    scale = lax.rsqrt(jnp.mean(inputs * inputs, axis=1, keepdims=True) + NORM_EPS)
    unit = inputs * scale
    first = jnp.sum(whole * unit, axis=0, keepdims=True)
    inner = whole * gain[...]
    whole = mixed_grad[...] + scale * (inner - unit * jnp.mean(inner * unit, axis=1, keepdims=True))
    token_grad_t[...] = whole.T

    def line(vector):
        short = LANES - vector.shape[1]
        return jnp.concatenate([vector, jnp.zeros((1, short), f32)], 1) if short else vector

    head_part = head_size // groups
    for owner in range(groups):
        lines = []
        for vector in (first, second[...]):
            mine = vector[:, owner * shard : (owner + 1) * shard]
            lines += [line(mine[:, at : at + LANES]) for at in range(0, shard, LANES)]
        for vector in (q_total[...], k_total):
            lines.append(line(vector[:, owner * head_part : (owner + 1) * head_part]))
        lines.append(jnp.zeros((rows - shard - len(lines), LANES), f32))
        grads[0, owner, shard:, :] = jnp.concatenate(lines, 0).astype(bf16)
    for core in range(2):
        for across in range(2):
            for along in range(2):
                block = block_at(where, core, across, along)
                for step in range(groups):
                    owner = lax.rem(where[0] + step, groups)
                    (send if core else keep)[across * 2 + along, step] = grads[block, owner]


def run_last(where, products, back, q_total, raw, normed, tokens_t, mixed_grad, gain, head_gains, cosine, sine, weights, second, kv_parts, sizes):
    width = tokens_t.shape[0]
    groups = lax.axis_size("grp")
    rows = width // groups + SMALL
    packed = shape((4, groups, rows, LANES), jnp.bfloat16)
    return staged_call(
        functools.partial(last_kernel, sizes),
        "last",
        kept("smem", where)
        + kept("vmem", products, back, q_total, raw, normed)
        + kept("staged", tokens_t)
        + kept("vmem", mixed_grad, gain, head_gains, cosine, sine, weights, second, *kv_parts),
        (shape(tokens_t.shape, jnp.float32), packed, packed),
        (vmem(),) * 3,
        [pltpu.VMEM((8, groups, rows, LANES), jnp.bfloat16)],
        24,
    )


def unpack_kernel(sizes, chunk, where, near, far, *refs):
    f32 = jnp.float32
    q_width, kv_width, _ = sizes
    gate, up, down_t, output, query, key, value = refs[:7]
    lines_out = refs[7:11]
    pack = refs[11]
    shard, width = chunk.shard, chunk.width
    projections = []
    small = None
    for core in range(2):
        for across in range(2):
            for along in range(2):
                place = (where[2] ^ across) * 2 + (where[3] ^ along)
                piece = jnp.where(where[1] == core, near[place], far[place])
                at = chunk.part
                high, low = (across, along) if core == 0 else (along, across)
                row = (core * 4 + high * 2 + low) * chunk.part
                pack[row : row + chunk.part, :] = piece[:at]
                projections.append(piece[at : at + shard])
                if small is None:
                    small = piece[at + shard :].astype(f32)
    for (kind, j), at in chunk.rows_at.items():
        if kind == "down":
            down_t[:, j * LANES : (j + 1) * LANES] = pack[at : at + width].astype(f32)
            continue
        out = {"gate": gate, "up": up, "out": output}[kind]
        stop = min((j + 1) * LANES, out.shape[1])
        out[:, j * LANES : stop] = pack[at : at + shard].astype(f32)[:, : stop - j * LANES]
    whole = jnp.concatenate(projections, 1).astype(f32)
    query[...] = whole[:, :q_width]
    key[...] = whole[:, q_width : q_width + kv_width]
    value[...] = whole[:, q_width + kv_width : q_width + 2 * kv_width]
    row = 0
    for out in lines_out:
        for at in range(0, out.shape[1], LANES):
            stop = min(at + LANES, out.shape[1])
            out[:, at:stop] = small[row : row + 1, : stop - at]
            row += 1


def run_unpack(where, chunk, sizes, near, far, hidden_width, own_hidden, head_part):
    f32 = jnp.float32
    q_width, kv_width, _ = sizes
    shard, width = chunk.shard, chunk.width
    return staged_call(
        functools.partial(unpack_kernel, sizes, chunk),
        "unpack",
        kept("smem", where) + kept("vmem", near, far),
        (
            shape((shard, hidden_width), f32),
            shape((shard, hidden_width), f32),
            shape((width, own_hidden), f32),
            shape((shard, width), f32),
            shape((shard, q_width), f32),
            shape((shard, kv_width), f32),
            shape((shard, kv_width), f32),
            shape((1, shard), f32),
            shape((1, shard), f32),
            shape((1, head_part), f32),
            shape((1, head_part), f32),
        ),
        (vmem(),) * 11,
        [pltpu.VMEM((chunk.rows, LANES), near.dtype)],
        24,
    )


def body(
    tokens,
    segments,
    out_grad,
    norm_gain,
    query_gain,
    key_gain,
    query_weight,
    key_weight,
    value_weight,
    output_weight,
    second_gain,
    gate_weight,
    up_weight,
    down_weight,
):
    f32, bf16 = jnp.float32, jnp.bfloat16
    groups = lax.axis_size("grp")
    place_z = lax.axis_index("grp")
    where = place_scalars()
    toks, width = tokens.shape
    shard = norm_gain.shape[0]
    head_part = query_gain.shape[0]
    head_size = head_part * groups
    hidden_width, own_hidden = gate_weight.shape[1], down_weight.shape[0]
    sizes = (query_weight.shape[1], key_weight.shape[1], head_size)
    w_chunk, g_chunk = chunks_of(shard, width, own_hidden, groups)
    tokens_t, out_grad_t = tokens.T, out_grad.T

    fence = lax.optimization_barrier
    own_first, own_second = run_pack(
        where, w_chunk, query_weight, key_weight, value_weight,
        gate_weight, up_weight, down_weight.T, output_weight,
    )
    first_z = [own_first] + [shift(own_first, step) for step in range(1, groups)]
    second_z = [own_second] + [shift(own_second, step) for step in range(1, groups)]

    gain_rows = -(-shard // LANES)
    seg_rows = -(-toks // LANES)
    _, segs = fence((own_first, segments))
    small = jnp.zeros((SMALL * LANES,), bf16)
    at = 0
    for line, count in (
        (norm_gain, gain_rows),
        (second_gain, gain_rows),
        (query_gain, 1),
        (key_gain, 1),
        (segs.astype(bf16), seg_rows),
    ):
        small = small + jnp.pad(line, (at, SMALL * LANES - at - line.shape[0]))
        at += count * LANES
    small = small.reshape(SMALL, LANES)
    small_behind = jnp.stack([small] + [shift(small, step) for step in range(1, groups)])

    small_behind = small_behind.astype(f32)
    small_all = small_behind[lax.rem(place_z + groups - jnp.arange(groups), groups)]
    at = 0
    gains = []
    for count, length in ((gain_rows, shard), (gain_rows, shard), (1, head_part), (1, head_part)):
        gains.append(lined(small_all[:, at : at + count], length))
        at += count
    gain_first, gain_second, gain_query, gain_key = gains
    head_gains = jnp.concatenate([gain_query, gain_key])
    segs = small_behind[:, at : at + seg_rows].reshape(groups, -1)[:, :toks]
    there = (place_z >= jnp.arange(groups))[:, None]
    key_seg = jnp.where(there, segs, -1.0).reshape(1, -1)
    own_seg = segs[0][:, None]
    earlier = ((key_seg < own_seg) & (key_seg >= 0.0)).astype(jnp.int32)
    positions = place_z * toks + jnp.arange(toks, dtype=jnp.int32) - jnp.sum(earlier, axis=1)
    half = head_size // 2
    inverse = ROPE_BASE ** (-(jnp.arange(half, dtype=f32) * 2.0 / head_size))
    angles = positions.astype(f32)[:, None] * inverse[None, :]
    cosine, sine = jnp.cos(angles), jnp.sin(angles)

    near = spread_chip(jnp.stack(first_z))
    near, second_z = fence((near, second_z))
    whole = jnp.stack(second_z)
    near, gain_first, gain_second, head_gains, cosine, sine, own_seg, key_seg = fence(
        (near, gain_first, gain_second, head_gains, cosine, sine, own_seg, key_seg)
    )
    normed, raw, query, key_value, proj_weights = run_proj(
        where, near, hop(near, 1), tokens_t, gain_first, head_gains, cosine, sine, sizes
    )
    held = [key_value]
    for step in range(1, groups):
        ahead = [(i, i + step) for i in range(groups - step)]
        held.append(lax.ppermute(key_value, "grp", ahead))
    whole = jnp.stack([whole, hop_split(whole, 4, 2)])
    far_whole = hop_split(whole, 2, 4)
    whole, held = fence((whole, held))
    other = hop(whole, 1)
    attended, exact, probs = run_attend(query, own_seg, key_seg, held, sizes)
    far_whole, attended, other = fence((far_whole, attended, other))
    pieces = [whole, far_whole, other, hop(far_whole, 1)]
    layer_out_t, mixed_grad, attended_grad, second_sum, keep, send = run_mlp(
        where, w_chunk, g_chunk, pieces, attended, tokens_t, out_grad_t, gain_second
    )
    got = hop(send, 1)
    query_grad, *kv_parts = run_attend_back(query, attended_grad, exact, probs, held, sizes)
    got, query_grad, kv_parts = fence((got, query_grad, kv_parts))
    kv_back = [kv_parts[0]]
    for step in range(1, groups):
        back = [(i + step, i) for i in range(groups - step)]
        kv_back.append(lax.ppermute(kv_parts[step], "grp", back))
    near_got = hop_split(add_low(keep[1], got[1]), 2, 4)
    query_parts = run_query_back(
        query_grad, raw, normed, head_gains, cosine, sine, proj_weights, sizes
    )
    near_got, kv_back, query_parts = fence((near_got, kv_back, query_parts))
    far_got = hop_split(add_low(keep[0, 1], got[0, 1], near_got[1]), 4, 2)
    token_grad_t, late_keep, late_send = run_last(
        where, *query_parts, raw, normed, tokens_t, mixed_grad, gain_first, head_gains, cosine, sine,
        proj_weights, second_sum, kv_back, sizes,
    )
    late_got = hop(late_send, 1)
    far_got, late_got = fence((far_got, late_got))
    early = fold_grp(
        [add_low(keep[0, 0, d], got[0, 0, d], near_got[0, d], far_got[d]) for d in range(groups)]
    )
    late = fold_blocks(late_keep, late_got)
    near = spread_chip(jnp.concatenate([early, fold_grp(late)]))
    far = hop(near, 1)
    (
        gate_sum, up_sum, down_sum_t, output_sum, query_sum, key_sum, value_sum,
        first_sum, second_sum, query_gsum, key_gsum,
    ) = run_unpack(where, g_chunk, sizes, near, far, hidden_width, own_hidden, head_part)
    return (
        layer_out_t.T,
        token_grad_t.T,
        first_sum.reshape(-1),
        query_gsum.reshape(-1),
        key_gsum.reshape(-1),
        query_sum,
        key_sum,
        value_sum,
        output_sum,
        second_sum.reshape(-1),
        gate_sum,
        up_sum,
        down_sum_t.T,
    )


def solution(mesh):
    placed = (
        P(("rep", "grp"), None),
        P(("rep", "grp")),
        P(("rep", "grp"), None),
        P("grp"),
        P("grp"),
        P("grp"),
        P("grp", None),
        P("grp", None),
        P("grp", None),
        P("grp", None),
        P("grp"),
        P("grp", None),
        P("grp", None),
        P("grp", None),
    )
    return jax.shard_map(
        body,
        mesh=mesh,
        in_specs=placed,
        out_specs=(
            P(("rep", "grp"), None),
            P(("rep", "grp"), None),
            P("grp"),
            P("grp"),
            P("grp"),
            P("grp", None),
            P("grp", None),
            P("grp", None),
            P("grp", None),
            P("grp"),
            P("grp", None),
            P("grp", None),
            P("grp", None),
        ),
        check_vma=False,
    )
```
